128 devices in a mesh: str: 16 (over x_lo, y, core), crs: 8 (over x_hi, z).
Axes of the slice: x: 4 (x_hi: 2, x_lo: 2; x = x_hi * 2 + x_lo), y: 4, z: 4, core: 2. Of those that a mesh axis runs over, the one named last changes fastest.
Arguments:
- voltage: float32 [4, 512, 16384], P(None, 'str', 'crs'), may hold values from -4 to 0.5
- photocurrent: float32 [4, 512, 16384], P(None, 'str', 'crs'), may hold values from 0.1 to 10
- shunt: float32 [512, 16384], P('str', 'crs'), may hold values from 0.02 to 0.5
- series: float32 [512, 16384], P('str', 'crs'), may hold values from 0.5 to 2
- pattern: int32 [512, 128], P('str', 'crs'), may hold values from 0 to 3
- diode_mask: int32 [512, 128], P('str', 'crs'), may hold values 0 or 1
- aggregate: int32 [512, 128], P('str', 'crs'), may hold values from 0 to 4095, as said below
- coarse_inverse: float32 [4096, 4096], P('crs'), as said below
Outputs:
- newton_step: float32 [4, 512, 16384], P(None, 'str', 'crs')
- residual: float32 [4, 512, 16384], P(None, 'str', 'crs')
The draws below stay inside these ranges and needn't reach their ends.
Inputs may be any that keep to these rules, and one draw needn't show every extreme that they name: `aggregate`: every value appears. coarse_inverse is symmetric positive definite.
All inputs are finite; a program needn't handle non-finite values. No bound on the sum of `diode_mask` on one device may be relied on, other than what follows from the above.
Results may differ from the reference program's by a relative error of at most 0.0003.
Values sent between devices are 32-bit elements; how exact they have to be, the bound alone decides.
A program may use at most 64 MiB of HBM per device.

```python
import math
import jax
import jax.numpy as jnp
from jax import lax

S = 4
AR = 16
ITERS = 3
NR = 512
NCOL = 16384
NB = 128
GROUPS_OVERALL = 4096


def vertex_ordering(key):
    return jax.random.permutation(jax.random.fold_in(key, 11), GROUPS_OVERALL)


def draw_photocurrent(key, part):
    first = jax.random.fold_in(jax.random.fold_in(key, 3), 0)
    rows = lax.broadcasted_iota(jnp.float32, (S, NR, NCOL), 1) / NR
    base = jnp.exp(jax.random.uniform(first, (S, NR, NCOL), jnp.float32, math.log(0.3), math.log(3.0)))
    return base * (1.0 + 2.0 * rows)


def draw_aggregate(key, part):
    offset = jax.random.randint(jax.random.fold_in(key, 13), (), 0, AR)
    rows = lax.broadcasted_iota(jnp.int32, (NR, NB), 0)
    cols = lax.broadcasted_iota(jnp.int32, (NR, NB), 1)
    group_tag = (rows + offset) % NR // AR * NB + cols
    reorder_vertices = vertex_ordering(key)
    return reorder_vertices[group_tag].astype(jnp.int32)


def cycle_bound(reach):
    ratio = jnp.exp(-1.0 / reach)
    return (1.0 + ratio) / (1.0 - ratio)


def draw_coarse_inverse(key, part):
    reorder_vertices = vertex_ordering(key)
    vertex_positions = jnp.zeros((GROUPS_OVERALL,), jnp.int32).at[reorder_vertices].set(jnp.arange(GROUPS_OVERALL, dtype=jnp.int32))
    own_key = jax.random.fold_in(key, 17)
    reach_key, rough_key, scale_key = jax.random.split(own_key, 3)
    agg_rows = NR // AR
    divisors = jax.random.uniform(reach_key, (2,), jnp.float32, 8.0, 16.0)
    scale_factors = jnp.exp(jax.random.uniform(scale_key, (GROUPS_OVERALL,), jnp.float32, math.log(0.7), math.log(1.4)))
    reach_along = agg_rows / divisors[0]
    reach_across = NB / divisors[1]
    along = (vertex_positions // NB).astype(jnp.float32)
    across = (vertex_positions % NB).astype(jnp.float32)
    gap_along = jnp.abs(along[:, None] - along[None, :])
    gap_along = jnp.minimum(gap_along, agg_rows - gap_along)
    gap_across = jnp.abs(across[:, None] - across[None, :])
    kernel = jnp.exp(-gap_along / reach_along - gap_across / reach_across)
    rough = jax.random.uniform(rough_key, (GROUPS_OVERALL, GROUPS_OVERALL), jnp.float32, -1.0, 1.0)
    rough = 0.5 * (rough + rough.T)
    bound = cycle_bound(reach_along) * cycle_bound(reach_across)
    rows = lax.broadcasted_iota(jnp.int32, (GROUPS_OVERALL, GROUPS_OVERALL), 0)
    cols = lax.broadcasted_iota(jnp.int32, (GROUPS_OVERALL, GROUPS_OVERALL), 1)
    matrix = kernel * (1.0 + 0.8 * rough) + jnp.where(rows == cols, 0.8 * bound + 0.2, jnp.float32(0.0))
    return scale_factors[:, None] * scale_factors[None, :] * matrix * (0.25 / (AR * 128.0 * bound))


def touch_ends(entries, key, least, top_value):
    longest = entries.shape.index(max(entries.shape))
    spots = []
    for shift in (0, 1):
        where = [jax.random.randint(jax.random.fold_in(key, axis), (), 0, length) for axis, length in enumerate(entries.shape)]
        where[longest] = (where[longest] + shift) % entries.shape[longest]
        spots.append(tuple(where))
    return entries.at[spots[0]].set(least).at[spots[1]].set(top_value)


def levels(key, dims, cuts, low, top_value):
    gain, own = 1.0, jax.random.fold_in(key, 6)
    for dim, shards_of in cuts:
        heights = jnp.exp(jax.random.uniform(jax.random.fold_in(own, dim), (shards_of,), jnp.float32, low / len(cuts), top_value / len(cuts)))
        gain = gain * jnp.repeat(heights, dims[dim] // shards_of).reshape([-1 if axis == dim else 1 for axis in range(len(dims))])
    return gain


def setup_inputs(seed: int = 0) -> dict:
    keys = jax.random.split(jax.random.key(seed), 9)
    voltage = jnp.clip(-4.0 + 4.5 * jax.random.uniform(keys[0], (S, NR, NCOL), jnp.float32) ** levels(keys[0], (S, NR, NCOL), ((1, 16), (2, 8)), -0.2, 0.2), -4.0, 0.5)
    photocurrent = draw_photocurrent(jax.random.fold_in(keys[8], 71), 0)
    shunt = jnp.clip(jnp.exp(math.log(0.5) - 3.218876 * jax.random.uniform(keys[2], (NR, NCOL), jnp.float32) ** levels(keys[2], (NR, NCOL), ((0, 16), (1, 8)), -0.2, 0.2)), 0.02, 0.5)
    series = jnp.clip(jnp.exp(math.log(2.0) - 1.3862944 * jax.random.uniform(keys[3], (NR, NCOL), jnp.float32) ** levels(keys[3], (NR, NCOL), ((0, 16), (1, 8)), -0.2, 0.2)), 0.5, 2.0)
    pattern = touch_ends(jax.random.randint(keys[4], (NR, NB), 0, 4), jax.random.fold_in(keys[4], 1), 0, 3).astype(jnp.int32)
    diode_mask = touch_ends((jax.random.randint(keys[5], (NR, NB), 0, 4) < 3).astype(jnp.int32), jax.random.fold_in(keys[5], 1), 0, 1)
    aggregate = draw_aggregate(jax.random.fold_in(keys[8], 71), 0)
    coarse_inverse = draw_coarse_inverse(jax.random.fold_in(keys[8], 71), 0)
    return dict(voltage=voltage, photocurrent=photocurrent, shunt=shunt, series=series, pattern=pattern, diode_mask=diode_mask, aggregate=aggregate, coarse_inverse=coarse_inverse)


LEVELS = (0.25, 0.5, 1.0, 2.0)
DIODE_SAT = 0.5


def widen(blocks):
    return jnp.repeat(blocks, 128, axis=1)


def cross_levels(pattern):
    total = jnp.zeros(pattern.shape, jnp.float32)
    for number in range(4):
        total = total + jnp.where(pattern == number, jnp.float32(LEVELS[number]), jnp.float32(0.0))
    return total


def neighbours(field):
    below = jnp.roll(field, -1, axis=0)
    above = jnp.roll(field, 1, axis=0)
    extended_width = jnp.pad(field, ((0, 0), (1, 1)))
    return below, above, extended_width[:, 2:], extended_width[:, :-2]


def reference(voltage, photocurrent, shunt, series, pattern, diode_mask, aggregate, coarse_inverse):
    cross_level = widen(cross_levels(pattern))
    padded_level = jnp.pad(cross_level, ((0, 0), (1, 1)))
    right_link = jnp.minimum(cross_level, padded_level[:, 2:])
    left_link = jnp.minimum(cross_level, padded_level[:, :-2])
    down_link = series
    up_link = jnp.roll(series, 1, axis=0)
    diode_area = widen(diode_mask.astype(jnp.float32))
    flat_groups = aggregate.reshape(-1)

    def solve_case(inputs):
        volts, current = inputs
        diode_derivative = DIODE_SAT * diode_area * jnp.exp(volts)
        below, above, right_cells, left_cells = neighbours(volts)
        imbalance = (shunt * volts + down_link * (volts - below) + up_link * (volts - above)
                     + right_link * (volts - right_cells) + left_link * (volts - left_cells)
                     + diode_derivative - DIODE_SAT * diode_area - current)
        diagonal = shunt + diode_derivative + down_link + up_link + right_link + left_link

        def operate(field):
            below, above, right_cells, left_cells = neighbours(field)
            return (diagonal * field - down_link * below - up_link * above
                    - right_link * right_cells - left_link * left_cells)

        def precondition(remainder):
            block_sums = remainder.reshape(NR, NB, 128).sum(axis=-1).reshape(-1)
            coarse = jax.ops.segment_sum(block_sums, flat_groups, num_segments=GROUPS_OVERALL)
            correction = jnp.dot(coarse, coarse_inverse, precision=lax.Precision.HIGHEST)
            return remainder / diagonal + widen(correction[aggregate])

        remainder = -imbalance
        newton_step = jnp.zeros_like(volts)
        smoothed = precondition(remainder)
        direction = smoothed
        product = jnp.sum(remainder * smoothed)
        for turn in range(ITERS):
            image = operate(direction)
            alpha = product / jnp.sum(direction * image)
            newton_step = newton_step + alpha * direction
            remainder = remainder - alpha * image
            if turn + 1 < ITERS:
                smoothed = precondition(remainder)
                fresh = jnp.sum(remainder * smoothed)
                direction = smoothed + (fresh / product) * direction
                product = fresh
        return newton_step, remainder

    newton_step, residual = lax.map(solve_case, (voltage, photocurrent))
    return newton_step, residual
```

```python
import jax
import jax.numpy as jnp
from jax import lax
from jax.experimental import pallas as pl
from jax.experimental.pallas import tpu as pltpu
from jax.sharding import PartitionSpec as P

MESH = pl.DeviceIdType.MESH
F32 = jnp.float32
BF16 = jnp.bfloat16

CASES = 4
ROWS = 32
BLOCKS = 16
STEP = 40
FIELD = (BLOCKS + 2) * STEP
NS = 16
NC = 8
SOLVES = 3
LEVELS = (0.25, 0.5, 1.0, 2.0)


def dot(a, b):
    return jnp.dot(a, b, preferred_element_type=F32)


def halves(x):
    high = x.astype(BF16)
    return high, (x - high.astype(F32)).astype(BF16)


def kernel(
    v_in, photo_in, shunt_in, series_in, pattern_in, mask_in, group_in, inverse_in,
    step_out, rest_out,
    vn, pn, shn, sn, patn, maskn, groupn, staged, a_high, a_low,
    ef, rf, qf, df, xf, uf, wf, dgf, inf, pcf,
    sf, rlf, llf, dmf,
    cb, gm, e_low, m_high, groups, e_turn, ones_pair, ones_wide,
    bu, bw, bq, sd, ss, su, er, el, lb,
    pk, su_s, sd_s, sl_s, sr_s, su_r, sd_r, sl_r, sr_r,
    hu_s, hd_s, hl_s, hr_s, hu_r, hd_r, hl_r, hr_r,
    s1, r1, s2, r2, s3, r3, s4, r4, f1s, f1r, f2s, f2r,
    y_now, t_now, t_tile, state, per_case,
    in_sem, out_sem, setup_send, setup_recv, halo_send, halo_recv, send_sem, recv_sem, last_send, last_recv,
):
    s = lax.axis_index("str")
    c = lax.axis_index("crs")

    def at_str(k):
        return (lax.rem(s + k, NS), c)

    def at_crs(k):
        return (s, lax.rem(c + k, NC))

    barrier = pltpu.get_barrier_semaphore()
    for k in range(1, NS):
        pl.semaphore_signal(barrier, inc=1, device_id=at_str(k), device_id_type=MESH)
    for k in range(1, NC):
        pl.semaphore_signal(barrier, inc=1, device_id=at_crs(k), device_id_type=MESH)

    loads = [
        pltpu.make_async_copy(v_in, vn, in_sem.at[0]),
        pltpu.make_async_copy(series_in, sn, in_sem.at[1]),
        pltpu.make_async_copy(pattern_in, patn, in_sem.at[2]),
        pltpu.make_async_copy(mask_in, maskn, in_sem.at[3]),
        pltpu.make_async_copy(group_in, groupn, in_sem.at[4]),
        pltpu.make_async_copy(shunt_in, shn, in_sem.at[5]),
        pltpu.make_async_copy(photo_in, pn, in_sem.at[6]),
    ]
    quarter = pl.multiple_of((s // 4) * 128, 128)
    for k in range(NC):
        loads.append(
            pltpu.make_async_copy(
                inverse_in.at[:, pl.ds(pl.multiple_of(k * 512 + quarter, 128), 128)], staged.at[k], in_sem.at[7 + k]
            )
        )
    for copy in loads:
        copy.start()

    lane = lax.broadcasted_iota(jnp.int32, (ROWS, 128), 1)
    case_of = lane // 32
    is_first = lane == 0
    is_last = lane == 127
    case8 = case_of[0:8]
    sub8 = lax.broadcasted_iota(jnp.int32, (8, 128), 0)
    spot = (lax.broadcasted_iota(jnp.int32, (ROWS, 128), 0) == lane - 32 * case_of).astype(F32)

    def remote(src, dst, send, recv, who):
        return pltpu.make_async_remote_copy(
            src_ref=src, dst_ref=dst, send_sem=send, recv_sem=recv, device_id=who, device_id_type=MESH
        )

    def arrived(ref, sem):
        pltpu.make_async_copy(ref, ref, sem).wait()

    def rows_of(case, row):
        return pl.ds(case * FIELD + STEP + row, BLOCKS, stride=STEP)

    def edges_out(f, up, down, left, right):
        for case in range(CASES):
            up[case * 16 : case * 16 + 16, :] = f[rows_of(case, 0), :]
            down[case * 16 : case * 16 + 16, :] = f[rows_of(case, ROWS - 1), :]
        for block, ref in ((0, left), (BLOCKS - 1, right)):
            first = (block + 1) * STEP
            tile = jnp.concatenate(
                [f[case * FIELD + first : case * FIELD + first + ROWS, :] for case in range(CASES)], axis=0
            ).T
            ref[0:8, :] = tile[0:8] if block == 0 else tile[120:128]

    def edges_in(f, above, below, left, right):
        for case in range(CASES):
            f[rows_of(case, -1), :] = above[case * 16 : case * 16 + 16, :]
            f[rows_of(case, ROWS), :] = below[case * 16 : case * 16 + 16, :]
        for first, row in ((0, left[7:8, :]), (17 * STEP, right[0:1, :])):
            tile = jnp.broadcast_to(row, (128, 128)).T
            for case in range(CASES):
                f[case * FIELD + first : case * FIELD + first + ROWS, :] = tile[case * ROWS : case * ROWS + ROWS]

    def exchange(bufs, send, recv):
        up_s, down_s, left_s, right_s, above_r, below_r, left_r, right_r = bufs
        copies = [
            remote(up_s, below_r, send.at[0], recv.at[0], at_str(NS - 1)),
            remote(down_s, above_r, send.at[1], recv.at[1], at_str(1)),
            remote(left_s, right_r, send.at[2], recv.at[2], at_crs(NC - 1)),
            remote(right_s, left_r, send.at[3], recv.at[3], at_crs(1)),
        ]
        for copy in copies:
            copy.start()
        return copies

    def neighbours(f, case, base):
        def part(shift):
            return f[pl.ds(case * FIELD + base + shift, ROWS), :]

        here = part(0)
        right = jnp.where(is_last, pltpu.roll(part(STEP), 127, 1), pltpu.roll(here, 127, 1))
        left = jnp.where(is_first, pltpu.roll(part(-STEP), 1, 1), pltpu.roll(here, 1, 1))
        return here, part(1), part(-1), right, left

    def links(j, base):
        flat = pl.ds(pl.multiple_of(j * ROWS, ROWS), ROWS)
        return sf[pl.ds(base, ROWS), :], sf[pl.ds(base - 1, ROWS), :], rlf[flat, :], llf[flat, :]

    def jacobian(f, case, base, link):
        down, up, right_link, left_link = link
        here, below, above, right, left = neighbours(f, case, base)
        diagonal = dgf[pl.ds(case * FIELD + base, ROWS), :]
        return here, diagonal * here - down * below - up * above - right_link * right - left_link * left

    def fold(x):
        return x[0:8] + x[8:16] + x[16:24] + x[24:32]

    def by_case(parts):
        total = jnp.zeros((8, 128), F32)
        for case in range(CASES):
            total = jnp.where(case8 == case, jnp.sum(parts[case], axis=(0, 1), keepdims=True), total)
        return total

    def case_sums(x):
        total = jnp.zeros((8, 128), F32)
        for case in range(CASES):
            one = jnp.sum(jnp.where(case8 == case, x, 0.0), axis=1, keepdims=True)
            total = jnp.where(case8 == case, one, total)
        return total


    def spread(x, column, rows=ROWS):
        return jnp.broadcast_to(x[:, column : column + 1], (rows, 128))

    for copy in loads[:5]:
        copy.wait()
    level = jnp.zeros((ROWS, BLOCKS), F32)
    for number in range(4):
        level = level + jnp.where(patn[...] == number, F32(LEVELS[number]), F32(0.0))
    pk[...] = jnp.zeros_like(pk)
    pk[:, 0:16] = groupn[...].astype(F32)
    pk[:, 16:32] = level
    packed = pk[...]

    def lay_out(j, _):
        base = pl.multiple_of((j + 1) * STEP, 8)
        cols = pl.ds(pl.multiple_of(j * 128, 128), 128)
        for case in range(CASES):
            ef[pl.ds(case * FIELD + base, ROWS), :] = vn[case, :, cols]
        sf[pl.ds(base, ROWS), :] = sn[:, cols]
        return 0

    lax.fori_loop(0, BLOCKS, lay_out, 0)
    edges_out(ef, su_s, sd_s, sl_s, sr_s)
    su_s[64:72, :] = packed[0:8]
    sd_s[64:72, :] = packed[24:32]
    sd_s[72:88, :] = sf[pl.ds(STEP + ROWS - 1, BLOCKS, stride=STEP), :]
    sl_s[8:40, :] = packed
    sr_s[8:40, :] = packed

    pl.semaphore_wait(barrier, NS - 1 + NC - 1)
    setup_copies = exchange((su_s, sd_s, sl_s, sr_s, sd_r, su_r, sl_r, sr_r), setup_send, setup_recv)

    groups[...] = jnp.zeros_like(groups)
    half_mask = maskn[...].astype(F32) * 0.5
    for j in range(BLOCKS):
        base = (j + 1) * STEP
        group = spread(packed, j).astype(jnp.int32)
        groups[base : base + ROWS, :] = group
        low = group // 32
        code = (low % 16) * 8 + low // 16
        lb[j * ROWS : j * ROWS + ROWS, 0:128] = (lane == code).astype(F32).astype(BF16)
        dmf[j * ROWS : j * ROWS + ROWS, :] = spread(half_mask, j)
    for k in range(4):
        e_turn[:, k * 128 : k * 128 + 128] = lb[k * 128 : k * 128 + 128, 0:128].astype(F32).T.astype(BF16)

    same = lax.broadcasted_iota(jnp.int32, (128, 128), 0) // 32
    across = lax.broadcasted_iota(jnp.int32, (128, 128), 1) // 32
    block_ones = (same == across).astype(F32).astype(BF16)
    ones_pair[0:128, :] = block_ones
    ones_pair[128:256, :] = block_ones
    for case in range(CASES):
        wide = (same == case).astype(F32).astype(BF16)
        ones_wide[0:128, case * 128 : case * 128 + 128] = wide
        ones_wide[128:256, case * 128 : case * 128 + 128] = wide

    for copy in loads[7:]:
        copy.wait()

    def pick(i, _):
        rows = pl.ds(pl.multiple_of(i * 32, 32), 32)
        for side in range(2):
            block = jnp.zeros((ROWS, 128), F32)
            for k in range(4):
                turn = lax.rem(32 * k + 128 - 32 * lax.rem(s, 4), 128)
                block = jnp.where(case_of == k, pltpu.roll(staged[side * 4 + k, rows, :], turn, 1), block)
            high, low = halves(block)
            a_high[rows, side * 128 : side * 128 + 128] = high
            a_low[rows, side * 128 : side * 128 + 128] = low
        return 0

    lax.fori_loop(0, 16, pick, 0)
    for copy in loads[5:7]:
        copy.wait()


    for copy in setup_copies:
        copy.wait()
    edges_in(ef, sd_r, su_r, sl_r, sr_r)
    sf[pl.ds(STEP - 1, BLOCKS, stride=STEP), :] = sd_r[72:88, :]
    above8 = sd_r[64:72, :]
    below8 = su_r[64:72, :]
    for j in range(BLOCKS):
        base = (j + 1) * STEP
        groups[base - 1 : base, :] = spread(above8, j, 8)[7:8].astype(jnp.int32)
        groups[base + ROWS : base + ROWS + 1, :] = spread(below8, j, 8)[0:1].astype(jnp.int32)
    packed_left = sl_r[8:40, :]
    packed_right = sr_r[8:40, :]
    groups[0:ROWS, :] = spread(packed_left, BLOCKS - 1).astype(jnp.int32)
    groups[17 * STEP : 17 * STEP + ROWS, :] = spread(packed_right, 0).astype(jnp.int32)

    open_left = jnp.where(c == 0, 0.0, 1.0).astype(F32)
    open_right = jnp.where(c == NC - 1, 0.0, 1.0).astype(F32)
    row_levels = (
        [spread(packed_left, 16 + BLOCKS - 1)] + [spread(packed, 16 + j) for j in range(BLOCKS)] + [spread(packed_right, 16)]
    )
    for j in range(BLOCKS):
        here = row_levels[j + 1]
        right = jnp.minimum(here, row_levels[j + 2])
        left = jnp.minimum(here, row_levels[j])
        if j == BLOCKS - 1:
            right = right * open_right
        if j == 0:
            left = left * open_left
        rlf[j * ROWS : j * ROWS + ROWS, :] = jnp.where(is_last, right, here)
        llf[j * ROWS : j * ROWS + ROWS, :] = jnp.where(is_first, left, here)
        er[j * ROWS : j * ROWS + ROWS, :] = right
        el[j * ROWS : j * ROWS + ROWS, :] = left

    def block_columns(j, base, sums, target):
        total = jnp.zeros((ROWS, 128), F32)
        for case in range(CASES):
            total = jnp.where(case_of == case, jnp.sum(sums[case], axis=1, keepdims=True), total)
        if target is not None:
            target[pl.ds(pl.multiple_of(j * ROWS, ROWS), ROWS), :] = total
        return total

    def to_scatter(j, base, total):
        flat = pl.ds(pl.multiple_of(j * ROWS, ROWS), ROWS)
        high, low = halves(total * m_high[pl.ds(base, ROWS), :])
        lb[flat, 0:128] = high
        lb[flat, 128:256] = low

    def codes(i, _):
        rows = pl.ds(pl.multiple_of(i * 80, 16), 80)
        group = groups[rows, :]
        lanes = lax.broadcasted_iota(jnp.int32, (80, 128), 1)
        e_low[rows, :] = (lanes == group // 32).astype(F32).astype(BF16)
        m_high[rows, :] = (lanes % 32 == group % 32).astype(F32)
        return 0

    lax.fori_loop(0, FIELD // 80, codes, 0)

    def start_values(j, sums):
        base = pl.multiple_of((j + 1) * STEP, 8)
        cols = pl.ds(pl.multiple_of(j * 128, 128), 128)
        flat = pl.ds(pl.multiple_of(j * ROWS, ROWS), ROWS)
        link = links(j, base)
        down, up, right_link, left_link = link
        shunt = shn[:, cols]
        half = dmf[flat, :]
        edge = jnp.where(is_last, right_link, 0.0) + jnp.where(is_first, left_link, 0.0)
        out, rests, plain = [], [], []
        for case in range(CASES):
            at = pl.ds(case * FIELD + base, ROWS)
            here, below, above, right, left = neighbours(ef, case, base)
            slope = half * jnp.exp(here)
            ground = shunt + slope + down + up
            diagonal = ground + right_link + left_link
            rest = pn[case, :, cols] - (
                shunt * here
                + down * (here - below)
                + up * (here - above)
                + right_link * (here - right)
                + left_link * (here - left)
                + slope
                - half
            )
            inverse = 1.0 / diagonal
            dgf[at, :] = diagonal
            inf[at, :] = inverse
            rf[at, :] = rest
            scaled = rest * inverse
            qf[at, :] = scaled
            out.append(sums[case] + fold(rest * scaled))
            rests.append(rest)
            plain.append(ground + edge)
        block_columns(j, base, plain, sd)
        ss[flat, :] = jnp.broadcast_to(jnp.sum(down, axis=1, keepdims=True), (ROWS, 128))
        su[flat, :] = jnp.broadcast_to(jnp.sum(up, axis=1, keepdims=True), (ROWS, 128))
        to_scatter(j, base, block_columns(j, base, rests, None))
        return tuple(out)

    zero = jnp.zeros((8, 128), F32)
    start_sums = lax.fori_loop(0, BLOCKS, start_values, (zero,) * CASES)


    def send_restricted(k):
        out = dot(e_turn[...], lb[...])
        s1[k] = (out[:, 0:128] + out[:, 128:256]).reshape(NS, 8, 128)
        for off in range(1, NS):
            who = at_str(off)
            remote(s1.at[k, who[0]], r1.at[k, s], send_sem.at[k, 0], recv_sem.at[k, 0], who).start()
        r1[k, s] = s1[k, s]

    def send_chunk(k, scalars):
        arrived(r1.at[k, 0 : NS - 1], recv_sem.at[k, 0])
        s2[k, 0:8, :] = jnp.sum(r1[k], axis=0)
        s2[k, 8:16, :] = scalars
        for off in range(1, NC):
            remote(s2.at[k], r2.at[k, c], send_sem.at[k, 1], recv_sem.at[k, 1], at_crs(off)).start()
        r2[k, c] = s2[k]

    def send_product(k):
        arrived(r2.at[k, 0 : NC - 1], recv_sem.at[k, 1])
        total = jnp.sum(r2[k], axis=0)
        t = total[0:8]
        t_tile[...] = t
        placed = jnp.concatenate([jnp.broadcast_to(t[i : i + 1], (ROWS, 128)) * spot for i in range(NC)], axis=0)
        high, low = halves(placed)
        both = dot(jnp.concatenate([high, low], axis=0), ones_pair[0:128, :]).astype(BF16)
        right = jnp.concatenate([both[0:256], both[256:512]], axis=1)
        out = dot(a_high[...], right)
        out = out[:, 0:128] + out[:, 128:256] + dot(a_low[...], both[0:256])
        y = jnp.sum(out.reshape(16, ROWS, 128) * spot[None], axis=1)
        s3[k, 0:16, :] = y
        own = t_tile[pl.ds(c, 1), :]
        s3[k, 16:24, :] = jnp.where(sub8 == 0, jnp.broadcast_to(own, (8, 128)), total[8:16])
        for off in range(1, NS):
            remote(s3.at[k], r3.at[k, s], send_sem.at[k, 2], recv_sem.at[k, 2], at_str(off)).start()
        r3[k, s] = s3[k]

    RZ, RR, ALPHA, BETA, RQ, QQ = range(6)

    def row(x, i):
        return jnp.broadcast_to(x[i : i + 1], (8, 128))

    def send_correction(k):
        arrived(r3.at[k, 0 : NS - 1], recv_sem.at[k, 2])
        total = jnp.sum(r3[k], axis=0)
        y = total[0:16]
        t = jnp.concatenate([r3[k, i, 16:17, :] for i in range(NS)], axis=0)
        sums = total[16:24]
        if k == 0:
            state[RR] = row(sums, 1)
        else:
            alpha = state[RZ] / row(sums, 1)
            state[ALPHA] = alpha
            state[QQ] = row(sums, 2)
            state[RQ] = row(sums, 3)
            y = y_now[...] - alpha[0:1] * y
            t = t_now[...] - alpha[0:1] * t
        y_now[...] = y
        t_now[...] = t
        s4[k, 0:16, :] = y
        s4[k, 16:24, :] = jnp.broadcast_to(jnp.sum(y * t, axis=0, keepdims=True), (8, 128))
        for off in range(1, NC):
            remote(s4.at[k], r4.at[k, c], send_sem.at[k, 3], recv_sem.at[k, 3], at_crs(off)).start()
        r4[k, c] = s4[k]

    def to_cases(slot, x):
        for case in range(CASES):
            per_case[slot, case] = jnp.broadcast_to(x[:, case * 32 : case * 32 + 1], (8, 128))

    def receive_correction(k):
        arrived(r4.at[k, 0 : NC - 1], recv_sem.at[k, 3])
        correction = jnp.concatenate([r4[k, i, 0:16, :] for i in range(NC)], axis=0)
        high, low = halves(correction)
        picked = dot(e_low[...], jnp.concatenate([high, low], axis=1))
        mask = m_high[...]
        gm[:, 0:128] = (picked[:, 0:128] * mask).astype(BF16)
        gm[:, 128:256] = (picked[:, 128:256] * mask).astype(BF16)
        cb[...] = dot(gm[...], ones_pair[...])
        coarse = case_sums(jnp.sum(r4[k, :, 16:24, :], axis=0))
        if k == 0:
            state[RZ] = state[RR] + coarse
        else:
            alpha = state[ALPHA]
            smooth = state[RR] - 2.0 * alpha * state[RQ] + alpha * alpha * state[QQ]
            fresh = smooth + coarse
            state[RR] = smooth
            state[BETA] = fresh / state[RZ]
            state[RZ] = fresh
            to_cases(0, alpha)
            to_cases(1, state[BETA])

    def block_level(k):
        alpha = state[ALPHA][0:1]
        beta = state[BETA][0:1]

        def body(j, _):
            base = pl.multiple_of((j + 1) * STEP, 8)
            flat = pl.ds(pl.multiple_of(j * ROWS, ROWS), ROWS)
            value = bu[flat, :]
            if k:
                value = value - alpha * bw[flat, :]
                bu[flat, :] = value
                value = value + beta * bq[flat, :]
            value = (
                value
                + sd[flat, :] * cb[pl.ds(base, ROWS), :]
                - ss[flat, :] * cb[pl.ds(base + 1, ROWS), :]
                - su[flat, :] * cb[pl.ds(base - 1, ROWS), :]
                - er[flat, :] * cb[pl.ds(base + STEP, ROWS), :]
                - el[flat, :] * cb[pl.ds(base - STEP, ROWS), :]
            )
            bq[flat, :] = value
            to_scatter(j, base, value)
            return 0

        lax.fori_loop(0, BLOCKS, body, 0)


    def widen_correction():
        wide = dot(gm[...], ones_wide[...])
        for case in range(CASES):
            pcf[case * FIELD : case * FIELD + FIELD, :] = wide[:, case * 128 : case * 128 + 128]

    def next_direction(k):
        widen_correction()

        def body(j, sums):
            base = pl.multiple_of((j + 1) * STEP, 8)
            link = links(j, base)
            out = []
            for case in range(CASES):
                at = pl.ds(case * FIELD + base, ROWS)
                here, image = jacobian(pcf, case, base, link)
                rest = rf[at, :]
                inverse = inf[at, :]
                image = image + uf[at, :]
                if k:
                    alpha = per_case[0, case][0:1]
                    beta = per_case[1, case][0:1]
                    last_image = qf[at, :]
                    last_direction = df[at, :]
                    change = alpha * wf[at, :]
                    uf[at, :] = uf[at, :] - change
                    image = image - change + beta * last_image
                    rest = rest - alpha * last_image
                    rf[at, :] = rest
                    step = alpha * last_direction
                    xf[at, :] = step if k == 1 else xf[at, :] + step
                direction = rest * inverse + here
                if k:
                    direction = direction + beta * last_direction
                qf[at, :] = image
                df[at, :] = direction
                out.append(sums[3 * case] + fold(direction * image))
                if k < SOLVES - 1:
                    scaled = image * inverse
                    ef[at, :] = scaled
                    out.append(sums[3 * case + 1] + fold(image * scaled))
                    out.append(sums[3 * case + 2] + fold(rest * scaled))
                else:
                    out.extend([sums[3 * case + 1], sums[3 * case + 2]])
            return tuple(out)

        sums = lax.fori_loop(0, BLOCKS, body, (zero,) * (3 * CASES))
        tile = zero
        for kind in range(3 if k < SOLVES - 1 else 1):
            one = by_case([sums[3 * case + kind] for case in range(CASES)])
            tile = jnp.where(sub8 == kind + 1, one, tile)
        return tile

    def start_halo(k):
        edges_out(ef, hu_s.at[k], hd_s.at[k], hl_s.at[k], hr_s.at[k])
        bufs = [ref.at[k] for ref in (hu_s, hd_s, hl_s, hr_s, hd_r, hu_r, hl_r, hr_r)]
        return exchange(bufs, halo_send.at[k], halo_recv.at[k])

    def apply_scaled(k, copies, target, sums_to):
        for copy in copies:
            copy.wait()
        edges_in(ef, hd_r.at[k], hu_r.at[k], hl_r.at[k], hr_r.at[k])

        def body(j, _):
            base = pl.multiple_of((j + 1) * STEP, 8)
            link = links(j, base)
            values = []
            for case in range(CASES):
                _, image = jacobian(ef, case, base, link)
                target[pl.ds(case * FIELD + base, ROWS), :] = image
                values.append(image)
            block_columns(j, base, values, sums_to)
            return 0

        lax.fori_loop(0, BLOCKS, body, 0)


    send_restricted(0)

    def scaled_rest(j, _):
        base = pl.multiple_of((j + 1) * STEP, 8)
        for case in range(CASES):
            at = pl.ds(case * FIELD + base, ROWS)
            ef[at, :] = qf[at, :]
        return 0

    lax.fori_loop(0, BLOCKS, scaled_rest, 0)
    tile = jnp.where(sub8 == 1, by_case(start_sums), zero)
    copies = start_halo(0)
    send_chunk(0, tile)
    apply_scaled(0, copies, uf, bu)
    send_product(0)
    send_correction(0)
    receive_correction(0)
    for k in range(1, SOLVES):
        block_level(k - 1)
        send_restricted(k)
        tile = next_direction(k - 1)
        copies = start_halo(k)
        send_chunk(k, tile)
        send_product(k)
        apply_scaled(k, copies, wf, bw)
        send_correction(k)
        receive_correction(k)


    f1s[...] = next_direction(SOLVES - 1)
    for off in range(1, NS):
        remote(f1s, f1r.at[s], last_send.at[0], last_recv.at[0], at_str(off)).start()
    f1r[s] = f1s[...]
    arrived(f1r.at[0 : NS - 1], last_recv.at[0])
    f2s[...] = jnp.sum(f1r[...], axis=0)
    for off in range(1, NC):
        remote(f2s, f2r.at[c], last_send.at[1], last_recv.at[1], at_crs(off)).start()
    f2r[c] = f2s[...]
    arrived(f2r.at[0 : NC - 1], last_recv.at[1])
    alpha = state[RZ] / row(jnp.sum(f2r[...], axis=0), 1)
    to_cases(0, alpha)

    stores = []
    for case in range(CASES):

        def finish(j, _, case=case):
            base = pl.multiple_of((j + 1) * STEP, 8)
            cols = pl.ds(pl.multiple_of(j * 128, 128), 128)
            at = pl.ds(case * FIELD + base, ROWS)
            last = per_case[0, case][0:1]
            vn[case, :, cols] = xf[at, :] + last * df[at, :]
            pn[case, :, cols] = rf[at, :] - last * qf[at, :]
            return 0

        lax.fori_loop(0, BLOCKS, finish, 0)
        for number, (src, dst) in enumerate(((vn, step_out), (pn, rest_out))):
            copy = pltpu.make_async_copy(src.at[case], dst.at[case], out_sem.at[number, case])
            copy.start()
            stores.append(copy)


    for k in range(SOLVES):
        arrived(r1.at[k, 0 : NS - 1], send_sem.at[k, 0])
        arrived(r2.at[k, 0 : NC - 1], send_sem.at[k, 1])
        arrived(r3.at[k, 0 : NS - 1], send_sem.at[k, 2])
        arrived(r4.at[k, 0 : NC - 1], send_sem.at[k, 3])
    arrived(f1r.at[0 : NS - 1], last_send.at[0])
    arrived(f2r.at[0 : NC - 1], last_send.at[1])
    for copy in stores:
        copy.wait()


def shards(*args):
    field = (CASES * FIELD, 128)
    flat = (BLOCKS * ROWS, 128)

    def vmem(shape, dtype=F32):
        return pltpu.VMEM(shape, dtype)

    dma = pltpu.SemaphoreType.DMA
    scratch = [
        vmem((CASES, ROWS, 2048)), vmem((CASES, ROWS, 2048)), vmem((ROWS, 2048)), vmem((ROWS, 2048)),
        vmem((ROWS, BLOCKS), jnp.int32), vmem((ROWS, BLOCKS), jnp.int32), vmem((ROWS, BLOCKS), jnp.int32),
        vmem((NC, 512, 128)), vmem((512, 256), BF16), vmem((512, 256), BF16),
        *[vmem(field) for _ in range(10)],
        vmem((FIELD, 128)), vmem(flat), vmem(flat), vmem(flat),
        vmem((FIELD, 128)), vmem((FIELD, 256), BF16), vmem((FIELD, 128), BF16), vmem((FIELD, 128)),
        vmem((FIELD, 128), jnp.int32), vmem((128, 512), BF16), vmem((256, 128), BF16), vmem((256, 512), BF16),
        *[vmem(flat) for _ in range(8)], vmem((512, 256), BF16),
        vmem((ROWS, 128)),
        vmem((72, 128)), vmem((88, 128)), vmem((40, 128)), vmem((40, 128)),
        vmem((72, 128)), vmem((88, 128)), vmem((40, 128)), vmem((40, 128)),
        vmem((SOLVES, 64, 128)), vmem((SOLVES, 64, 128)), vmem((SOLVES, 8, 128)), vmem((SOLVES, 8, 128)),
        vmem((SOLVES, 64, 128)), vmem((SOLVES, 64, 128)), vmem((SOLVES, 8, 128)), vmem((SOLVES, 8, 128)),
        vmem((SOLVES, NS, 8, 128)), vmem((SOLVES, NS, 8, 128)),
        vmem((SOLVES, 16, 128)), vmem((SOLVES, NC, 16, 128)),
        vmem((SOLVES, 24, 128)), vmem((SOLVES, NS, 24, 128)),
        vmem((SOLVES, 24, 128)), vmem((SOLVES, NC, 24, 128)),
        vmem((8, 128)), vmem((NS, 8, 128)), vmem((8, 128)), vmem((NC, 8, 128)),
        vmem((16, 128)), vmem((16, 128)), vmem((8, 128)), vmem((6, 8, 128)), vmem((2, CASES, 8, 128)),
        dma((15,)), dma((2, CASES)), dma((4,)), dma((4,)), dma((SOLVES, 4)), dma((SOLVES, 4)),
        dma((SOLVES, 4)), dma((SOLVES, 4)), dma((2,)), dma((2,)),
    ]
    return pl.pallas_call(
        kernel,
        out_shape=[jax.ShapeDtypeStruct((CASES, ROWS, 2048), F32)] * 2,
        in_specs=[pl.BlockSpec(memory_space=pl.ANY)] * 8,
        out_specs=[pl.BlockSpec(memory_space=pl.ANY)] * 2,
        scratch_shapes=scratch,
        compiler_params=pltpu.CompilerParams(collective_id=0, has_side_effects=True, vmem_limit_bytes=50 * 2**20),
        name="newton",
    )(*args)


def solution(mesh):
    field = P(None, "str", "crs")
    plane = P("str", "crs")
    return jax.shard_map(
        shards,
        mesh=mesh,
        in_specs=(field, field, plane, plane, plane, plane, plane, P("crs", None)),
        out_specs=(field, field),
        check_vma=False,
    )
```

```python
import itertools

import jax
import jax.numpy as jnp
from jax import lax
from jax.experimental import pallas as pl
from jax.experimental.pallas import tpu as pltpu
from jax.sharding import PartitionSpec as P

MESH = pl.DeviceIdType.MESH
F32 = jnp.float32
BF16 = jnp.bfloat16

CASES = 4
ROWS = 32
BLOCKS = 16
STEP = 40
FIELD = (BLOCKS + 2) * STEP
NS = 16
NC = 8
SOLVES = 3
LEVELS = (0.25, 0.5, 1.0, 2.0)


def dot(a, b):
    return jnp.dot(a, b, preferred_element_type=F32)


def halves(x):
    high = x.astype(BF16)
    return high, (x - high.astype(F32)).astype(BF16)


def kernel(
    v_in, photo_in, shunt_in, series_in, pattern_in, mask_in, group_in, inverse_in,
    xf_out, df_out, rf_out, qf_out, alpha_out,
    vn, pn, shn, sn, patn, maskn, groupn, staged, a_high, a_low,
    ef, rf, qf, df, xf, uf, wf, dgf, inf, pcf,
    sf, rlf, llf, dmf,
    cb, gm, e_low, m_high, groups, e_turn, ones_pair, ones_wide,
    bu, bw, bq, sd, ss, su, er, el, lb,
    pk, turned, su_s, sd_s, sl_s, sr_s, su_r, sd_r, sl_r, sr_r,
    hu_s, hd_s, hl_s, hr_s, hu_r, hd_r, hl_r, hr_r,
    s1, r1, s2, r2, s3, r3, s4, r4, fs, fr,
    y_now, t_now, t_tile, state, per_case, local,
    in_sem, setup_send, setup_recv, halo_send, halo_recv, send_sem, recv_sem, last_send, last_recv,
):
    s = lax.axis_index("str")
    c = lax.axis_index("crs")

    def at_str(k):
        return (lax.rem(s + k, NS), c)

    def at_crs(k):
        return (s, lax.rem(c + k, NC))

    str_at = {}
    for key in itertools.product(range(2), range(4), range(2)):
        x_lo, y, core = (lax.rem(p + k, n) for p, k, n in zip((s // 8, lax.rem(s // 2, 4), lax.rem(s, 2)), key, (2, 4, 2)))
        str_at[key] = (x_lo * 4 + y) * 2 + core
    crs_at = {}
    for key in itertools.product(range(2), range(4)):
        x_hi, z = (lax.rem(p + k, n) for p, k, n in zip((c // 4, lax.rem(c, 4)), key, (2, 4)))
        crs_at[key] = x_hi * 4 + z

    def far_first(key):
        x_lo, y, core, x_hi, z = key
        across = 1 if x_lo else 2 * x_hi
        return -(across + min(y, 4 - y) + min(z, 4 - z) + 0.5 * core)

    everyone = sorted(itertools.product(range(2), range(4), range(2), range(2), range(4)), key=far_first)[:-1]
    everyone = [(key, (str_at[key[:3]], crs_at[key[3:]])) for key in everyone]
    str_peers = [(who[0], c) for key, who in everyone if key[3:] == (0, 0)]
    crs_peers = [(s, who[1]) for key, who in everyone if key[:3] == (0, 0, 0)]

    barrier = pltpu.get_barrier_semaphore()
    for who in str_peers + crs_peers:
        pl.semaphore_signal(barrier, inc=1, device_id=who, device_id_type=MESH)

    loads = [
        pltpu.make_async_copy(v_in, vn, in_sem.at[0]),
        pltpu.make_async_copy(series_in, sn, in_sem.at[1]),
        pltpu.make_async_copy(pattern_in, patn, in_sem.at[2]),
        pltpu.make_async_copy(mask_in, maskn, in_sem.at[3]),
        pltpu.make_async_copy(group_in, groupn, in_sem.at[4]),
        pltpu.make_async_copy(shunt_in, shn, in_sem.at[5]),
        pltpu.make_async_copy(photo_in, pn, in_sem.at[6]),
    ]
    quarter = pl.multiple_of((s // 4) * 128, 128)
    for k in range(NC):
        loads.append(
            pltpu.make_async_copy(
                inverse_in.at[:, pl.ds(pl.multiple_of(k * 512 + quarter, 128), 128)], staged.at[k], in_sem.at[7 + k]
            )
        )
    for copy in loads:
        copy.start()

    lane = lax.broadcasted_iota(jnp.int32, (ROWS, 128), 1)
    case_of = lane // 32
    is_first = lane == 0
    is_last = lane == 127
    case8 = case_of[0:8]
    sub8 = lax.broadcasted_iota(jnp.int32, (8, 128), 0)
    spot = (lax.broadcasted_iota(jnp.int32, (ROWS, 128), 0) == lane - 32 * case_of).astype(F32)

    def remote(src, dst, send, recv, who):
        return pltpu.make_async_remote_copy(
            src_ref=src, dst_ref=dst, send_sem=send, recv_sem=recv, device_id=who, device_id_type=MESH
        )

    def arrived(ref, sem):
        pltpu.make_async_copy(ref, ref, sem).wait()

    def rows_of(case, row):
        return pl.ds(case * FIELD + STEP + row, BLOCKS, stride=STEP)

    def edges_out(f, up, down, left, right):
        for case in range(CASES):
            up[case * 16 : case * 16 + 16, :] = f[rows_of(case, 0), :]
            down[case * 16 : case * 16 + 16, :] = f[rows_of(case, ROWS - 1), :]
        for block, ref in ((0, left), (BLOCKS - 1, right)):
            first = (block + 1) * STEP
            tile = jnp.concatenate(
                [f[case * FIELD + first : case * FIELD + first + ROWS, :] for case in range(CASES)], axis=0
            ).T
            ref[0:8, :] = tile[0:8] if block == 0 else tile[120:128]

    def edges_in(f, above, below, left, right):
        for case in range(CASES):
            f[rows_of(case, -1), :] = above[case * 16 : case * 16 + 16, :]
            f[rows_of(case, ROWS), :] = below[case * 16 : case * 16 + 16, :]
        for first, row in ((0, left[7:8, :]), (17 * STEP, right[0:1, :])):
            tile = jnp.broadcast_to(row, (128, 128)).T
            for case in range(CASES):
                f[case * FIELD + first : case * FIELD + first + ROWS, :] = tile[case * ROWS : case * ROWS + ROWS]

    def exchange(bufs, send, recv):
        up_s, down_s, left_s, right_s, above_r, below_r, left_r, right_r = bufs
        copies = [
            remote(up_s, below_r, send.at[0], recv.at[0], at_str(NS - 1)),
            remote(down_s, above_r, send.at[1], recv.at[1], at_str(1)),
            remote(left_s, right_r, send.at[2], recv.at[2], at_crs(NC - 1)),
            remote(right_s, left_r, send.at[3], recv.at[3], at_crs(1)),
        ]
        for copy in copies:
            copy.start()
        return copies

    def neighbours(f, case, base):
        def part(shift):
            return f[pl.ds(case * FIELD + base + shift, ROWS), :]

        here = part(0)
        right = pltpu.roll(jnp.where(is_first, part(STEP), here), 127, 1)
        left = pltpu.roll(jnp.where(is_last, part(-STEP), here), 1, 1)
        return here, part(1), part(-1), right, left

    def links(j, base):
        flat = pl.ds(pl.multiple_of(j * ROWS, ROWS), ROWS)
        return sf[pl.ds(base, ROWS), :], sf[pl.ds(base - 1, ROWS), :], rlf[flat, :], llf[flat, :]

    def jacobian(f, case, base, link):
        down, up, right_link, left_link = link
        here, below, above, right, left = neighbours(f, case, base)
        diagonal = dgf[pl.ds(case * FIELD + base, ROWS), :]
        return here, diagonal * here - down * below - up * above - right_link * right - left_link * left

    def fold(x):
        return x[0:8] + x[8:16] + x[16:24] + x[24:32]

    def by_case(parts):
        total = jnp.zeros((8, 128), F32)
        for case in range(CASES):
            total = jnp.where(case8 == case, jnp.sum(parts[case], axis=(0, 1), keepdims=True), total)
        return total

    def case_sums(x):
        total = jnp.zeros((8, 128), F32)
        for case in range(CASES):
            one = jnp.sum(jnp.where(case8 == case, x, 0.0), axis=1, keepdims=True)
            total = jnp.where(case8 == case, one, total)
        return total


    def spread(x, column, rows=ROWS):
        return jnp.broadcast_to(x[:, column : column + 1], (rows, 128))

    for copy in loads[:5]:
        copy.wait()
    level = jnp.zeros((BLOCKS, ROWS), F32)
    for number in range(4):
        level = level + jnp.where(patn[...] == number, F32(LEVELS[number]), F32(0.0))
    turned[...] = jnp.zeros_like(turned)
    turned[0:16, 0:32] = groupn[...].astype(F32)
    turned[16:32, 0:32] = level
    turned[32:48, 0:32] = maskn[...].astype(F32) * 0.5
    pk[...] = turned[...].T[0:ROWS]
    packed = pk[...]

    def lay_out(j, _):
        base = pl.multiple_of((j + 1) * STEP, 8)
        cols = pl.ds(pl.multiple_of(j * 128, 128), 128)
        for case in range(CASES):
            ef[pl.ds(case * FIELD + base, ROWS), :] = vn[case, :, cols]
        sf[pl.ds(base, ROWS), :] = sn[:, cols]
        return 0

    lax.fori_loop(0, BLOCKS, lay_out, 0)
    edges_out(ef, su_s, sd_s, sl_s, sr_s)
    su_s[64:72, :] = packed[0:8]
    sd_s[64:72, :] = packed[24:32]
    sd_s[72:88, :] = sf[pl.ds(STEP + ROWS - 1, BLOCKS, stride=STEP), :]
    sl_s[1:2, :] = turned[0:1, :]
    sl_s[2:3, :] = turned[16:17, :]
    sr_s[1:2, :] = turned[15:16, :]
    sr_s[2:3, :] = turned[31:32, :]

    pl.semaphore_wait(barrier, NS - 1 + NC - 1)
    setup_copies = exchange((su_s, sd_s, sl_s, sr_s, sd_r, su_r, sl_r, sr_r), setup_send, setup_recv)

    groups[...] = jnp.zeros_like(groups)
    for j in range(BLOCKS):
        base = (j + 1) * STEP
        group = spread(packed, j).astype(jnp.int32)
        groups[base : base + ROWS, :] = group
        low = group // 32
        code = (low % 16) * 8 + low // 16
        lb[j * ROWS : j * ROWS + ROWS, 0:128] = (lane == code).astype(F32).astype(BF16)
        dmf[j * ROWS : j * ROWS + ROWS, :] = spread(packed, 32 + j)
    for k in range(4):
        e_turn[:, k * 128 : k * 128 + 128] = lb[k * 128 : k * 128 + 128, 0:128].astype(F32).T.astype(BF16)

    same = lax.broadcasted_iota(jnp.int32, (128, 128), 0) // 32
    across = lax.broadcasted_iota(jnp.int32, (128, 128), 1) // 32
    block_ones = (same == across).astype(F32).astype(BF16)
    ones_pair[0:128, :] = block_ones
    ones_pair[128:256, :] = block_ones
    for case in range(CASES):
        wide = (same == case).astype(F32).astype(BF16)
        ones_wide[0:128, case * 128 : case * 128 + 128] = wide
        ones_wide[128:256, case * 128 : case * 128 + 128] = wide

    for copy in loads[7:]:
        copy.wait()

    def pick(i, _):
        rows = pl.ds(pl.multiple_of(i * 32, 32), 32)
        for side in range(2):
            block = jnp.zeros((ROWS, 128), F32)
            for k in range(4):
                turn = lax.rem(32 * k + 128 - 32 * lax.rem(s, 4), 128)
                block = jnp.where(case_of == k, pltpu.roll(staged[side * 4 + k, rows, :], turn, 1), block)
            high, low = halves(block)
            a_high[rows, side * 128 : side * 128 + 128] = high
            a_low[rows, side * 128 : side * 128 + 128] = low
        return 0

    lax.fori_loop(0, 16, pick, 0)
    for copy in loads[5:7]:
        copy.wait()


    for copy in setup_copies:
        copy.wait()
    edges_in(ef, sd_r, su_r, sl_r, sr_r)
    sf[pl.ds(STEP - 1, BLOCKS, stride=STEP), :] = sd_r[72:88, :]
    above8 = sd_r[64:72, :]
    below8 = su_r[64:72, :]
    for j in range(BLOCKS):
        base = (j + 1) * STEP
        groups[base - 1 : base, :] = spread(above8, j, 8)[7:8].astype(jnp.int32)
        groups[base + ROWS : base + ROWS + 1, :] = spread(below8, j, 8)[0:1].astype(jnp.int32)
    packed_left = jnp.broadcast_to(sl_r[1:2, :], (128, 128)).T[0:ROWS]
    packed_right = jnp.broadcast_to(sr_r[1:2, :], (128, 128)).T[0:ROWS]
    groups[0:ROWS, :] = packed_left.astype(jnp.int32)
    groups[17 * STEP : 17 * STEP + ROWS, :] = packed_right.astype(jnp.int32)
    level_left = jnp.broadcast_to(sl_r[2:3, :], (128, 128)).T[0:ROWS]
    level_right = jnp.broadcast_to(sr_r[2:3, :], (128, 128)).T[0:ROWS]

    open_left = jnp.where(c == 0, 0.0, 1.0).astype(F32)
    open_right = jnp.where(c == NC - 1, 0.0, 1.0).astype(F32)
    row_levels = (
        [level_left] + [spread(packed, 16 + j) for j in range(BLOCKS)] + [level_right]
    )
    for j in range(BLOCKS):
        here = row_levels[j + 1]
        right = jnp.minimum(here, row_levels[j + 2])
        left = jnp.minimum(here, row_levels[j])
        if j == BLOCKS - 1:
            right = right * open_right
        if j == 0:
            left = left * open_left
        rlf[j * ROWS : j * ROWS + ROWS, :] = jnp.where(is_last, right, here)
        llf[j * ROWS : j * ROWS + ROWS, :] = jnp.where(is_first, left, here)
        er[j * ROWS : j * ROWS + ROWS, :] = right
        el[j * ROWS : j * ROWS + ROWS, :] = left

    def block_columns(j, base, sums, target):
        total = jnp.zeros((ROWS, 128), F32)
        for case in range(CASES):
            total = jnp.where(case_of == case, jnp.sum(sums[case], axis=1, keepdims=True), total)
        if target is not None:
            target[pl.ds(pl.multiple_of(j * ROWS, ROWS), ROWS), :] = total
        return total

    def to_scatter(j, base, total):
        flat = pl.ds(pl.multiple_of(j * ROWS, ROWS), ROWS)
        high, low = halves(total * m_high[pl.ds(base, ROWS), :])
        lb[flat, 0:128] = high
        lb[flat, 128:256] = low

    def codes(i, _):
        rows = pl.ds(pl.multiple_of(i * 80, 16), 80)
        group = groups[rows, :]
        lanes = lax.broadcasted_iota(jnp.int32, (80, 128), 1)
        e_low[rows, :] = (lanes == group // 32).astype(F32).astype(BF16)
        m_high[rows, :] = (lanes % 32 == group % 32).astype(F32)
        return 0

    lax.fori_loop(0, FIELD // 80, codes, 0)

    def start_rest(j, _):
        base = pl.multiple_of((j + 1) * STEP, 8)
        cols = pl.ds(pl.multiple_of(j * 128, 128), 128)
        flat = pl.ds(pl.multiple_of(j * ROWS, ROWS), ROWS)
        down, up, right_link, left_link = links(j, base)
        shunt = shn[:, cols]
        half = dmf[flat, :]
        rests = []
        for case in range(CASES):
            at = pl.ds(case * FIELD + base, ROWS)
            here, below, above, right, left = neighbours(ef, case, base)
            slope = half * jnp.exp(here)
            rest = pn[case, :, cols] - (
                shunt * here
                + down * (here - below)
                + up * (here - above)
                + right_link * (here - right)
                + left_link * (here - left)
                + slope
                - half
            )
            dgf[at, :] = slope
            rf[at, :] = rest
            rests.append(rest)
        to_scatter(j, base, block_columns(j, base, rests, None))
        return 0

    def start_scaled(j, sums):
        base = pl.multiple_of((j + 1) * STEP, 8)
        cols = pl.ds(pl.multiple_of(j * 128, 128), 128)
        flat = pl.ds(pl.multiple_of(j * ROWS, ROWS), ROWS)
        down, up, right_link, left_link = links(j, base)
        shunt = shn[:, cols]
        edge = jnp.where(is_last, right_link, 0.0) + jnp.where(is_first, left_link, 0.0)
        out, plain = [], []
        for case in range(CASES):
            at = pl.ds(case * FIELD + base, ROWS)
            ground = shunt + dgf[at, :] + down + up
            diagonal = ground + right_link + left_link
            inverse = 1.0 / diagonal
            rest = rf[at, :]
            scaled = rest * inverse
            dgf[at, :] = diagonal
            inf[at, :] = inverse
            ef[at, :] = scaled
            out.append(sums[case] + fold(rest * scaled))
            plain.append(ground + edge)
        block_columns(j, base, plain, sd)
        ss[flat, :] = jnp.broadcast_to(jnp.sum(down, axis=1, keepdims=True), (ROWS, 128))
        su[flat, :] = jnp.broadcast_to(jnp.sum(up, axis=1, keepdims=True), (ROWS, 128))
        return tuple(out)

    zero = jnp.zeros((8, 128), F32)
    lax.fori_loop(0, BLOCKS, start_rest, 0)


    def send_restricted(k):
        out = dot(e_turn[...], lb[...])
        s1[k] = (out[:, 0:128] + out[:, 128:256]).reshape(NS, 8, 128)
        for who in str_peers:
            remote(s1.at[k, who[0]], r1.at[k, s], send_sem.at[k, 0], recv_sem.at[k, 0], who).start()
        r1[k, s] = s1[k, s]

    def send_chunk(k, scalars):
        arrived(r1.at[k, 0 : NS - 1], recv_sem.at[k, 0])
        s2[k, 0:8, :] = jnp.sum(r1[k], axis=0)
        s2[k, 8:16, :] = scalars
        for who in crs_peers:
            remote(s2.at[k], r2.at[k, c], send_sem.at[k, 1], recv_sem.at[k, 1], who).start()
        r2[k, c] = s2[k]

    def send_product(k):
        arrived(r2.at[k, 0 : NC - 1], recv_sem.at[k, 1])
        total = jnp.sum(r2[k], axis=0)
        t = total[0:8]
        t_tile[...] = t
        placed = jnp.concatenate([jnp.broadcast_to(t[i : i + 1], (ROWS, 128)) * spot for i in range(NC)], axis=0)
        high, low = halves(placed)
        both = dot(jnp.concatenate([high, low], axis=0), ones_pair[0:128, :]).astype(BF16)
        right = jnp.concatenate([both[0:256], both[256:512]], axis=1)
        out = dot(a_high[...], right)
        out = out[:, 0:128] + out[:, 128:256] + dot(a_low[...], both[0:256])
        y = jnp.sum(out.reshape(16, ROWS, 128) * spot[None], axis=1)
        s3[k, 0:16, :] = y
        own = t_tile[pl.ds(c, 1), :]
        s3[k, 16:24, :] = jnp.where(sub8 == 0, jnp.broadcast_to(own, (8, 128)), total[8:16])
        for who in str_peers:
            remote(s3.at[k], r3.at[k, s], send_sem.at[k, 2], recv_sem.at[k, 2], who).start()
        r3[k, s] = s3[k]

    RZ, RR, ALPHA, BETA, RQ, QQ = range(6)

    def row(x, i):
        return jnp.broadcast_to(x[i : i + 1], (8, 128))

    def send_correction(k):
        arrived(r3.at[k, 0 : NS - 1], recv_sem.at[k, 2])
        total = jnp.sum(r3[k], axis=0)
        y = total[0:16]
        t = jnp.concatenate([r3[k, i, 16:17, :] for i in range(NS)], axis=0)
        sums = total[16:24]
        if k == 0:
            state[RR] = row(sums, 1)
        else:
            alpha = state[RZ] / row(sums, 1)
            state[ALPHA] = alpha
            state[QQ] = row(sums, 2)
            state[RQ] = row(sums, 3)
            y = y_now[...] - alpha[0:1] * y
            t = t_now[...] - alpha[0:1] * t
        y_now[...] = y
        t_now[...] = t
        s4[k, 0:16, :] = y
        s4[k, 16:24, :] = jnp.broadcast_to(jnp.sum(y * t, axis=0, keepdims=True), (8, 128))
        for who in crs_peers:
            remote(s4.at[k], r4.at[k, c], send_sem.at[k, 3], recv_sem.at[k, 3], who).start()
        r4[k, c] = s4[k]

    def to_cases(slot, x):
        for case in range(CASES):
            per_case[slot, case] = jnp.broadcast_to(x[:, case * 32 : case * 32 + 1], (8, 128))

    def receive_correction(k):
        arrived(r4.at[k, 0 : NC - 1], recv_sem.at[k, 3])
        correction = jnp.concatenate([r4[k, i, 0:16, :] for i in range(NC)], axis=0)
        high, low = halves(correction)
        picked = dot(e_low[...], jnp.concatenate([high, low], axis=1))
        mask = m_high[...]
        gm[:, 0:128] = (picked[:, 0:128] * mask).astype(BF16)
        gm[:, 128:256] = (picked[:, 128:256] * mask).astype(BF16)
        cb[...] = dot(gm[...], ones_pair[...])
        coarse = case_sums(jnp.sum(r4[k, :, 16:24, :], axis=0))
        if k == 0:
            state[RZ] = state[RR] + coarse
        else:
            alpha = state[ALPHA]
            smooth = state[RR] - 2.0 * alpha * state[RQ] + alpha * alpha * state[QQ]
            fresh = smooth + coarse
            state[RR] = smooth
            state[BETA] = fresh / state[RZ]
            state[RZ] = fresh
            to_cases(0, alpha)
            to_cases(1, state[BETA])

    def block_level(k):
        alpha = state[ALPHA][0:1]
        beta = state[BETA][0:1]
        final = k == SOLVES - 1

        def body(j, energy):
            base = pl.multiple_of((j + 1) * STEP, 8)
            flat = pl.ds(pl.multiple_of(j * ROWS, ROWS), ROWS)
            value = bu[flat, :]
            if k:
                value = value - alpha * bw[flat, :]
                if not final:
                    bu[flat, :] = value
                value = value + beta * bq[flat, :]
            here = cb[pl.ds(base, ROWS), :]
            stencil = (
                sd[flat, :] * here
                - ss[flat, :] * cb[pl.ds(base + 1, ROWS), :]
                - su[flat, :] * cb[pl.ds(base - 1, ROWS), :]
                - er[flat, :] * cb[pl.ds(base + STEP, ROWS), :]
                - el[flat, :] * cb[pl.ds(base - STEP, ROWS), :]
            )
            if final:
                return energy + fold(here * (stencil + 2.0 * value))
            value = value + stencil
            bq[flat, :] = value
            to_scatter(j, base, value)
            return energy

        return lax.fori_loop(0, BLOCKS, body, zero)


    def widen_correction():
        wide = dot(gm[...], ones_wide[...])
        for case in range(CASES):
            pcf[case * FIELD : case * FIELD + FIELD, :] = wide[:, case * 128 : case * 128 + 128]

    def next_direction(k):
        widen_correction()
        final = k == SOLVES - 1
        kinds = {0: 3, SOLVES - 2: 5, SOLVES - 1: 0}[k]

        def body(j, sums):
            base = pl.multiple_of((j + 1) * STEP, 8)
            cols = pl.ds(pl.multiple_of(j * 128, 128), 128)
            link = links(j, base)
            out = []
            for case in range(CASES):
                at = pl.ds(case * FIELD + base, ROWS)
                here, image = jacobian(pcf, case, base, link)
                rest = rf[at, :]
                inverse = inf[at, :]
                smooth = uf[at, :]
                if k:
                    alpha = per_case[0, case][0:1]
                    beta = per_case[1, case][0:1]
                    last_image = qf[at, :]
                    last_direction = df[at, :]
                    smooth = smooth - alpha * wf[at, :]
                    image = image + beta * last_image
                    rest = rest - alpha * last_image
                    step = alpha * last_direction
                    if k > 1:
                        step = step + xf[at, :]
                image = image + smooth
                direction = rest * inverse + here
                if k:
                    direction = direction + beta * last_direction
                if final:
                    xf_out[case, :, cols] = step
                    rf_out[case, :, cols] = rest
                    df_out[case, :, cols] = direction
                    qf_out[case, :, cols] = image
                    continue
                if k:
                    uf[at, :] = smooth
                    rf[at, :] = rest
                    xf[at, :] = step
                qf[at, :] = image
                df[at, :] = direction
                scaled = image * inverse
                ef[at, :] = scaled
                terms = [direction * image, image * scaled, rest * scaled, rest * inverse * smooth, scaled * smooth]
                out.extend(sums[kinds * case + i] + fold(terms[i]) for i in range(kinds))
            return tuple(out)

        sums = lax.fori_loop(0, BLOCKS, body, (zero,) * (kinds * CASES))
        tile = zero
        for kind in range(kinds):
            one = by_case([sums[kinds * case + kind] for case in range(CASES)])
            tile = jnp.where(sub8 == kind + 1, one, tile)
        return tile

    def start_halo(k):
        edges_out(ef, hu_s.at[k], hd_s.at[k], hl_s.at[k], hr_s.at[k])
        bufs = [ref.at[k] for ref in (hu_s, hd_s, hl_s, hr_s, hd_r, hu_r, hl_r, hr_r)]
        return exchange(bufs, halo_send.at[k], halo_recv.at[k])

    def apply_scaled(k, copies, target, sums_to):
        for copy in copies:
            copy.wait()
        edges_in(ef, hd_r.at[k], hu_r.at[k], hl_r.at[k], hr_r.at[k])

        def body(j, sums):
            base = pl.multiple_of((j + 1) * STEP, 8)
            link = links(j, base)
            values, out = [], []
            for case in range(CASES):
                here, image = jacobian(ef, case, base, link)
                target[pl.ds(case * FIELD + base, ROWS), :] = image
                values.append(image)
                if k == SOLVES - 1:
                    out.append(sums[case] + fold(here * image))
            block_columns(j, base, values, sums_to)
            return tuple(out)

        return lax.fori_loop(0, BLOCKS, body, (zero,) * (CASES if k == SOLVES - 1 else 0))


    send_restricted(0)
    start_sums = lax.fori_loop(0, BLOCKS, start_scaled, (zero,) * CASES)
    tile = jnp.where(sub8 == 1, by_case(start_sums), zero)
    copies = start_halo(0)
    send_chunk(0, tile)
    apply_scaled(0, copies, uf, bu)
    send_product(0)
    send_correction(0)
    receive_correction(0)
    for k in range(1, SOLVES):
        block_level(k - 1)
        send_restricted(k)
        tile = next_direction(k - 1)
        if k == SOLVES - 1:
            local[...] = tile
        copies = start_halo(k)
        send_chunk(k, tile)
        send_product(k)
        scaled_sums = apply_scaled(k, copies, wf, bw)
        send_correction(k)
        receive_correction(k)


    alpha = state[ALPHA]
    beta = state[BETA]
    energy = jnp.sum(block_level(SOLVES - 1), axis=0, keepdims=True)
    dq, qq, rq, eu, qu = (row(local[...], i) for i in range(1, 6))
    energy = (
        energy
        + (eu - 2.0 * alpha * qu + alpha * alpha * by_case(scaled_sums))
        + 2.0 * beta * (rq - alpha * qq)
        + beta * beta * dq
    )
    here = s * NC + c
    fs[...] = energy[0:1]
    for _, who in everyone:
        remote(fs, fr.at[here], last_send.at[0], last_recv.at[0], who).start()
    fr[here] = fs[...]
    next_direction(SOLVES - 1)
    arrived(fr.at[0 : NS * NC - 1], last_recv.at[0])
    alpha = state[RZ] / jnp.broadcast_to(jnp.sum(fr[...], axis=0), (8, 128))
    for case in range(CASES):
        alpha_out[case : case + 1, :] = jnp.broadcast_to(alpha[0:1, case * 32 : case * 32 + 1], (1, 2048))


    for k in range(SOLVES):
        arrived(r1.at[k, 0 : NS - 1], send_sem.at[k, 0])
        arrived(r2.at[k, 0 : NC - 1], send_sem.at[k, 1])
        arrived(r3.at[k, 0 : NS - 1], send_sem.at[k, 2])
        arrived(r4.at[k, 0 : NC - 1], send_sem.at[k, 3])
    arrived(fr.at[0 : NS * NC - 1], last_send.at[0])


def shards(voltage, photocurrent, shunt, series, pattern, diode_mask, aggregate, coarse_inverse):
    field = (CASES * FIELD, 128)
    flat = (BLOCKS * ROWS, 128)

    def vmem(shape, dtype=F32):
        return pltpu.VMEM(shape, dtype)

    dma = pltpu.SemaphoreType.DMA
    scratch = [
        vmem((CASES, ROWS, 2048)), vmem((CASES, ROWS, 2048)), vmem((ROWS, 2048)), vmem((ROWS, 2048)),
        vmem((BLOCKS, ROWS), jnp.int32), vmem((BLOCKS, ROWS), jnp.int32), vmem((BLOCKS, ROWS), jnp.int32),
        vmem((NC, 512, 128)), vmem((512, 256), BF16), vmem((512, 256), BF16),
        *[vmem(field) for _ in range(10)],
        vmem((FIELD, 128)), vmem(flat), vmem(flat), vmem(flat),
        vmem((FIELD, 128)), vmem((FIELD, 256), BF16), vmem((FIELD, 128), BF16), vmem((FIELD, 128)),
        vmem((FIELD, 128), jnp.int32), vmem((128, 512), BF16), vmem((256, 128), BF16), vmem((256, 512), BF16),
        *[vmem(flat) for _ in range(8)], vmem((512, 256), BF16),
        vmem((ROWS, 128)), vmem((128, 128)),
        vmem((72, 128)), vmem((88, 128)), vmem((8, 128)), vmem((8, 128)),
        vmem((72, 128)), vmem((88, 128)), vmem((8, 128)), vmem((8, 128)),
        vmem((SOLVES, 64, 128)), vmem((SOLVES, 64, 128)), vmem((SOLVES, 8, 128)), vmem((SOLVES, 8, 128)),
        vmem((SOLVES, 64, 128)), vmem((SOLVES, 64, 128)), vmem((SOLVES, 8, 128)), vmem((SOLVES, 8, 128)),
        vmem((SOLVES, NS, 8, 128)), vmem((SOLVES, NS, 8, 128)),
        vmem((SOLVES, 16, 128)), vmem((SOLVES, NC, 16, 128)),
        vmem((SOLVES, 24, 128)), vmem((SOLVES, NS, 24, 128)),
        vmem((SOLVES, 24, 128)), vmem((SOLVES, NC, 24, 128)),
        vmem((1, 128)), vmem((NS * NC, 1, 128)),
        vmem((16, 128)), vmem((16, 128)), vmem((8, 128)), vmem((6, 8, 128)), vmem((2, CASES, 8, 128)), vmem((8, 128)),
        dma((15,)), dma((4,)), dma((4,)), dma((SOLVES, 4)), dma((SOLVES, 4)),
        dma((SOLVES, 4)), dma((SOLVES, 4)), dma((1,)), dma((1,)),
    ]
    tall = jax.ShapeDtypeStruct((CASES, ROWS, 2048), F32)
    step, direction, rest, image, alpha = pl.pallas_call(
        kernel,
        out_shape=[tall] * 4 + [jax.ShapeDtypeStruct((CASES, 2048), F32)],
        in_specs=[pl.BlockSpec(memory_space=pltpu.HBM)] * 8,
        out_specs=[pl.BlockSpec(memory_space=pltpu.VMEM)] * 5,
        scratch_shapes=scratch,
        compiler_params=pltpu.CompilerParams(collective_id=0, has_side_effects=True, vmem_limit_bytes=54 * 2**20),
        name="newton",
    )(voltage, photocurrent, shunt, series, pattern.T, diode_mask.T, aggregate.T, coarse_inverse)
    alpha = alpha[:, None, :]
    return step + alpha * direction, rest - alpha * image


def solution(mesh):
    field = P(None, "str", "crs")
    plane = P("str", "crs")
    return jax.shard_map(
        shards,
        mesh=mesh,
        in_specs=(field, field, plane, plane, plane, plane, plane, P("crs", None)),
        out_specs=(field, field),
        check_vma=False,
    )
```

```python
import itertools

import jax
import jax.numpy as jnp
from jax import lax
from jax.experimental import pallas as pl
from jax.experimental.pallas import tpu as pltpu
from jax.sharding import PartitionSpec as P

MESH = pl.DeviceIdType.MESH
F32 = jnp.float32
BF16 = jnp.bfloat16

CASES = 4
ROWS = 32
BLOCKS = 16
STEP = 40
FIELD = (BLOCKS + 2) * STEP
NS = 16
NC = 8
CHIPS = NS // 2
SOLVES = 3
LEVELS = (0.25, 0.5, 1.0, 2.0)


def dot(a, b):
    return jnp.dot(a, b, preferred_element_type=F32)


def halves(x):
    high = x.astype(BF16)
    return high, (x - high.astype(F32)).astype(BF16)


def kernel(
    v_in, photo_in, shunt_in, series_in, pattern_in, mask_in, group_in, inverse_in,
    xf_out, df_out, rf_out, qf_out, alpha_out,
    vn, pn, shn, sn, patn, maskn, groupn, staged, a_high, a_low,
    ef, rf, qf, df, xf, uf, wf, dgf, inf, pcf,
    sf, rlf, llf, dmf,
    cb, gm, e_low, m_high, groups, e_turn, ones_pair, ones_wide,
    bu, bw, bq, br, sd, ss, su, er, el, lb,
    pk, turned, su_s, sd_s, sl_s, sr_s, su_r, sd_r, sl_r, sr_r,
    hu_s, hd_s, hl_s, hr_s, hu_r, hd_r, hl_r, hr_r,
    s1, r1, s2, r2, s3, r3, s4, r4, fs, fr,
    y_now, t_now, t_tile, state, per_case, local, local_w, sc_s, sc_r,
    in_sem, setup_send, setup_recv, halo_send, halo_recv, send_sem, recv_sem, last_send, last_recv, sc_send, sc_recv,
):
    s = lax.axis_index("str")
    chip = s // 2
    c = lax.axis_index("crs")

    def at_str(k):
        return (lax.rem(s + k, NS), c)

    def at_crs(k):
        return (s, lax.rem(c + k, NC))

    str_at = {}
    for key in itertools.product(range(2), range(4), range(2)):
        x_lo, y, core = (lax.rem(p + k, n) for p, k, n in zip((s // 8, lax.rem(s // 2, 4), lax.rem(s, 2)), key, (2, 4, 2)))
        str_at[key] = (x_lo * 4 + y) * 2 + core
    crs_at = {}
    for key in itertools.product(range(2), range(4)):
        x_hi, z = (lax.rem(p + k, n) for p, k, n in zip((c // 4, lax.rem(c, 4)), key, (2, 4)))
        crs_at[key] = x_hi * 4 + z

    def far_first(key):
        x_lo, y, core, x_hi, z = key
        across = 1 if x_lo else 2 * x_hi
        return -(across + min(y, 4 - y) + min(z, 4 - z) + 0.5 * core)

    everyone = sorted(itertools.product(range(2), range(4), range(2), range(2), range(4)), key=far_first)[:-1]
    everyone = [(key, (str_at[key[:3]], crs_at[key[3:]])) for key in everyone]
    str_peers = [(who[0], c) for key, who in everyone if key[3:] == (0, 0)]
    chip_peers = [(who[0], c) for key, who in everyone if key[2:] == (0, 0, 0)]
    sibling = (str_at[(0, 0, 1)], c)
    crs_peers = [(s, who[1]) for key, who in everyone if key[:3] == (0, 0, 0)]

    barrier = pltpu.get_barrier_semaphore()
    for who in str_peers + crs_peers:
        pl.semaphore_signal(barrier, inc=1, device_id=who, device_id_type=MESH)

    loads = [
        pltpu.make_async_copy(v_in, vn, in_sem.at[0]),
        pltpu.make_async_copy(series_in, sn, in_sem.at[1]),
        pltpu.make_async_copy(pattern_in, patn, in_sem.at[2]),
        pltpu.make_async_copy(mask_in, maskn, in_sem.at[3]),
        pltpu.make_async_copy(group_in, groupn, in_sem.at[4]),
        pltpu.make_async_copy(shunt_in, shn, in_sem.at[5]),
        pltpu.make_async_copy(photo_in, pn, in_sem.at[6]),
    ]
    quarter = pl.multiple_of((chip // 2) * 128, 128)
    for k in range(NC):
        loads.append(
            pltpu.make_async_copy(
                inverse_in.at[:, pl.ds(pl.multiple_of(k * 512 + quarter, 128), 128)], staged.at[k], in_sem.at[7 + k]
            )
        )
    for copy in loads:
        copy.start()

    lane = lax.broadcasted_iota(jnp.int32, (ROWS, 128), 1)
    case_of = lane // 32
    is_first = lane == 0
    is_last = lane == 127
    case8 = case_of[0:8]
    sub8 = lax.broadcasted_iota(jnp.int32, (8, 128), 0)
    spot = (lax.broadcasted_iota(jnp.int32, (ROWS, 128), 0) == lane - 32 * case_of).astype(F32)

    def remote(src, dst, send, recv, who):
        return pltpu.make_async_remote_copy(
            src_ref=src, dst_ref=dst, send_sem=send, recv_sem=recv, device_id=who, device_id_type=MESH
        )

    def arrived(ref, sem):
        pltpu.make_async_copy(ref, ref, sem).wait()

    def rows_of(case, row):
        return pl.ds(case * FIELD + STEP + row, BLOCKS, stride=STEP)

    def edges_out(f, up, down, left, right):
        for case in range(CASES):
            up[case * 16 : case * 16 + 16, :] = f[rows_of(case, 0), :]
            down[case * 16 : case * 16 + 16, :] = f[rows_of(case, ROWS - 1), :]
        for block, ref in ((0, left), (BLOCKS - 1, right)):
            first = (block + 1) * STEP
            tile = jnp.concatenate(
                [f[case * FIELD + first : case * FIELD + first + ROWS, :] for case in range(CASES)], axis=0
            ).T
            ref[0:8, :] = tile[0:8] if block == 0 else tile[120:128]

    def edges_in(f, above, below, left, right):
        for case in range(CASES):
            f[rows_of(case, -1), :] = above[case * 16 : case * 16 + 16, :]
            f[rows_of(case, ROWS), :] = below[case * 16 : case * 16 + 16, :]
        for first, row in ((0, left[7:8, :]), (17 * STEP, right[0:1, :])):
            tile = jnp.broadcast_to(row, (128, 128)).T
            for case in range(CASES):
                f[case * FIELD + first : case * FIELD + first + ROWS, :] = tile[case * ROWS : case * ROWS + ROWS]

    def exchange(bufs, send, recv):
        up_s, down_s, left_s, right_s, above_r, below_r, left_r, right_r = bufs
        copies = [
            remote(up_s, below_r, send.at[0], recv.at[0], at_str(NS - 1)),
            remote(down_s, above_r, send.at[1], recv.at[1], at_str(1)),
            remote(left_s, right_r, send.at[2], recv.at[2], at_crs(NC - 1)),
            remote(right_s, left_r, send.at[3], recv.at[3], at_crs(1)),
        ]
        for copy in copies:
            copy.start()
        return copies

    def neighbours(f, case, base):
        def part(shift):
            return f[pl.ds(case * FIELD + base + shift, ROWS), :]

        here = part(0)
        right = pltpu.roll(jnp.where(is_first, part(STEP), here), 127, 1)
        left = pltpu.roll(jnp.where(is_last, part(-STEP), here), 1, 1)
        return here, part(1), part(-1), right, left

    def links(j, base):
        flat = pl.ds(pl.multiple_of(j * ROWS, ROWS), ROWS)
        return sf[pl.ds(base, ROWS), :], sf[pl.ds(base - 1, ROWS), :], rlf[flat, :], llf[flat, :]

    def jacobian(f, case, base, link):
        down, up, right_link, left_link = link
        here, below, above, right, left = neighbours(f, case, base)
        diagonal = dgf[pl.ds(case * FIELD + base, ROWS), :]
        return here, diagonal * here - down * below - up * above - right_link * right - left_link * left

    def fold(x):
        return x[0:8] + x[8:16] + x[16:24] + x[24:32]

    def by_case(parts):
        total = jnp.zeros((8, 128), F32)
        for case in range(CASES):
            total = jnp.where(case8 == case, jnp.sum(parts[case], axis=(0, 1), keepdims=True), total)
        return total

    def case_sums(x):
        total = jnp.zeros((8, 128), F32)
        for case in range(CASES):
            one = jnp.sum(jnp.where(case8 == case, x, 0.0), axis=1, keepdims=True)
            total = jnp.where(case8 == case, one, total)
        return total


    def spread(x, column, rows=ROWS):
        return jnp.broadcast_to(x[:, column : column + 1], (rows, 128))

    def clear(i, _):
        rows = pl.ds(pl.multiple_of(i * 80, 16), 80)
        for f in (ef, wf, qf, df, xf):
            f[rows, :] = jnp.zeros((80, 128), F32)
        return 0

    lax.fori_loop(0, CASES * FIELD // 80, clear, 0)
    sf[...] = jnp.zeros_like(sf)
    bw[...] = jnp.zeros_like(bw)
    bq[...] = jnp.zeros_like(bq)
    state[...] = jnp.zeros_like(state)
    per_case[...] = jnp.zeros_like(per_case)
    for copy in loads[:5]:
        copy.wait()
    level = jnp.zeros((BLOCKS, ROWS), F32)
    for number in range(4):
        level = level + jnp.where(patn[...] == number, F32(LEVELS[number]), F32(0.0))
    turned[...] = jnp.zeros_like(turned)
    turned[0:16, 0:32] = groupn[...].astype(F32)
    turned[16:32, 0:32] = level
    turned[32:48, 0:32] = maskn[...].astype(F32) * 0.5
    pk[...] = turned[...].T[0:ROWS]
    packed = pk[...]

    def lay_out(j, _):
        base = pl.multiple_of((j + 1) * STEP, 8)
        cols = pl.ds(pl.multiple_of(j * 128, 128), 128)
        for case in range(CASES):
            ef[pl.ds(case * FIELD + base, ROWS), :] = vn[case, :, cols]
        sf[pl.ds(base, ROWS), :] = sn[:, cols]
        return 0

    lax.fori_loop(0, BLOCKS, lay_out, 0)
    edges_out(ef, su_s, sd_s, sl_s, sr_s)
    su_s[64:72, :] = packed[0:8]
    sd_s[64:72, :] = packed[24:32]
    sd_s[72:88, :] = sf[pl.ds(STEP + ROWS - 1, BLOCKS, stride=STEP), :]
    sl_s[1:2, :] = turned[0:1, :]
    sl_s[2:3, :] = turned[16:17, :]
    sr_s[1:2, :] = turned[15:16, :]
    sr_s[2:3, :] = turned[31:32, :]

    pl.semaphore_wait(barrier, NS - 1 + NC - 1)
    setup_copies = exchange((su_s, sd_s, sl_s, sr_s, sd_r, su_r, sl_r, sr_r), setup_send, setup_recv)

    groups[...] = jnp.zeros_like(groups)
    for j in range(BLOCKS):
        base = (j + 1) * STEP
        group = spread(packed, j).astype(jnp.int32)
        groups[base : base + ROWS, :] = group
        low = group // 32
        code = (low % 16) // 2 * 16 + low // 16 * 2 + low % 2
        lb[j * ROWS : j * ROWS + ROWS, 0:128] = (lane == code).astype(F32).astype(BF16)
        dmf[j * ROWS : j * ROWS + ROWS, :] = spread(packed, 32 + j)
    for k in range(4):
        e_turn[:, k * 128 : k * 128 + 128] = lb[k * 128 : k * 128 + 128, 0:128].astype(F32).T.astype(BF16)

    same = lax.broadcasted_iota(jnp.int32, (128, 128), 0) // 32
    across = lax.broadcasted_iota(jnp.int32, (128, 128), 1) // 32
    block_ones = (same == across).astype(F32).astype(BF16)
    ones_pair[0:128, :] = block_ones
    ones_pair[128:256, :] = block_ones
    for case in range(CASES):
        wide = (same == case).astype(F32).astype(BF16)
        ones_wide[0:128, case * 128 : case * 128 + 128] = wide
        ones_wide[128:256, case * 128 : case * 128 + 128] = wide

    row_levels = [spread(packed, 16 + j) for j in range(BLOCKS)]
    blank = jnp.zeros((ROWS, 128), F32)
    row_levels = [blank] + row_levels + [blank]
    for j in range(BLOCKS):
        here = row_levels[j + 1]
        right = jnp.minimum(here, row_levels[j + 2])
        left = jnp.minimum(here, row_levels[j])
        rlf[j * ROWS : j * ROWS + ROWS, :] = jnp.where(is_last, right, here)
        llf[j * ROWS : j * ROWS + ROWS, :] = jnp.where(is_first, left, here)
        er[j * ROWS : j * ROWS + ROWS, :] = right
        el[j * ROWS : j * ROWS + ROWS, :] = left

    def block_columns(j, base, sums, target):
        total = jnp.zeros((ROWS, 128), F32)
        for case in range(CASES):
            total = jnp.where(case_of == case, jnp.sum(sums[case], axis=1, keepdims=True), total)
        if target is not None:
            target[pl.ds(pl.multiple_of(j * ROWS, ROWS), ROWS), :] = total
        return total

    def to_scatter(j, base, total):
        flat = pl.ds(pl.multiple_of(j * ROWS, ROWS), ROWS)
        high, low = halves(total * m_high[pl.ds(base, ROWS), :])
        lb[flat, 0:128] = high
        lb[flat, 128:256] = low

    def codes(i, _):
        rows = pl.ds(pl.multiple_of(i * 80, 16), 80)
        group = groups[rows, :]
        lanes = lax.broadcasted_iota(jnp.int32, (80, 128), 1)
        e_low[rows, :] = (lanes == group // 32).astype(F32).astype(BF16)
        m_high[rows, :] = (lanes % 32 == group % 32).astype(F32)
        return 0

    lax.fori_loop(0, FIELD // 80, codes, 0)
    for copy in loads[5:7]:
        copy.wait()

    def start_rest(j, _):
        base = pl.multiple_of((j + 1) * STEP, 8)
        cols = pl.ds(pl.multiple_of(j * 128, 128), 128)
        flat = pl.ds(pl.multiple_of(j * ROWS, ROWS), ROWS)
        down, up, right_link, left_link = links(j, base)
        shunt = shn[:, cols]
        half = dmf[flat, :]
        rests = []
        for case in range(CASES):
            at = pl.ds(case * FIELD + base, ROWS)
            here, below, above, right, left = neighbours(ef, case, base)
            slope = half * jnp.exp(here)
            rest = pn[case, :, cols] - (
                shunt * here
                + down * (here - below)
                + up * (here - above)
                + right_link * (here - right)
                + left_link * (here - left)
                + slope
                - half
            )
            dgf[at, :] = slope
            rf[at, :] = rest
            rests.append(rest)
        block_columns(j, base, rests, br)
        return 0

    def start_scaled(j, sums):
        base = pl.multiple_of((j + 1) * STEP, 8)
        cols = pl.ds(pl.multiple_of(j * 128, 128), 128)
        flat = pl.ds(pl.multiple_of(j * ROWS, ROWS), ROWS)
        down, up, right_link, left_link = links(j, base)
        shunt = shn[:, cols]
        edge = jnp.where(is_last, right_link, 0.0) + jnp.where(is_first, left_link, 0.0)
        out, plain = [], []
        for case in range(CASES):
            at = pl.ds(case * FIELD + base, ROWS)
            ground = shunt + dgf[at, :] + down + up
            diagonal = ground + right_link + left_link
            inverse = 1.0 / diagonal
            rest = rf[at, :]
            scaled = rest * inverse
            dgf[at, :] = diagonal
            inf[at, :] = inverse
            ef[at, :] = scaled
            out.append(sums[case] + fold(rest * scaled))
            plain.append(ground + edge)
        block_columns(j, base, plain, sd)
        ss[flat, :] = jnp.broadcast_to(jnp.sum(down, axis=1, keepdims=True), (ROWS, 128))
        su[flat, :] = jnp.broadcast_to(jnp.sum(up, axis=1, keepdims=True), (ROWS, 128))
        return tuple(out)

    zero = jnp.zeros((8, 128), F32)
    lax.fori_loop(0, BLOCKS, start_rest, 0)

    for copy in setup_copies:
        copy.wait()
    edges_in(ef, sd_r, su_r, sl_r, sr_r)
    sf[pl.ds(STEP - 1, BLOCKS, stride=STEP), :] = sd_r[72:88, :]
    open_left = jnp.where(c == 0, 0.0, 1.0).astype(F32)
    open_right = jnp.where(c == NC - 1, 0.0, 1.0).astype(F32)
    level_left = jnp.broadcast_to(sl_r[2:3, :], (128, 128)).T[0:ROWS]
    level_right = jnp.broadcast_to(sr_r[2:3, :], (128, 128)).T[0:ROWS]
    for block, slot, level_there, is_open, is_edge, link, edge in (
        (0, 0, level_left, open_left, is_first, llf, el),
        (BLOCKS - 1, BLOCKS + 1, level_right, open_right, is_last, rlf, er),
    ):
        rows = pl.ds(block * ROWS, ROWS)
        here = row_levels[block + 1]
        value = jnp.minimum(here, level_there) * is_open
        link[rows, :] = jnp.where(is_edge, value, here)
        edge[rows, :] = value
        total = br[rows, :]
        for case in range(CASES):
            at = pl.ds(case * FIELD + (block + 1) * STEP, ROWS)
            there = ef[pl.ds(case * FIELD + slot * STEP, ROWS), :]
            more = jnp.where(is_edge, value * (there - ef[at, :]), 0.0)
            rf[at, :] = rf[at, :] + more
            total = total + jnp.where(case_of == case, jnp.sum(more, axis=1, keepdims=True), 0.0)
        br[rows, :] = total
    for first in (True, False):
        edge_row = 0 if first else ROWS - 1
        link = sf[pl.ds(STEP + (-1 if first else edge_row), BLOCKS, stride=STEP), :]
        rows = pl.ds(edge_row, BLOCKS, stride=ROWS)
        total = br[rows, :]
        for case in range(CASES):
            if first:
                more = link * (ef[rows_of(case, -1), :] - ef[rows_of(case, 0), :])
            else:
                more = link * ef[rows_of(case, ROWS), :]
            rf[rows_of(case, edge_row), :] = rf[rows_of(case, edge_row), :] + more
            total = total + jnp.where(case_of[0:BLOCKS] == case, jnp.sum(more, axis=1, keepdims=True), 0.0)
        br[rows, :] = total

    def scatter_rest(j, _):
        to_scatter(j, pl.multiple_of((j + 1) * STEP, 8), br[pl.ds(pl.multiple_of(j * ROWS, ROWS), ROWS), :])
        return 0

    lax.fori_loop(0, BLOCKS, scatter_rest, 0)

    def prepare_rest():
        above8 = sd_r[64:72, :]
        below8 = su_r[64:72, :]
        for j in range(BLOCKS):
            base = (j + 1) * STEP
            groups[base - 1 : base, :] = spread(above8, j, 8)[7:8].astype(jnp.int32)
            groups[base + ROWS : base + ROWS + 1, :] = spread(below8, j, 8)[0:1].astype(jnp.int32)
        for first, row_there in ((0, sl_r[1:2, :]), (17 * STEP, sr_r[1:2, :])):
            groups[first : first + ROWS, :] = jnp.broadcast_to(row_there, (128, 128)).T[0:ROWS].astype(jnp.int32)
        lax.fori_loop(0, FIELD // 80, codes, 0)
        for copy in loads[7:]:
            copy.wait()

        def pick(i, _):
            rows = pl.ds(pl.multiple_of(i * 32, 32), 32)
            for block in range(4):
                parts = []
                for half in range(2):
                    turn = lax.rem(64 * half + 128 - 64 * lax.rem(chip, 2), 128)
                    parts.append(pltpu.roll(staged[block * 2 + half, rows, :], turn, 1))
                high, low = halves(jnp.where(lane < 64, parts[0], parts[1]))
                a_high[rows, block * 128 : block * 128 + 128] = high
                a_low[rows, block * 128 : block * 128 + 128] = low
            return 0

        lax.fori_loop(0, 16, pick, 0)


    def send_restricted(k):
        out = dot(e_turn[...], lb[...])
        s1[k] = (out[:, 0:128] + out[:, 128:256]).reshape(CHIPS, 16, 128)
        for who in str_peers:
            remote(s1.at[k, who[0] // 2], r1.at[k, s], send_sem.at[k, 0], recv_sem.at[k, 0], who).start()
        r1[k, s] = s1[k, chip]

    def swap_sums(k, tile):
        sc_s[k] = tile
        copy = remote(sc_s.at[k], sc_r.at[k], sc_send.at[k], sc_recv.at[k], sibling)
        copy.start()
        return copy

    def send_chunk(k, swap):
        swap.wait()
        arrived(r1.at[k, 0 : NS - 1], recv_sem.at[k, 0])
        s2[k, 0:16, :] = jnp.sum(r1[k], axis=0)
        s2[k, 16:24, :] = sc_s[k] + sc_r[k]
        for who in crs_peers:
            remote(s2.at[k], r2.at[k, c], send_sem.at[k, 1], recv_sem.at[k, 1], who).start()
        r2[k, c] = s2[k]

    def send_product(k):
        arrived(r2.at[k, 0 : NC - 1], recv_sem.at[k, 1])
        total = jnp.sum(r2[k], axis=0)
        t = total[0:16]
        t_tile[...] = t
        placed = jnp.concatenate([jnp.broadcast_to(t[i : i + 1], (ROWS, 128)) * spot for i in range(16)], axis=0)
        high, low = halves(placed)
        both = dot(jnp.concatenate([high, low], axis=0), ones_pair[0:128, :]).astype(BF16)
        right = jnp.concatenate([both[0:512], both[512:1024]], axis=1)
        out = dot(a_high[...], right)
        out = out[:, 0:128] + out[:, 128:256] + dot(a_low[...], both[0:512])
        y = jnp.sum(out.reshape(16, ROWS, 128) * spot[None], axis=1)
        s3[k, 0:16, :] = y
        tile = total[16:24]
        for i in range(2):
            own = t_tile[pl.ds(2 * c + i, 1), :]
            tile = jnp.where(sub8 == i, jnp.broadcast_to(own, (8, 128)), tile)
        s3[k, 16:24, :] = tile
        for who in chip_peers:
            remote(s3.at[k], r3.at[k, chip], send_sem.at[k, 2], recv_sem.at[k, 2], who).start()
        r3[k, chip] = s3[k]

    RZ, RR, ALPHA, BETA, RQ, QQ = range(6)

    def row(x, i):
        return jnp.broadcast_to(x[i : i + 1], (8, 128))

    def send_correction(k, first=False):
        arrived(r3.at[k, 0 : CHIPS - 1], recv_sem.at[k, 2])
        total = jnp.sum(r3[k], axis=0)
        y = total[0:16]
        t = jnp.concatenate([r3[k, i, 16:18, :] for i in range(CHIPS)], axis=0)
        sums = total[16:24]
        if first:
            state[RR] = row(sums, 2)
        else:
            alpha = state[RZ] / row(sums, 2)
            state[ALPHA] = alpha
            state[QQ] = row(sums, 3)
            state[RQ] = row(sums, 4)
            y = y_now[...] - alpha[0:1] * y
            t = t_now[...] - alpha[0:1] * t
        y_now[...] = y
        t_now[...] = t
        s4[k, 0:16, :] = y
        s4[k, 16:24, :] = jnp.broadcast_to(jnp.sum(y * t, axis=0, keepdims=True), (8, 128))
        for who in crs_peers:
            remote(s4.at[k], r4.at[k, c], send_sem.at[k, 3], recv_sem.at[k, 3], who).start()
        r4[k, c] = s4[k]

    def to_cases(slot, x):
        for case in range(CASES):
            per_case[slot, case] = jnp.broadcast_to(x[:, case * 32 : case * 32 + 1], (8, 128))

    def receive_correction(k, first=False):
        arrived(r4.at[k, 0 : NC - 1], recv_sem.at[k, 3])
        correction = jnp.concatenate([r4[k, i, 0:16, :] for i in range(NC)], axis=0)
        high, low = halves(correction)
        picked = dot(e_low[...], jnp.concatenate([high, low], axis=1))
        mask = m_high[...]
        gm[:, 0:128] = (picked[:, 0:128] * mask).astype(BF16)
        gm[:, 128:256] = (picked[:, 128:256] * mask).astype(BF16)
        cb[...] = dot(gm[...], ones_pair[...])
        coarse = case_sums(jnp.sum(r4[k, :, 16:24, :], axis=0))
        if first:
            state[RZ] = state[RR] + coarse
        else:
            alpha = state[ALPHA]
            smooth = state[RR] - 2.0 * alpha * state[RQ] + alpha * alpha * state[QQ]
            fresh = smooth + coarse
            state[RR] = smooth
            state[BETA] = fresh / state[RZ]
            state[RZ] = fresh
            to_cases(0, alpha)
            to_cases(1, state[BETA])

    def block_level(final=False):
        alpha = state[ALPHA][0:1]
        beta = state[BETA][0:1]

        def body(j, energy):
            base = pl.multiple_of((j + 1) * STEP, 8)
            flat = pl.ds(pl.multiple_of(j * ROWS, ROWS), ROWS)
            value = bu[flat, :] - alpha * bw[flat, :]
            if not final:
                bu[flat, :] = value
            value = value + beta * bq[flat, :]
            here = cb[pl.ds(base, ROWS), :]
            stencil = (
                sd[flat, :] * here
                - ss[flat, :] * cb[pl.ds(base + 1, ROWS), :]
                - su[flat, :] * cb[pl.ds(base - 1, ROWS), :]
                - er[flat, :] * cb[pl.ds(base + STEP, ROWS), :]
                - el[flat, :] * cb[pl.ds(base - STEP, ROWS), :]
            )
            if final:
                return energy + fold(here * (stencil + 2.0 * value))
            value = value + stencil
            bq[flat, :] = value
            to_scatter(j, base, value)
            return energy

        return lax.fori_loop(0, BLOCKS, body, zero)


    def widen_correction():
        wide = dot(gm[...], ones_wide[...])
        for case in range(CASES):
            pcf[case * FIELD : case * FIELD + FIELD, :] = wide[:, case * 128 : case * 128 + 128]

    def next_direction(final=False):
        widen_correction()
        kinds = 0 if final else 5

        def body(j, sums):
            base = pl.multiple_of((j + 1) * STEP, 8)
            cols = pl.ds(pl.multiple_of(j * 128, 128), 128)
            link = links(j, base)
            out = []
            for case in range(CASES):
                at = pl.ds(case * FIELD + base, ROWS)
                here, image = jacobian(pcf, case, base, link)
                rest = rf[at, :]
                inverse = inf[at, :]
                alpha = per_case[0, case][0:1]
                beta = per_case[1, case][0:1]
                last_image = qf[at, :]
                last_direction = df[at, :]
                smooth = uf[at, :] - alpha * wf[at, :]
                image = image + beta * last_image + smooth
                rest = rest - alpha * last_image
                step = xf[at, :] + alpha * last_direction
                direction = rest * inverse + here + beta * last_direction
                if final:
                    xf_out[case, :, cols] = step
                    rf_out[case, :, cols] = rest
                    df_out[case, :, cols] = direction
                    qf_out[case, :, cols] = image
                    continue
                uf[at, :] = smooth
                rf[at, :] = rest
                xf[at, :] = step
                qf[at, :] = image
                df[at, :] = direction
                scaled = image * inverse
                ef[at, :] = scaled
                terms = [direction * image, image * scaled, rest * scaled, rest * inverse * smooth, scaled * smooth]
                out.extend(sums[kinds * case + i] + fold(terms[i]) for i in range(kinds))
            return tuple(out)

        sums = lax.fori_loop(0, BLOCKS, body, (zero,) * (kinds * CASES))
        tile = zero
        for kind in range(kinds):
            one = by_case([sums[kinds * case + kind] for case in range(CASES)])
            tile = jnp.where(sub8 == kind + 2, one, tile)
        return tile

    def start_halo(k):
        edges_out(ef, hu_s.at[k], hd_s.at[k], hl_s.at[k], hr_s.at[k])
        bufs = [ref.at[k] for ref in (hu_s, hd_s, hl_s, hr_s, hd_r, hu_r, hl_r, hr_r)]
        return exchange(bufs, halo_send.at[k], halo_recv.at[k])

    def apply_scaled(k, copies, target, sums_to):
        for copy in copies:
            copy.wait()
        edges_in(ef, hd_r.at[k], hu_r.at[k], hl_r.at[k], hr_r.at[k])

        def body(j, sums):
            base = pl.multiple_of((j + 1) * STEP, 8)
            link = links(j, base)
            values, out = [], []
            for case in range(CASES):
                here, image = jacobian(ef, case, base, link)
                target[pl.ds(case * FIELD + base, ROWS), :] = image
                values.append(image)
                out.append(sums[case] + fold(here * image))
            block_columns(j, base, values, sums_to)
            return tuple(out)

        return lax.fori_loop(0, BLOCKS, body, (zero,) * CASES)


    send_restricted(0)
    start_sums = lax.fori_loop(0, BLOCKS, start_scaled, (zero,) * CASES)
    swap = swap_sums(0, jnp.where(sub8 == 2, by_case(start_sums), zero))
    copies = start_halo(0)
    send_chunk(0, swap)
    prepare_rest()
    send_product(0)
    apply_scaled(0, copies, uf, bu)
    send_correction(0, first=True)
    receive_correction(0, first=True)

    def solve(k, _):
        block_level()
        send_restricted(k)
        tile = next_direction()
        local[...] = tile
        swap = swap_sums(k, tile)
        copies = start_halo(k)
        send_chunk(k, swap)
        send_product(k)
        local_w[...] = by_case(apply_scaled(k, copies, wf, bw))
        send_correction(k)
        receive_correction(k)
        return 0

    lax.fori_loop(1, SOLVES, solve, 0)


    alpha = state[ALPHA]
    beta = state[BETA]
    energy = jnp.sum(block_level(final=True), axis=0, keepdims=True)
    dq, qq, rq, eu, qu = (row(local[...], i) for i in range(2, 7))
    energy = (
        energy
        + (eu - 2.0 * alpha * qu + alpha * alpha * local_w[...])
        + 2.0 * beta * (rq - alpha * qq)
        + beta * beta * dq
    )
    here = s * NC + c
    fs[...] = energy[0:1]
    for _, who in everyone:
        remote(fs, fr.at[here], last_send.at[0], last_recv.at[0], who).start()
    fr[here] = fs[...]
    next_direction(final=True)
    arrived(fr.at[0 : NS * NC - 1], last_recv.at[0])
    alpha = state[RZ] / jnp.broadcast_to(jnp.sum(fr[...], axis=0), (8, 128))
    for case in range(CASES):
        alpha_out[case : case + 1, :] = jnp.broadcast_to(alpha[0:1, case * 32 : case * 32 + 1], (1, 2048))


    for k in range(SOLVES):
        arrived(r1.at[k, 0 : NS - 1], send_sem.at[k, 0])
        arrived(r2.at[k, 0 : NC - 1], send_sem.at[k, 1])
        arrived(r3.at[k, 0 : CHIPS - 1], send_sem.at[k, 2])
        arrived(r4.at[k, 0 : NC - 1], send_sem.at[k, 3])
    arrived(fr.at[0 : NS * NC - 1], last_send.at[0])


def shards(voltage, photocurrent, shunt, series, pattern, diode_mask, aggregate, coarse_inverse):
    field = (CASES * FIELD, 128)
    flat = (BLOCKS * ROWS, 128)

    def vmem(shape, dtype=F32):
        return pltpu.VMEM(shape, dtype)

    dma = pltpu.SemaphoreType.DMA
    scratch = [
        vmem((CASES, ROWS, 2048)), vmem((CASES, ROWS, 2048)), vmem((ROWS, 2048)), vmem((ROWS, 2048)),
        vmem((BLOCKS, ROWS), jnp.int32), vmem((BLOCKS, ROWS), jnp.int32), vmem((BLOCKS, ROWS), jnp.int32),
        vmem((NC, 512, 128)), vmem((512, 512), BF16), vmem((512, 512), BF16),
        *[vmem(field) for _ in range(10)],
        vmem((FIELD, 128)), vmem(flat), vmem(flat), vmem(flat),
        vmem((FIELD, 128)), vmem((FIELD, 256), BF16), vmem((FIELD, 128), BF16), vmem((FIELD, 128)),
        vmem((FIELD, 128), jnp.int32), vmem((128, 512), BF16), vmem((256, 128), BF16), vmem((256, 512), BF16),
        *[vmem(flat) for _ in range(9)], vmem((512, 256), BF16),
        vmem((ROWS, 128)), vmem((128, 128)),
        vmem((72, 128)), vmem((88, 128)), vmem((8, 128)), vmem((8, 128)),
        vmem((72, 128)), vmem((88, 128)), vmem((8, 128)), vmem((8, 128)),
        vmem((SOLVES, 64, 128)), vmem((SOLVES, 64, 128)), vmem((SOLVES, 8, 128)), vmem((SOLVES, 8, 128)),
        vmem((SOLVES, 64, 128)), vmem((SOLVES, 64, 128)), vmem((SOLVES, 8, 128)), vmem((SOLVES, 8, 128)),
        vmem((SOLVES, CHIPS, 16, 128)), vmem((SOLVES, NS, 16, 128)),
        vmem((SOLVES, 24, 128)), vmem((SOLVES, NC, 24, 128)),
        vmem((SOLVES, 24, 128)), vmem((SOLVES, CHIPS, 24, 128)),
        vmem((SOLVES, 24, 128)), vmem((SOLVES, NC, 24, 128)),
        vmem((1, 128)), vmem((NS * NC, 1, 128)),
        vmem((16, 128)), vmem((16, 128)), vmem((16, 128)), vmem((6, 8, 128)), vmem((2, CASES, 8, 128)), vmem((8, 128)), vmem((8, 128)),
        vmem((SOLVES, 8, 128)), vmem((SOLVES, 8, 128)),
        dma((15,)), dma((4,)), dma((4,)), dma((SOLVES, 4)), dma((SOLVES, 4)),
        dma((SOLVES, 4)), dma((SOLVES, 4)), dma((1,)), dma((1,)), dma((SOLVES,)), dma((SOLVES,)),
    ]
    tall = jax.ShapeDtypeStruct((CASES, ROWS, 2048), F32)
    step, direction, rest, image, alpha = pl.pallas_call(
        kernel,
        out_shape=[tall] * 4 + [jax.ShapeDtypeStruct((CASES, 2048), F32)],
        in_specs=[pl.BlockSpec(memory_space=pltpu.HBM)] * 8,
        out_specs=[pl.BlockSpec(memory_space=pltpu.VMEM)] * 5,
        scratch_shapes=scratch,
        compiler_params=pltpu.CompilerParams(collective_id=0, has_side_effects=True, vmem_limit_bytes=54 * 2**20),
        name="newton",
    )(voltage, photocurrent, shunt, series, pattern.T, diode_mask.T, aggregate.T, coarse_inverse)
    alpha = alpha[:, None, :]
    return step + alpha * direction, rest - alpha * image


def solution(mesh):
    field = P(None, "str", "crs")
    plane = P("str", "crs")
    return jax.shard_map(
        shards,
        mesh=mesh,
        in_specs=(field, field, plane, plane, plane, plane, plane, P("crs", None)),
        out_specs=(field, field),
        check_vma=False,
    )
```

```python
import itertools

import jax
import jax.numpy as jnp
from jax import lax
from jax.experimental import pallas as pl
from jax.experimental.pallas import tpu as pltpu
from jax.sharding import PartitionSpec as P

MESH = pl.DeviceIdType.MESH
F32 = jnp.float32
BF16 = jnp.bfloat16

CASES = 4
ROWS = 32
BLOCKS = 16
STEP = 40
FIELD = (BLOCKS + 2) * STEP
NS = 16
NC = 8
SOLVES = 3
LEVELS = (0.25, 0.5, 1.0, 2.0)


def dot(a, b):
    return jnp.dot(a, b, preferred_element_type=F32)


def halves(x):
    high = x.astype(BF16)
    return high, (x - high.astype(F32)).astype(BF16)


def kernel(
    v_in, photo_in, shunt_in, series_in, pattern_in, mask_in, group_in, inverse_in,
    xf_out, df_out, rf_out, qf_out, alpha_out,
    xn, dn, vn, pn, shn, sn, patn, maskn, groupn, staged, a_high, a_low,
    ef, rf, qf, df, xf, uf, wf, dgf, inf, pcf,
    sf, rlf, llf, dmf,
    cb, gm, e_low, m_high, groups, e_turn, ones_pair, ones_wide,
    bu, bw, bq, br, sd, ss, su, er, el, lb,
    pk, turned, su_s, sd_s, sl_s, sr_s, su_r, sd_r, sl_r, sr_r,
    hu_s, hd_s, hl_s, hr_s, hu_r, hd_r, hl_r, hr_r,
    s1, r1, s2, r2, s3, r3, s4, r4, fs, fr,
    y_now, t_now, t_tile, state, per_case, local, local_w,
    in_sem, out_sem, setup_send, setup_recv, halo_send, halo_recv, send_sem, recv_sem, last_send, last_recv,
):
    s = lax.axis_index("str")
    c = lax.axis_index("crs")

    def at_str(k):
        return (lax.rem(s + k, NS), c)

    def at_crs(k):
        return (s, lax.rem(c + k, NC))

    str_at = {}
    for key in itertools.product(range(2), range(4), range(2)):
        x_lo, y, core = (lax.rem(p + k, n) for p, k, n in zip((s // 8, lax.rem(s // 2, 4), lax.rem(s, 2)), key, (2, 4, 2)))
        str_at[key] = (x_lo * 4 + y) * 2 + core
    crs_at = {}
    for key in itertools.product(range(2), range(4)):
        x_hi, z = (lax.rem(p + k, n) for p, k, n in zip((c // 4, lax.rem(c, 4)), key, (2, 4)))
        crs_at[key] = x_hi * 4 + z

    def far_first(key):
        x_lo, y, core, x_hi, z = key
        across = 1 if x_lo else 2 * x_hi
        return -(across + min(y, 4 - y) + min(z, 4 - z) + 0.5 * core)

    everyone = sorted(itertools.product(range(2), range(4), range(2), range(2), range(4)), key=far_first)[:-1]
    everyone = [(key, (str_at[key[:3]], crs_at[key[3:]])) for key in everyone]
    str_peers = [(who[0], c) for key, who in everyone if key[3:] == (0, 0)]
    crs_peers = [(s, who[1]) for key, who in everyone if key[:3] == (0, 0, 0)]

    barrier = pltpu.get_barrier_semaphore()
    for who in str_peers + crs_peers:
        pl.semaphore_signal(barrier, inc=1, device_id=who, device_id_type=MESH)

    loads = [
        pltpu.make_async_copy(v_in, vn, in_sem.at[0]),
        pltpu.make_async_copy(series_in, sn, in_sem.at[1]),
        pltpu.make_async_copy(pattern_in, patn, in_sem.at[2]),
        pltpu.make_async_copy(mask_in, maskn, in_sem.at[3]),
        pltpu.make_async_copy(group_in, groupn, in_sem.at[4]),
        pltpu.make_async_copy(shunt_in, shn, in_sem.at[5]),
        pltpu.make_async_copy(photo_in, pn, in_sem.at[6]),
    ]
    quarter = pl.multiple_of((s // 4) * 128, 128)
    for k in range(NC):
        loads.append(
            pltpu.make_async_copy(
                inverse_in.at[:, pl.ds(pl.multiple_of(k * 512 + quarter, 128), 128)], staged.at[k], in_sem.at[7 + k]
            )
        )
    for copy in loads:
        copy.start()

    lane = lax.broadcasted_iota(jnp.int32, (ROWS, 128), 1)
    case_of = lane // 32
    is_first = lane == 0
    is_last = lane == 127
    case8 = case_of[0:8]
    sub8 = lax.broadcasted_iota(jnp.int32, (8, 128), 0)
    spot = (lax.broadcasted_iota(jnp.int32, (ROWS, 128), 0) == lane - 32 * case_of).astype(F32)

    def remote(src, dst, send, recv, who):
        return pltpu.make_async_remote_copy(
            src_ref=src, dst_ref=dst, send_sem=send, recv_sem=recv, device_id=who, device_id_type=MESH
        )

    def arrived(ref, sem):
        pltpu.make_async_copy(ref, ref, sem).wait()

    def rows_of(case, row):
        return pl.ds(case * FIELD + STEP + row, BLOCKS, stride=STEP)

    def edges_out(f, up, down, left, right):
        for case in range(CASES):
            up[case * 16 : case * 16 + 16, :] = f[rows_of(case, 0), :]
            down[case * 16 : case * 16 + 16, :] = f[rows_of(case, ROWS - 1), :]
        for block, ref in ((0, left), (BLOCKS - 1, right)):
            first = (block + 1) * STEP
            tile = jnp.concatenate(
                [f[case * FIELD + first : case * FIELD + first + ROWS, :] for case in range(CASES)], axis=0
            ).T
            ref[0:8, :] = tile[0:8] if block == 0 else tile[120:128]

    def edges_in(f, above, below, left, right):
        for case in range(CASES):
            f[rows_of(case, -1), :] = above[case * 16 : case * 16 + 16, :]
            f[rows_of(case, ROWS), :] = below[case * 16 : case * 16 + 16, :]
        for first, row in ((0, left[7:8, :]), (17 * STEP, right[0:1, :])):
            tile = jnp.broadcast_to(row, (128, 128)).T
            for case in range(CASES):
                f[case * FIELD + first : case * FIELD + first + ROWS, :] = tile[case * ROWS : case * ROWS + ROWS]

    def exchange(bufs, send, recv):
        up_s, down_s, left_s, right_s, above_r, below_r, left_r, right_r = bufs
        copies = [
            remote(up_s, below_r, send.at[0], recv.at[0], at_str(NS - 1)),
            remote(down_s, above_r, send.at[1], recv.at[1], at_str(1)),
            remote(left_s, right_r, send.at[2], recv.at[2], at_crs(NC - 1)),
            remote(right_s, left_r, send.at[3], recv.at[3], at_crs(1)),
        ]
        for copy in copies:
            copy.start()
        return copies

    def neighbours(f, case, base):
        def part(shift):
            return f[pl.ds(case * FIELD + base + shift, ROWS), :]

        here = part(0)
        right = pltpu.roll(jnp.where(is_first, part(STEP), here), 127, 1)
        left = pltpu.roll(jnp.where(is_last, part(-STEP), here), 1, 1)
        return here, part(1), part(-1), right, left

    def links(j, base):
        flat = pl.ds(pl.multiple_of(j * ROWS, ROWS), ROWS)
        return sf[pl.ds(base, ROWS), :], sf[pl.ds(base - 1, ROWS), :], rlf[flat, :], llf[flat, :]

    def jacobian(f, case, base, link):
        down, up, right_link, left_link = link
        here, below, above, right, left = neighbours(f, case, base)
        diagonal = dgf[pl.ds(case * FIELD + base, ROWS), :]
        return here, diagonal * here - down * below - up * above - right_link * right - left_link * left

    def fold(x):
        return x[0:8] + x[8:16] + x[16:24] + x[24:32]

    def by_case(parts):
        total = jnp.zeros((8, 128), F32)
        for case in range(CASES):
            total = jnp.where(case8 == case, jnp.sum(parts[case], axis=(0, 1), keepdims=True), total)
        return total

    def case_sums(x):
        total = jnp.zeros((8, 128), F32)
        for case in range(CASES):
            one = jnp.sum(jnp.where(case8 == case, x, 0.0), axis=1, keepdims=True)
            total = jnp.where(case8 == case, one, total)
        return total


    def spread(x, column, rows=ROWS):
        return jnp.broadcast_to(x[:, column : column + 1], (rows, 128))

    def clear(i, _):
        rows = pl.ds(pl.multiple_of(i * 80, 16), 80)
        for f in (ef, wf, qf, df, xf):
            f[rows, :] = jnp.zeros((80, 128), F32)
        return 0

    lax.fori_loop(0, CASES * FIELD // 80, clear, 0)
    sf[...] = jnp.zeros_like(sf)
    bw[...] = jnp.zeros_like(bw)
    bq[...] = jnp.zeros_like(bq)
    state[...] = jnp.zeros_like(state)
    per_case[...] = jnp.zeros_like(per_case)
    for copy in loads[:5]:
        copy.wait()
    level = jnp.zeros((BLOCKS, ROWS), F32)
    for number in range(4):
        level = level + jnp.where(patn[...] == number, F32(LEVELS[number]), F32(0.0))
    turned[...] = jnp.zeros_like(turned)
    turned[0:16, 0:32] = groupn[...].astype(F32)
    turned[16:32, 0:32] = level
    turned[32:48, 0:32] = maskn[...].astype(F32) * 0.5
    pk[...] = turned[...].T[0:ROWS]
    packed = pk[...]

    def lay_out(j, _):
        base = pl.multiple_of((j + 1) * STEP, 8)
        cols = pl.ds(pl.multiple_of(j * 128, 128), 128)
        for case in range(CASES):
            ef[pl.ds(case * FIELD + base, ROWS), :] = vn[case, :, cols]
        sf[pl.ds(base, ROWS), :] = sn[:, cols]
        return 0

    lax.fori_loop(0, BLOCKS, lay_out, 0)
    edges_out(ef, su_s, sd_s, sl_s, sr_s)
    su_s[64:72, :] = packed[0:8]
    sd_s[64:72, :] = packed[24:32]
    sd_s[72:88, :] = sf[pl.ds(STEP + ROWS - 1, BLOCKS, stride=STEP), :]
    sl_s[1:2, :] = turned[0:1, :]
    sl_s[2:3, :] = turned[16:17, :]
    sr_s[1:2, :] = turned[15:16, :]
    sr_s[2:3, :] = turned[31:32, :]

    pl.semaphore_wait(barrier, NS - 1 + NC - 1)
    setup_copies = exchange((su_s, sd_s, sl_s, sr_s, sd_r, su_r, sl_r, sr_r), setup_send, setup_recv)

    groups[...] = jnp.zeros_like(groups)
    for j in range(BLOCKS):
        base = (j + 1) * STEP
        group = spread(packed, j).astype(jnp.int32)
        groups[base : base + ROWS, :] = group
        low = group // 32
        code = (low % 16) * 8 + low // 16
        lb[j * ROWS : j * ROWS + ROWS, 0:128] = (lane == code).astype(F32).astype(BF16)
        dmf[j * ROWS : j * ROWS + ROWS, :] = spread(packed, 32 + j)
    for k in range(4):
        e_turn[:, k * 128 : k * 128 + 128] = lb[k * 128 : k * 128 + 128, 0:128].astype(F32).T.astype(BF16)

    same = lax.broadcasted_iota(jnp.int32, (128, 128), 0) // 32
    across = lax.broadcasted_iota(jnp.int32, (128, 128), 1) // 32
    block_ones = (same == across).astype(F32).astype(BF16)
    ones_pair[0:128, :] = block_ones
    ones_pair[128:256, :] = block_ones
    for case in range(CASES):
        wide = (same == case).astype(F32).astype(BF16)
        ones_wide[0:128, case * 128 : case * 128 + 128] = wide
        ones_wide[128:256, case * 128 : case * 128 + 128] = wide

    row_levels = [spread(packed, 16 + j) for j in range(BLOCKS)]
    blank = jnp.zeros((ROWS, 128), F32)
    row_levels = [blank] + row_levels + [blank]
    for j in range(BLOCKS):
        here = row_levels[j + 1]
        right = jnp.minimum(here, row_levels[j + 2])
        left = jnp.minimum(here, row_levels[j])
        rlf[j * ROWS : j * ROWS + ROWS, :] = jnp.where(is_last, right, here)
        llf[j * ROWS : j * ROWS + ROWS, :] = jnp.where(is_first, left, here)
        er[j * ROWS : j * ROWS + ROWS, :] = right
        el[j * ROWS : j * ROWS + ROWS, :] = left

    def block_columns(j, base, sums, target):
        total = jnp.zeros((ROWS, 128), F32)
        for case in range(CASES):
            total = jnp.where(case_of == case, jnp.sum(sums[case], axis=1, keepdims=True), total)
        if target is not None:
            target[pl.ds(pl.multiple_of(j * ROWS, ROWS), ROWS), :] = total
        return total

    def to_scatter(j, base, total):
        flat = pl.ds(pl.multiple_of(j * ROWS, ROWS), ROWS)
        high, low = halves(total * m_high[pl.ds(base, ROWS), :])
        lb[flat, 0:128] = high
        lb[flat, 128:256] = low

    def codes(i, _):
        rows = pl.ds(pl.multiple_of(i * 80, 16), 80)
        group = groups[rows, :]
        lanes = lax.broadcasted_iota(jnp.int32, (80, 128), 1)
        e_low[rows, :] = (lanes == group // 32).astype(F32).astype(BF16)
        m_high[rows, :] = (lanes % 32 == group % 32).astype(F32)
        return 0

    lax.fori_loop(0, FIELD // 80, codes, 0)
    for copy in loads[5:7]:
        copy.wait()

    def start_rest(j, _):
        base = pl.multiple_of((j + 1) * STEP, 8)
        cols = pl.ds(pl.multiple_of(j * 128, 128), 128)
        flat = pl.ds(pl.multiple_of(j * ROWS, ROWS), ROWS)
        down, up, right_link, left_link = links(j, base)
        shunt = shn[:, cols]
        half = dmf[flat, :]
        rests = []
        for case in range(CASES):
            at = pl.ds(case * FIELD + base, ROWS)
            here, below, above, right, left = neighbours(ef, case, base)
            slope = half * jnp.exp(here)
            rest = pn[case, :, cols] - (
                shunt * here
                + down * (here - below)
                + up * (here - above)
                + right_link * (here - right)
                + left_link * (here - left)
                + slope
                - half
            )
            dgf[at, :] = slope
            rf[at, :] = rest
            rests.append(rest)
        block_columns(j, base, rests, br)
        return 0

    def start_scaled(j, sums):
        base = pl.multiple_of((j + 1) * STEP, 8)
        cols = pl.ds(pl.multiple_of(j * 128, 128), 128)
        flat = pl.ds(pl.multiple_of(j * ROWS, ROWS), ROWS)
        down, up, right_link, left_link = links(j, base)
        shunt = shn[:, cols]
        edge = jnp.where(is_last, right_link, 0.0) + jnp.where(is_first, left_link, 0.0)
        out, plain = [], []
        for case in range(CASES):
            at = pl.ds(case * FIELD + base, ROWS)
            ground = shunt + dgf[at, :] + down + up
            diagonal = ground + right_link + left_link
            inverse = 1.0 / diagonal
            rest = rf[at, :]
            scaled = rest * inverse
            dgf[at, :] = diagonal
            inf[at, :] = inverse
            ef[at, :] = scaled
            out.append(sums[case] + fold(rest * scaled))
            plain.append(ground + edge)
        block_columns(j, base, plain, sd)
        ss[flat, :] = jnp.broadcast_to(jnp.sum(down, axis=1, keepdims=True), (ROWS, 128))
        su[flat, :] = jnp.broadcast_to(jnp.sum(up, axis=1, keepdims=True), (ROWS, 128))
        return tuple(out)

    zero = jnp.zeros((8, 128), F32)
    lax.fori_loop(0, BLOCKS, start_rest, 0)

    for copy in setup_copies:
        copy.wait()
    edges_in(ef, sd_r, su_r, sl_r, sr_r)
    sf[pl.ds(STEP - 1, BLOCKS, stride=STEP), :] = sd_r[72:88, :]
    open_left = jnp.where(c == 0, 0.0, 1.0).astype(F32)
    open_right = jnp.where(c == NC - 1, 0.0, 1.0).astype(F32)
    level_left = jnp.broadcast_to(sl_r[2:3, :], (128, 128)).T[0:ROWS]
    level_right = jnp.broadcast_to(sr_r[2:3, :], (128, 128)).T[0:ROWS]
    for block, slot, level_there, is_open, is_edge, link, edge in (
        (0, 0, level_left, open_left, is_first, llf, el),
        (BLOCKS - 1, BLOCKS + 1, level_right, open_right, is_last, rlf, er),
    ):
        rows = pl.ds(block * ROWS, ROWS)
        here = row_levels[block + 1]
        value = jnp.minimum(here, level_there) * is_open
        link[rows, :] = jnp.where(is_edge, value, here)
        edge[rows, :] = value
        total = br[rows, :]
        for case in range(CASES):
            at = pl.ds(case * FIELD + (block + 1) * STEP, ROWS)
            there = ef[pl.ds(case * FIELD + slot * STEP, ROWS), :]
            more = jnp.where(is_edge, value * (there - ef[at, :]), 0.0)
            rf[at, :] = rf[at, :] + more
            total = total + jnp.where(case_of == case, jnp.sum(more, axis=1, keepdims=True), 0.0)
        br[rows, :] = total
    for first in (True, False):
        edge_row = 0 if first else ROWS - 1
        link = sf[pl.ds(STEP + (-1 if first else edge_row), BLOCKS, stride=STEP), :]
        rows = pl.ds(edge_row, BLOCKS, stride=ROWS)
        total = br[rows, :]
        for case in range(CASES):
            if first:
                more = link * (ef[rows_of(case, -1), :] - ef[rows_of(case, 0), :])
            else:
                more = link * ef[rows_of(case, ROWS), :]
            rf[rows_of(case, edge_row), :] = rf[rows_of(case, edge_row), :] + more
            total = total + jnp.where(case_of[0:BLOCKS] == case, jnp.sum(more, axis=1, keepdims=True), 0.0)
        br[rows, :] = total

    def scatter_rest(j, _):
        to_scatter(j, pl.multiple_of((j + 1) * STEP, 8), br[pl.ds(pl.multiple_of(j * ROWS, ROWS), ROWS), :])
        return 0

    lax.fori_loop(0, BLOCKS, scatter_rest, 0)

    def prepare_rest():
        above8 = sd_r[64:72, :]
        below8 = su_r[64:72, :]
        for j in range(BLOCKS):
            base = (j + 1) * STEP
            groups[base - 1 : base, :] = spread(above8, j, 8)[7:8].astype(jnp.int32)
            groups[base + ROWS : base + ROWS + 1, :] = spread(below8, j, 8)[0:1].astype(jnp.int32)
        for first, row_there in ((0, sl_r[1:2, :]), (17 * STEP, sr_r[1:2, :])):
            groups[first : first + ROWS, :] = jnp.broadcast_to(row_there, (128, 128)).T[0:ROWS].astype(jnp.int32)
        lax.fori_loop(0, FIELD // 80, codes, 0)
        for copy in loads[7:]:
            copy.wait()

        def pick(i, _):
            rows = pl.ds(pl.multiple_of(i * 32, 32), 32)
            for side in range(2):
                block = jnp.zeros((ROWS, 128), F32)
                for k in range(4):
                    turn = lax.rem(32 * k + 128 - 32 * lax.rem(s, 4), 128)
                    block = jnp.where(case_of == k, pltpu.roll(staged[side * 4 + k, rows, :], turn, 1), block)
                high, low = halves(block)
                a_high[rows, side * 128 : side * 128 + 128] = high
                a_low[rows, side * 128 : side * 128 + 128] = low
            return 0

        lax.fori_loop(0, 16, pick, 0)


    def send_restricted(k):
        out = dot(e_turn[...], lb[...])
        s1[k] = (out[:, 0:128] + out[:, 128:256]).reshape(NS, 8, 128)
        for who in str_peers:
            remote(s1.at[k, who[0]], r1.at[k, s], send_sem.at[k, 0], recv_sem.at[k, 0], who).start()
        r1[k, s] = s1[k, s]

    def send_chunk(k, tile):
        arrived(r1.at[k, 0 : NS - 1], recv_sem.at[k, 0])
        s2[k, 0:8, :] = jnp.sum(r1[k], axis=0)
        s2[k, 8:12, :] = tile[0:4]
        for who in crs_peers:
            remote(s2.at[k], r2.at[k, c], send_sem.at[k, 1], recv_sem.at[k, 1], who).start()
        r2[k, c] = s2[k]

    def send_product(k):
        arrived(r2.at[k, 0 : NC - 1], recv_sem.at[k, 1])
        total = jnp.sum(r2[k], axis=0)
        t = total[0:8]
        t_tile[...] = t
        placed = jnp.concatenate([jnp.broadcast_to(t[i : i + 1], (ROWS, 128)) * spot for i in range(NC)], axis=0)
        high, low = halves(placed)
        both = dot(jnp.concatenate([high, low], axis=0), ones_pair[0:128, :]).astype(BF16)
        right = jnp.concatenate([both[0:256], both[256:512]], axis=1)
        out = dot(a_high[...], right)
        out = out[:, 0:128] + out[:, 128:256] + dot(a_low[...], both[0:256])
        y = jnp.sum(out.reshape(16, ROWS, 128) * spot[None], axis=1)
        s3[k, 0:16, :] = y
        own = t_tile[pl.ds(c, 1), :]
        s3[k, 16:20, :] = jnp.where(sub8[0:4] == 0, jnp.broadcast_to(own, (4, 128)), total[8:12])
        for who in str_peers:
            remote(s3.at[k], r3.at[k, s], send_sem.at[k, 2], recv_sem.at[k, 2], who).start()
        r3[k, s] = s3[k]

    RZ, RR, ALPHA, BETA, RQ, QQ = range(6)

    def row(x, i):
        return jnp.broadcast_to(x[i : i + 1], (8, 128))

    def send_correction(k, first=False):
        arrived(r3.at[k, 0 : NS - 1], recv_sem.at[k, 2])
        total = jnp.sum(r3[k], axis=0)
        y = total[0:16]
        t = jnp.concatenate([r3[k, i, 16:17, :] for i in range(NS)], axis=0)
        sums = total[16:20]
        if first:
            state[RR] = row(sums, 1)
        else:
            alpha = state[RZ] / row(sums, 1)
            state[ALPHA] = alpha
            state[QQ] = row(sums, 2)
            state[RQ] = row(sums, 3)
            y = y_now[...] - alpha[0:1] * y
            t = t_now[...] - alpha[0:1] * t
        y_now[...] = y
        t_now[...] = t
        s4[k, 0:16, :] = y
        s4[k, 16:17, :] = jnp.sum(y * t, axis=0, keepdims=True)
        for who in crs_peers:
            remote(s4.at[k], r4.at[k, c], send_sem.at[k, 3], recv_sem.at[k, 3], who).start()
        r4[k, c] = s4[k]

    def to_cases(slot, x):
        for case in range(CASES):
            per_case[slot, case] = jnp.broadcast_to(x[:, case * 32 : case * 32 + 1], (8, 128))

    def receive_correction(k, first=False):
        arrived(r4.at[k, 0 : NC - 1], recv_sem.at[k, 3])
        correction = jnp.concatenate([r4[k, i, 0:16, :] for i in range(NC)], axis=0)
        high, low = halves(correction)
        picked = dot(e_low[...], jnp.concatenate([high, low], axis=1))
        mask = m_high[...]
        gm[:, 0:128] = (picked[:, 0:128] * mask).astype(BF16)
        gm[:, 128:256] = (picked[:, 128:256] * mask).astype(BF16)
        cb[...] = dot(gm[...], ones_pair[...])
        coarse = case_sums(jnp.broadcast_to(jnp.sum(r4[k, :, 16:17, :], axis=0), (8, 128)))
        if first:
            state[RZ] = state[RR] + coarse
        else:
            alpha = state[ALPHA]
            smooth = state[RR] - 2.0 * alpha * state[RQ] + alpha * alpha * state[QQ]
            fresh = smooth + coarse
            state[RR] = smooth
            state[BETA] = fresh / state[RZ]
            state[RZ] = fresh
            to_cases(0, alpha)
            to_cases(1, state[BETA])

    def block_level(final=False):
        alpha = state[ALPHA][0:1]
        beta = state[BETA][0:1]

        def body(j, energy):
            base = pl.multiple_of((j + 1) * STEP, 8)
            flat = pl.ds(pl.multiple_of(j * ROWS, ROWS), ROWS)
            value = bu[flat, :] - alpha * bw[flat, :]
            if not final:
                bu[flat, :] = value
            value = value + beta * bq[flat, :]
            here = cb[pl.ds(base, ROWS), :]
            stencil = (
                sd[flat, :] * here
                - ss[flat, :] * cb[pl.ds(base + 1, ROWS), :]
                - su[flat, :] * cb[pl.ds(base - 1, ROWS), :]
                - er[flat, :] * cb[pl.ds(base + STEP, ROWS), :]
                - el[flat, :] * cb[pl.ds(base - STEP, ROWS), :]
            )
            if final:
                return energy + fold(here * (stencil + 2.0 * value))
            value = value + stencil
            bq[flat, :] = value
            to_scatter(j, base, value)
            return energy

        return lax.fori_loop(0, BLOCKS, body, zero)


    def widen_correction():
        wide = dot(gm[...], ones_wide[...])
        for case in range(CASES):
            pcf[case * FIELD : case * FIELD + FIELD, :] = wide[:, case * 128 : case * 128 + 128]

    def next_direction(final=False):
        widen_correction()
        kinds = 0 if final else 5

        def body(j, sums):
            base = pl.multiple_of((j + 1) * STEP, 8)
            cols = pl.ds(pl.multiple_of(j * 128, 128), 128)
            link = links(j, base)
            out = []
            for case in range(CASES):
                at = pl.ds(case * FIELD + base, ROWS)
                here, image = jacobian(pcf, case, base, link)
                rest = rf[at, :]
                inverse = inf[at, :]
                alpha = per_case[0, case][0:1]
                beta = per_case[1, case][0:1]
                last_image = qf[at, :]
                last_direction = df[at, :]
                smooth = uf[at, :] - alpha * wf[at, :]
                image = image + beta * last_image + smooth
                rest = rest - alpha * last_image
                step = xf[at, :] + alpha * last_direction
                direction = rest * inverse + here + beta * last_direction
                if final:
                    xn[case, :, cols] = step
                    vn[case, :, cols] = rest
                    dn[case, :, cols] = direction
                    pn[case, :, cols] = image
                    continue
                uf[at, :] = smooth
                rf[at, :] = rest
                xf[at, :] = step
                qf[at, :] = image
                df[at, :] = direction
                scaled = image * inverse
                ef[at, :] = scaled
                terms = [direction * image, image * scaled, rest * scaled, rest * inverse * smooth, scaled * smooth]
                out.extend(sums[kinds * case + i] + fold(terms[i]) for i in range(kinds))
            return tuple(out)

        sums = lax.fori_loop(0, BLOCKS, body, (zero,) * (kinds * CASES))
        tile = zero
        for kind in range(kinds):
            one = by_case([sums[kinds * case + kind] for case in range(CASES)])
            tile = jnp.where(sub8 == kind + 1, one, tile)
        return tile

    def start_halo(k):
        edges_out(ef, hu_s.at[k], hd_s.at[k], hl_s.at[k], hr_s.at[k])
        bufs = [ref.at[k] for ref in (hu_s, hd_s, hl_s, hr_s, hd_r, hu_r, hl_r, hr_r)]
        return exchange(bufs, halo_send.at[k], halo_recv.at[k])

    def apply_scaled(k, copies, target, sums_to):
        for copy in copies:
            copy.wait()
        edges_in(ef, hd_r.at[k], hu_r.at[k], hl_r.at[k], hr_r.at[k])

        def body(j, sums):
            base = pl.multiple_of((j + 1) * STEP, 8)
            link = links(j, base)
            values, out = [], []
            for case in range(CASES):
                here, image = jacobian(ef, case, base, link)
                target[pl.ds(case * FIELD + base, ROWS), :] = image
                values.append(image)
                out.append(sums[case] + fold(here * image))
            block_columns(j, base, values, sums_to)
            return tuple(out)

        return lax.fori_loop(0, BLOCKS, body, (zero,) * CASES)


    send_restricted(0)
    start_sums = lax.fori_loop(0, BLOCKS, start_scaled, (zero,) * CASES)
    tile = jnp.where(sub8 == 1, by_case(start_sums), zero)
    copies = start_halo(0)
    send_chunk(0, tile)
    prepare_rest()
    send_product(0)
    apply_scaled(0, copies, uf, bu)
    send_correction(0, first=True)
    receive_correction(0, first=True)

    def solve(k, _):
        block_level()
        send_restricted(k)
        tile = next_direction()
        local[...] = tile
        copies = start_halo(k)
        send_chunk(k, tile)
        send_product(k)
        local_w[...] = by_case(apply_scaled(k, copies, wf, bw))
        send_correction(k)
        receive_correction(k)
        return 0

    lax.fori_loop(1, SOLVES, solve, 0)


    alpha = state[ALPHA]
    beta = state[BETA]
    energy = jnp.sum(block_level(final=True), axis=0, keepdims=True)
    dq, qq, rq, eu, qu = (row(local[...], i) for i in range(1, 6))
    energy = (
        energy
        + (eu - 2.0 * alpha * qu + alpha * alpha * local_w[...])
        + 2.0 * beta * (rq - alpha * qq)
        + beta * beta * dq
    )
    here = s * NC + c
    fs[...] = energy[0:1]
    for _, who in everyone:
        remote(fs, fr.at[here], last_send.at[0], last_recv.at[0], who).start()
    fr[here] = fs[...]
    next_direction(final=True)
    stores = [
        pltpu.make_async_copy(src, dst, out_sem.at[i])
        for i, (src, dst) in enumerate(((xn, xf_out), (dn, df_out), (vn, rf_out), (pn, qf_out)))
    ]
    for copy in stores:
        copy.start()
    arrived(fr.at[0 : NS * NC - 1], last_recv.at[0])
    alpha = state[RZ] / jnp.broadcast_to(jnp.sum(fr[...], axis=0), (8, 128))
    for case in range(CASES):
        alpha_out[case : case + 1, :] = jnp.broadcast_to(alpha[0:1, case * 32 : case * 32 + 1], (1, 2048))


    for copy in stores:
        copy.wait()

    for k in range(SOLVES):
        arrived(r1.at[k, 0 : NS - 1], send_sem.at[k, 0])
        arrived(r2.at[k, 0 : NC - 1], send_sem.at[k, 1])
        arrived(r3.at[k, 0 : NS - 1], send_sem.at[k, 2])
        arrived(r4.at[k, 0 : NC - 1], send_sem.at[k, 3])
    arrived(fr.at[0 : NS * NC - 1], last_send.at[0])


def shards(voltage, photocurrent, shunt, series, pattern, diode_mask, aggregate, coarse_inverse):
    field = (CASES * FIELD, 128)
    flat = (BLOCKS * ROWS, 128)

    def vmem(shape, dtype=F32):
        return pltpu.VMEM(shape, dtype)

    dma = pltpu.SemaphoreType.DMA
    scratch = [
        *[vmem((CASES, ROWS, 2048)) for _ in range(4)], vmem((ROWS, 2048)), vmem((ROWS, 2048)),
        vmem((BLOCKS, ROWS), jnp.int32), vmem((BLOCKS, ROWS), jnp.int32), vmem((BLOCKS, ROWS), jnp.int32),
        vmem((NC, 512, 128)), vmem((512, 256), BF16), vmem((512, 256), BF16),
        *[vmem(field) for _ in range(10)],
        vmem((FIELD, 128)), vmem(flat), vmem(flat), vmem(flat),
        vmem((FIELD, 128)), vmem((FIELD, 256), BF16), vmem((FIELD, 128), BF16), vmem((FIELD, 128)),
        vmem((FIELD, 128), jnp.int32), vmem((128, 512), BF16), vmem((256, 128), BF16), vmem((256, 512), BF16),
        *[vmem(flat) for _ in range(9)], vmem((512, 256), BF16),
        vmem((ROWS, 128)), vmem((128, 128)),
        vmem((72, 128)), vmem((88, 128)), vmem((8, 128)), vmem((8, 128)),
        vmem((72, 128)), vmem((88, 128)), vmem((8, 128)), vmem((8, 128)),
        vmem((SOLVES, 64, 128)), vmem((SOLVES, 64, 128)), vmem((SOLVES, 8, 128)), vmem((SOLVES, 8, 128)),
        vmem((SOLVES, 64, 128)), vmem((SOLVES, 64, 128)), vmem((SOLVES, 8, 128)), vmem((SOLVES, 8, 128)),
        vmem((SOLVES, NS, 8, 128)), vmem((SOLVES, NS, 8, 128)),
        vmem((SOLVES, 12, 128)), vmem((SOLVES, NC, 12, 128)),
        vmem((SOLVES, 20, 128)), vmem((SOLVES, NS, 20, 128)),
        vmem((SOLVES, 17, 128)), vmem((SOLVES, NC, 17, 128)),
        vmem((1, 128)), vmem((NS * NC, 1, 128)),
        vmem((16, 128)), vmem((16, 128)), vmem((8, 128)), vmem((6, 8, 128)), vmem((2, CASES, 8, 128)), vmem((8, 128)), vmem((8, 128)),
        dma((15,)), dma((4,)), dma((4,)), dma((4,)), dma((SOLVES, 4)), dma((SOLVES, 4)),
        dma((SOLVES, 4)), dma((SOLVES, 4)), dma((1,)), dma((1,)),
    ]
    tall = jax.ShapeDtypeStruct((CASES, ROWS, 2048), F32)
    step, direction, rest, image, alpha = pl.pallas_call(
        kernel,
        out_shape=[tall] * 4 + [jax.ShapeDtypeStruct((CASES, 2048), F32)],
        in_specs=[pl.BlockSpec(memory_space=pltpu.HBM)] * 8,
        out_specs=[pl.BlockSpec(memory_space=pltpu.HBM)] * 4 + [pl.BlockSpec(memory_space=pltpu.VMEM)],
        scratch_shapes=scratch,
        compiler_params=pltpu.CompilerParams(collective_id=0, has_side_effects=True, vmem_limit_bytes=54 * 2**20),
        name="newton",
    )(voltage, photocurrent, shunt, series, pattern.T, diode_mask.T, aggregate.T, coarse_inverse)
    alpha = alpha[:, None, :]
    return step + alpha * direction, rest - alpha * image


def solution(mesh):
    field = P(None, "str", "crs")
    plane = P("str", "crs")
    return jax.shard_map(
        shards,
        mesh=mesh,
        in_specs=(field, field, plane, plane, plane, plane, plane, P("crs", None)),
        out_specs=(field, field),
        check_vma=False,
    )
```

```python
import itertools

import jax
import jax.numpy as jnp
from jax import lax
from jax.experimental import pallas as pl
from jax.experimental.pallas import tpu as pltpu
from jax.sharding import PartitionSpec as P

MESH = pl.DeviceIdType.MESH
F32 = jnp.float32
BF16 = jnp.bfloat16

CASES = 4
ROWS = 32
BLOCKS = 16
STEP = 40
FIELD = (BLOCKS + 2) * STEP
NS = 16
NC = 8
SOLVES = 3
LEVELS = (0.25, 0.5, 1.0, 2.0)


def dot(a, b):
    return jnp.dot(a, b, preferred_element_type=F32)


def halves(x):
    high = x.astype(BF16)
    return high, (x - high.astype(F32)).astype(BF16)


def kernel(
    v_in, photo_in, shunt_in, series_in, pattern_in, mask_in, group_in, inverse_in,
    xf_out, df_out, rf_out, qf_out, alpha_out,
    xn, dn, vn, pn, shn, sn, patn, maskn, groupn, staged, a_high, a_low,
    ef, rf, qf, df, xf, uf, wf, dgf, inf, pcf,
    sf, rlf, llf, dmf,
    cb, gm, e_low, m_high, groups, e_turn, ones_pair, ones_wide,
    bu, bw, bq, br, sd, ss, su, er, el, lb,
    pk, turned, su_s, sd_s, sl_s, sr_s, su_r, sd_r, sl_r, sr_r,
    hu_s, hd_s, hl_s, hr_s, hu_r, hd_r, hl_r, hr_r,
    s1, r1, s2, r2, s3, r3, s4, r4, fs, fr,
    y_now, t_now, t_tile, state, per_case, local, local_w,
    in_sem, out_sem, setup_send, setup_recv, halo_send, halo_recv, send_sem, recv_sem, last_send, last_recv,
):
    s = lax.axis_index("str")
    c = lax.axis_index("crs")

    def at_str(k):
        return (lax.rem(s + k, NS), c)

    def at_crs(k):
        return (s, lax.rem(c + k, NC))

    str_at = {}
    for key in itertools.product(range(2), range(4), range(2)):
        x_lo, y, core = (lax.rem(p + k, n) for p, k, n in zip((s // 8, lax.rem(s // 2, 4), lax.rem(s, 2)), key, (2, 4, 2)))
        str_at[key] = (x_lo * 4 + y) * 2 + core
    crs_at = {}
    for key in itertools.product(range(2), range(4)):
        x_hi, z = (lax.rem(p + k, n) for p, k, n in zip((c // 4, lax.rem(c, 4)), key, (2, 4)))
        crs_at[key] = x_hi * 4 + z

    def far_first(key):
        x_lo, y, core, x_hi, z = key
        across = 1 if x_lo else 2 * x_hi
        return -(across + min(y, 4 - y) + min(z, 4 - z) + 0.5 * core)

    everyone = sorted(itertools.product(range(2), range(4), range(2), range(2), range(4)), key=far_first)[:-1]
    everyone = [(key, (str_at[key[:3]], crs_at[key[3:]])) for key in everyone]
    str_peers = [(who[0], c) for key, who in everyone if key[3:] == (0, 0)]
    crs_peers = [(s, who[1]) for key, who in everyone if key[:3] == (0, 0, 0)]

    barrier = pltpu.get_barrier_semaphore()
    for who in str_peers + crs_peers:
        pl.semaphore_signal(barrier, inc=1, device_id=who, device_id_type=MESH)

    loads = [
        pltpu.make_async_copy(v_in, vn, in_sem.at[0]),
        pltpu.make_async_copy(series_in, sn, in_sem.at[1]),
        pltpu.make_async_copy(pattern_in, patn, in_sem.at[2]),
        pltpu.make_async_copy(mask_in, maskn, in_sem.at[3]),
        pltpu.make_async_copy(group_in, groupn, in_sem.at[4]),
        pltpu.make_async_copy(shunt_in, shn, in_sem.at[5]),
        pltpu.make_async_copy(photo_in, pn, in_sem.at[6]),
    ]
    quarter = pl.multiple_of((s // 4) * 128, 128)
    for k in range(NC):
        loads.append(
            pltpu.make_async_copy(
                inverse_in.at[:, pl.ds(pl.multiple_of(k * 512 + quarter, 128), 128)], staged.at[k], in_sem.at[7 + k]
            )
        )
    for copy in loads:
        copy.start()

    lane = lax.broadcasted_iota(jnp.int32, (ROWS, 128), 1)
    case_of = lane // 32
    is_first = lane == 0
    is_last = lane == 127
    case8 = case_of[0:8]
    sub8 = lax.broadcasted_iota(jnp.int32, (8, 128), 0)
    spot = (lax.broadcasted_iota(jnp.int32, (ROWS, 128), 0) == lane - 32 * case_of).astype(F32)

    def remote(src, dst, send, recv, who):
        return pltpu.make_async_remote_copy(
            src_ref=src, dst_ref=dst, send_sem=send, recv_sem=recv, device_id=who, device_id_type=MESH
        )

    def arrived(ref, sem):
        pltpu.make_async_copy(ref, ref, sem).wait()

    def rows_of(case, row):
        return pl.ds(case * FIELD + STEP + row, BLOCKS, stride=STEP)

    def edges_out(f, up, down, left, right):
        for case in range(CASES):
            up[case * 16 : case * 16 + 16, :] = f[rows_of(case, 0), :]
            down[case * 16 : case * 16 + 16, :] = f[rows_of(case, ROWS - 1), :]
        for block, ref in ((0, left), (BLOCKS - 1, right)):
            first = (block + 1) * STEP
            tile = jnp.concatenate(
                [f[case * FIELD + first : case * FIELD + first + ROWS, :] for case in range(CASES)], axis=0
            ).T
            ref[0:8, :] = tile[0:8] if block == 0 else tile[120:128]

    def edges_in(f, above, below, left, right):
        for case in range(CASES):
            f[rows_of(case, -1), :] = above[case * 16 : case * 16 + 16, :]
            f[rows_of(case, ROWS), :] = below[case * 16 : case * 16 + 16, :]
        for first, row in ((0, left[7:8, :]), (17 * STEP, right[0:1, :])):
            tile = jnp.broadcast_to(row, (128, 128)).T
            for case in range(CASES):
                f[case * FIELD + first : case * FIELD + first + ROWS, :] = tile[case * ROWS : case * ROWS + ROWS]

    def exchange(bufs, send, recv):
        up_s, down_s, left_s, right_s, above_r, below_r, left_r, right_r = bufs
        copies = [
            remote(up_s, below_r, send.at[0], recv.at[0], at_str(NS - 1)),
            remote(down_s, above_r, send.at[1], recv.at[1], at_str(1)),
            remote(left_s, right_r, send.at[2], recv.at[2], at_crs(NC - 1)),
            remote(right_s, left_r, send.at[3], recv.at[3], at_crs(1)),
        ]
        for copy in copies:
            copy.start()
        return copies

    def neighbours(f, case, base):
        def part(shift):
            return f[pl.ds(case * FIELD + base + shift, ROWS), :]

        here = part(0)
        right = pltpu.roll(jnp.where(is_first, part(STEP), here), 127, 1)
        left = pltpu.roll(jnp.where(is_last, part(-STEP), here), 1, 1)
        return here, part(1), part(-1), right, left

    def links(j, base):
        flat = pl.ds(pl.multiple_of(j * ROWS, ROWS), ROWS)
        return sf[pl.ds(base, ROWS), :], sf[pl.ds(base - 1, ROWS), :], rlf[flat, :], llf[flat, :]

    def jacobian(f, case, base, link):
        down, up, right_link, left_link = link
        here, below, above, right, left = neighbours(f, case, base)
        diagonal = dgf[pl.ds(case * FIELD + base, ROWS), :]
        return here, diagonal * here - down * below - up * above - right_link * right - left_link * left

    def fold(x):
        return x[0:8] + x[8:16] + x[16:24] + x[24:32]

    def by_case(parts):
        total = jnp.zeros((8, 128), F32)
        for case in range(CASES):
            total = jnp.where(case8 == case, jnp.sum(parts[case], axis=(0, 1), keepdims=True), total)
        return total

    def case_sums(x):
        total = jnp.zeros((8, 128), F32)
        for case in range(CASES):
            one = jnp.sum(jnp.where(case8 == case, x, 0.0), axis=1, keepdims=True)
            total = jnp.where(case8 == case, one, total)
        return total


    def spread(x, column, rows=ROWS):
        return jnp.broadcast_to(x[:, column : column + 1], (rows, 128))

    def clear(i, _):
        rows = pl.ds(pl.multiple_of(i * 80, 16), 80)
        for f in (ef, wf, qf, df, xf):
            f[rows, :] = jnp.zeros((80, 128), F32)
        return 0

    lax.fori_loop(0, CASES * FIELD // 80, clear, 0)
    sf[...] = jnp.zeros_like(sf)
    bw[...] = jnp.zeros_like(bw)
    bq[...] = jnp.zeros_like(bq)
    state[...] = jnp.zeros_like(state)
    per_case[...] = jnp.zeros_like(per_case)
    for copy in loads[:5]:
        copy.wait()
    level = jnp.zeros((BLOCKS, ROWS), F32)
    for number in range(4):
        level = level + jnp.where(patn[...] == number, F32(LEVELS[number]), F32(0.0))
    turned[...] = jnp.zeros_like(turned)
    turned[0:16, 0:32] = groupn[...].astype(F32)
    turned[16:32, 0:32] = level
    turned[32:48, 0:32] = maskn[...].astype(F32) * 0.5
    pk[...] = turned[...].T[0:ROWS]
    packed = pk[...]

    def lay_out(j, _):
        base = pl.multiple_of((j + 1) * STEP, 8)
        cols = pl.ds(pl.multiple_of(j * 128, 128), 128)
        for case in range(CASES):
            ef[pl.ds(case * FIELD + base, ROWS), :] = vn[case, :, cols]
        sf[pl.ds(base, ROWS), :] = sn[:, cols]
        return 0

    lax.fori_loop(0, BLOCKS, lay_out, 0)
    edges_out(ef, su_s, sd_s, sl_s, sr_s)
    su_s[64:72, :] = packed[0:8]
    sd_s[64:72, :] = packed[24:32]
    sd_s[72:88, :] = sf[pl.ds(STEP + ROWS - 1, BLOCKS, stride=STEP), :]
    sl_s[1:2, :] = turned[0:1, :]
    sl_s[2:3, :] = turned[16:17, :]
    sr_s[1:2, :] = turned[15:16, :]
    sr_s[2:3, :] = turned[31:32, :]

    pl.semaphore_wait(barrier, NS - 1 + NC - 1)
    setup_copies = exchange((su_s, sd_s, sl_s, sr_s, sd_r, su_r, sl_r, sr_r), setup_send, setup_recv)

    groups[...] = jnp.zeros_like(groups)
    for j in range(BLOCKS):
        base = (j + 1) * STEP
        group = spread(packed, j).astype(jnp.int32)
        groups[base : base + ROWS, :] = group
        low = group // 32
        code = (low % 16) * 8 + low // 16
        lb[j * ROWS : j * ROWS + ROWS, 0:128] = (lane == code).astype(F32).astype(BF16)
        dmf[j * ROWS : j * ROWS + ROWS, :] = spread(packed, 32 + j)
    for k in range(4):
        e_turn[:, k * 128 : k * 128 + 128] = lb[k * 128 : k * 128 + 128, 0:128].astype(F32).T.astype(BF16)

    same = lax.broadcasted_iota(jnp.int32, (128, 128), 0) // 32
    across = lax.broadcasted_iota(jnp.int32, (128, 128), 1) // 32
    block_ones = (same == across).astype(F32).astype(BF16)
    ones_pair[0:128, :] = block_ones
    ones_pair[128:256, :] = block_ones
    for case in range(CASES):
        wide = (same == case).astype(F32).astype(BF16)
        ones_wide[0:128, case * 128 : case * 128 + 128] = wide
        ones_wide[128:256, case * 128 : case * 128 + 128] = wide

    row_levels = [spread(packed, 16 + j) for j in range(BLOCKS)]
    blank = jnp.zeros((ROWS, 128), F32)
    row_levels = [blank] + row_levels + [blank]
    for j in range(BLOCKS):
        here = row_levels[j + 1]
        right = jnp.minimum(here, row_levels[j + 2])
        left = jnp.minimum(here, row_levels[j])
        rlf[j * ROWS : j * ROWS + ROWS, :] = jnp.where(is_last, right, here)
        llf[j * ROWS : j * ROWS + ROWS, :] = jnp.where(is_first, left, here)
        er[j * ROWS : j * ROWS + ROWS, :] = right
        el[j * ROWS : j * ROWS + ROWS, :] = left

    def block_columns(j, base, sums, target):
        total = jnp.zeros((ROWS, 128), F32)
        for case in range(CASES):
            total = jnp.where(case_of == case, jnp.sum(sums[case], axis=1, keepdims=True), total)
        if target is not None:
            target[pl.ds(pl.multiple_of(j * ROWS, ROWS), ROWS), :] = total
        return total

    def to_scatter(j, base, total):
        flat = pl.ds(pl.multiple_of(j * ROWS, ROWS), ROWS)
        high, low = halves(total * m_high[pl.ds(base, ROWS), :])
        lb[flat, 0:128] = high
        lb[flat, 128:256] = low

    def codes(i, _):
        rows = pl.ds(pl.multiple_of(i * 80, 16), 80)
        group = groups[rows, :]
        lanes = lax.broadcasted_iota(jnp.int32, (80, 128), 1)
        e_low[rows, :] = (lanes == group // 32).astype(F32).astype(BF16)
        m_high[rows, :] = (lanes % 32 == group % 32).astype(F32)
        return 0

    lax.fori_loop(0, FIELD // 80, codes, 0)
    for copy in loads[5:7]:
        copy.wait()

    def start_rest(j, _):
        base = pl.multiple_of((j + 1) * STEP, 8)
        cols = pl.ds(pl.multiple_of(j * 128, 128), 128)
        flat = pl.ds(pl.multiple_of(j * ROWS, ROWS), ROWS)
        down, up, right_link, left_link = links(j, base)
        shunt = shn[:, cols]
        half = dmf[flat, :]
        rests = []
        for case in range(CASES):
            at = pl.ds(case * FIELD + base, ROWS)
            here, below, above, right, left = neighbours(ef, case, base)
            slope = half * jnp.exp(here)
            rest = pn[case, :, cols] - (
                shunt * here
                + down * (here - below)
                + up * (here - above)
                + right_link * (here - right)
                + left_link * (here - left)
                + slope
                - half
            )
            dgf[at, :] = slope
            rf[at, :] = rest
            rests.append(rest)
        block_columns(j, base, rests, br)
        return 0

    def start_scaled(j, sums):
        base = pl.multiple_of((j + 1) * STEP, 8)
        cols = pl.ds(pl.multiple_of(j * 128, 128), 128)
        flat = pl.ds(pl.multiple_of(j * ROWS, ROWS), ROWS)
        down, up, right_link, left_link = links(j, base)
        shunt = shn[:, cols]
        edge = jnp.where(is_last, right_link, 0.0) + jnp.where(is_first, left_link, 0.0)
        out, plain = [], []
        for case in range(CASES):
            at = pl.ds(case * FIELD + base, ROWS)
            ground = shunt + dgf[at, :] + down + up
            diagonal = ground + right_link + left_link
            inverse = 1.0 / diagonal
            rest = rf[at, :]
            scaled = rest * inverse
            dgf[at, :] = diagonal
            inf[at, :] = inverse
            ef[at, :] = scaled
            out.append(sums[case] + fold(rest * scaled))
            plain.append(ground + edge)
        block_columns(j, base, plain, sd)
        ss[flat, :] = jnp.broadcast_to(jnp.sum(down, axis=1, keepdims=True), (ROWS, 128))
        su[flat, :] = jnp.broadcast_to(jnp.sum(up, axis=1, keepdims=True), (ROWS, 128))
        return tuple(out)

    zero = jnp.zeros((8, 128), F32)
    lax.fori_loop(0, BLOCKS, start_rest, 0)

    for copy in setup_copies:
        copy.wait()
    edges_in(ef, sd_r, su_r, sl_r, sr_r)
    sf[pl.ds(STEP - 1, BLOCKS, stride=STEP), :] = sd_r[72:88, :]
    open_left = jnp.where(c == 0, 0.0, 1.0).astype(F32)
    open_right = jnp.where(c == NC - 1, 0.0, 1.0).astype(F32)
    level_left = jnp.broadcast_to(sl_r[2:3, :], (128, 128)).T[0:ROWS]
    level_right = jnp.broadcast_to(sr_r[2:3, :], (128, 128)).T[0:ROWS]
    for block, slot, level_there, is_open, is_edge, link, edge in (
        (0, 0, level_left, open_left, is_first, llf, el),
        (BLOCKS - 1, BLOCKS + 1, level_right, open_right, is_last, rlf, er),
    ):
        rows = pl.ds(block * ROWS, ROWS)
        here = row_levels[block + 1]
        value = jnp.minimum(here, level_there) * is_open
        link[rows, :] = jnp.where(is_edge, value, here)
        edge[rows, :] = value
        total = br[rows, :]
        for case in range(CASES):
            at = pl.ds(case * FIELD + (block + 1) * STEP, ROWS)
            there = ef[pl.ds(case * FIELD + slot * STEP, ROWS), :]
            more = jnp.where(is_edge, value * (there - ef[at, :]), 0.0)
            rf[at, :] = rf[at, :] + more
            total = total + jnp.where(case_of == case, jnp.sum(more, axis=1, keepdims=True), 0.0)
        br[rows, :] = total
    for first in (True, False):
        edge_row = 0 if first else ROWS - 1
        link = sf[pl.ds(STEP + (-1 if first else edge_row), BLOCKS, stride=STEP), :]
        rows = pl.ds(edge_row, BLOCKS, stride=ROWS)
        total = br[rows, :]
        for case in range(CASES):
            if first:
                more = link * (ef[rows_of(case, -1), :] - ef[rows_of(case, 0), :])
            else:
                more = link * ef[rows_of(case, ROWS), :]
            rf[rows_of(case, edge_row), :] = rf[rows_of(case, edge_row), :] + more
            total = total + jnp.where(case_of[0:BLOCKS] == case, jnp.sum(more, axis=1, keepdims=True), 0.0)
        br[rows, :] = total

    def scatter_rest(j, _):
        to_scatter(j, pl.multiple_of((j + 1) * STEP, 8), br[pl.ds(pl.multiple_of(j * ROWS, ROWS), ROWS), :])
        return 0

    lax.fori_loop(0, BLOCKS, scatter_rest, 0, unroll=4)

    def prepare_rest():
        above8 = sd_r[64:72, :]
        below8 = su_r[64:72, :]
        for j in range(BLOCKS):
            base = (j + 1) * STEP
            groups[base - 1 : base, :] = spread(above8, j, 8)[7:8].astype(jnp.int32)
            groups[base + ROWS : base + ROWS + 1, :] = spread(below8, j, 8)[0:1].astype(jnp.int32)
        for first, row_there in ((0, sl_r[1:2, :]), (17 * STEP, sr_r[1:2, :])):
            groups[first : first + ROWS, :] = jnp.broadcast_to(row_there, (128, 128)).T[0:ROWS].astype(jnp.int32)
        lax.fori_loop(0, FIELD // 80, codes, 0)
        for copy in loads[7:]:
            copy.wait()

        def pick(i, _):
            rows = pl.ds(pl.multiple_of(i * 32, 32), 32)
            for side in range(2):
                block = jnp.zeros((ROWS, 128), F32)
                for k in range(4):
                    turn = lax.rem(32 * k + 128 - 32 * lax.rem(s, 4), 128)
                    block = jnp.where(case_of == k, pltpu.roll(staged[side * 4 + k, rows, :], turn, 1), block)
                high, low = halves(block)
                a_high[rows, side * 128 : side * 128 + 128] = high
                a_low[rows, side * 128 : side * 128 + 128] = low
            return 0

        lax.fori_loop(0, 16, pick, 0)


    def send_restricted(k):
        out = dot(e_turn[...], lb[...])
        s1[k] = (out[:, 0:128] + out[:, 128:256]).reshape(NS, 8, 128)
        for who in str_peers:
            remote(s1.at[k, who[0]], r1.at[k, s], send_sem.at[k, 0], recv_sem.at[k, 0], who).start()
        r1[k, s] = s1[k, s]

    def send_chunk(k, tile):
        arrived(r1.at[k, 0 : NS - 1], recv_sem.at[k, 0])
        s2[k, 0:8, :] = jnp.sum(r1[k], axis=0)
        s2[k, 8:12, :] = tile[0:4]
        for who in crs_peers:
            remote(s2.at[k], r2.at[k, c], send_sem.at[k, 1], recv_sem.at[k, 1], who).start()
        r2[k, c] = s2[k]

    def send_product(k):
        arrived(r2.at[k, 0 : NC - 1], recv_sem.at[k, 1])
        total = jnp.sum(r2[k], axis=0)
        t = total[0:8]
        t_tile[...] = t
        placed = jnp.concatenate([jnp.broadcast_to(t[i : i + 1], (ROWS, 128)) * spot for i in range(NC)], axis=0)
        high, low = halves(placed)
        both = dot(jnp.concatenate([high, low], axis=0), ones_pair[0:128, :]).astype(BF16)
        right = jnp.concatenate([both[0:256], both[256:512]], axis=1)
        out = dot(a_high[...], right)
        out = out[:, 0:128] + out[:, 128:256] + dot(a_low[...], both[0:256])
        y = jnp.sum(out.reshape(16, ROWS, 128) * spot[None], axis=1)
        s3[k, 0:16, :] = y
        own = t_tile[pl.ds(c, 1), :]
        s3[k, 16:20, :] = jnp.where(sub8[0:4] == 0, jnp.broadcast_to(own, (4, 128)), total[8:12])
        for who in str_peers:
            remote(s3.at[k], r3.at[k, s], send_sem.at[k, 2], recv_sem.at[k, 2], who).start()
        r3[k, s] = s3[k]

    RZ, RR, ALPHA, BETA, RQ, QQ = range(6)

    def row(x, i):
        return jnp.broadcast_to(x[i : i + 1], (8, 128))

    def send_correction(k, first=False):
        arrived(r3.at[k, 0 : NS - 1], recv_sem.at[k, 2])
        total = jnp.sum(r3[k], axis=0)
        y = total[0:16]
        t = jnp.concatenate([r3[k, i, 16:17, :] for i in range(NS)], axis=0)
        sums = total[16:20]
        if first:
            state[RR] = row(sums, 1)
        else:
            alpha = state[RZ] / row(sums, 1)
            state[ALPHA] = alpha
            state[QQ] = row(sums, 2)
            state[RQ] = row(sums, 3)
            y = y_now[...] - alpha[0:1] * y
            t = t_now[...] - alpha[0:1] * t
        y_now[...] = y
        t_now[...] = t
        s4[k, 0:16, :] = y
        s4[k, 16:17, :] = jnp.sum(y * t, axis=0, keepdims=True)
        for who in crs_peers:
            remote(s4.at[k], r4.at[k, c], send_sem.at[k, 3], recv_sem.at[k, 3], who).start()
        r4[k, c] = s4[k]
        if not first:
            bu[...] = bu[...] - alpha[0:1] * bw[...]

    def to_cases(slot, x):
        for case in range(CASES):
            per_case[slot, case] = jnp.broadcast_to(x[:, case * 32 : case * 32 + 1], (8, 128))

    def receive_correction(k, first=False):
        arrived(r4.at[k, 0 : NC - 1], recv_sem.at[k, 3])
        correction = jnp.concatenate([r4[k, i, 0:16, :] for i in range(NC)], axis=0)
        high, low = halves(correction)
        picked = dot(e_low[...], jnp.concatenate([high, low], axis=1))
        mask = m_high[...]
        gm[:, 0:128] = (picked[:, 0:128] * mask).astype(BF16)
        gm[:, 128:256] = (picked[:, 128:256] * mask).astype(BF16)
        cb[...] = dot(gm[...], ones_pair[...])
        coarse = case_sums(jnp.broadcast_to(jnp.sum(r4[k, :, 16:17, :], axis=0), (8, 128)))
        if first:
            state[RZ] = state[RR] + coarse
        else:
            alpha = state[ALPHA]
            smooth = state[RR] - 2.0 * alpha * state[RQ] + alpha * alpha * state[QQ]
            fresh = smooth + coarse
            state[RR] = smooth
            state[BETA] = fresh / state[RZ]
            state[RZ] = fresh

    def block_level(final=False):
        beta = state[BETA][0:1]

        def body(j, energy):
            base = pl.multiple_of((j + 1) * STEP, 8)
            flat = pl.ds(pl.multiple_of(j * ROWS, ROWS), ROWS)
            value = bu[flat, :] + beta * bq[flat, :]
            here = cb[pl.ds(base, ROWS), :]
            stencil = (
                sd[flat, :] * here
                - ss[flat, :] * cb[pl.ds(base + 1, ROWS), :]
                - su[flat, :] * cb[pl.ds(base - 1, ROWS), :]
                - er[flat, :] * cb[pl.ds(base + STEP, ROWS), :]
                - el[flat, :] * cb[pl.ds(base - STEP, ROWS), :]
            )
            if final:
                return energy + fold(here * (stencil + 2.0 * value))
            value = value + stencil
            bq[flat, :] = value
            to_scatter(j, base, value)
            return energy

        return lax.fori_loop(0, BLOCKS, body, zero, unroll=4)


    def widen_correction():
        wide = dot(gm[...], ones_wide[...])
        for case in range(CASES):
            pcf[case * FIELD : case * FIELD + FIELD, :] = wide[:, case * 128 : case * 128 + 128]

    def next_direction(final=False):
        to_cases(0, state[ALPHA])
        to_cases(1, state[BETA])
        widen_correction()
        kinds = 0 if final else 5

        def body(j, sums):
            base = pl.multiple_of((j + 1) * STEP, 8)
            cols = pl.ds(pl.multiple_of(j * 128, 128), 128)
            link = links(j, base)
            out = []
            for case in range(CASES):
                at = pl.ds(case * FIELD + base, ROWS)
                here, image = jacobian(pcf, case, base, link)
                rest = rf[at, :]
                inverse = inf[at, :]
                alpha = per_case[0, case][0:1]
                beta = per_case[1, case][0:1]
                last_image = qf[at, :]
                last_direction = df[at, :]
                smooth = uf[at, :] - alpha * wf[at, :]
                image = image + beta * last_image + smooth
                rest = rest - alpha * last_image
                step = xf[at, :] + alpha * last_direction
                direction = rest * inverse + here + beta * last_direction
                if final:
                    xn[case, :, cols] = step
                    vn[case, :, cols] = rest
                    dn[case, :, cols] = direction
                    pn[case, :, cols] = image
                    continue
                uf[at, :] = smooth
                rf[at, :] = rest
                xf[at, :] = step
                qf[at, :] = image
                df[at, :] = direction
                scaled = image * inverse
                ef[at, :] = scaled
                terms = [direction * image, image * scaled, rest * scaled, rest * inverse * smooth, scaled * smooth]
                out.extend(sums[kinds * case + i] + fold(terms[i]) for i in range(kinds))
            return tuple(out)

        sums = lax.fori_loop(0, BLOCKS, body, (zero,) * (kinds * CASES))
        tile = zero
        for kind in range(kinds):
            one = by_case([sums[kinds * case + kind] for case in range(CASES)])
            tile = jnp.where(sub8 == kind + 1, one, tile)
        return tile

    def start_halo(k):
        edges_out(ef, hu_s.at[k], hd_s.at[k], hl_s.at[k], hr_s.at[k])
        bufs = [ref.at[k] for ref in (hu_s, hd_s, hl_s, hr_s, hd_r, hu_r, hl_r, hr_r)]
        return exchange(bufs, halo_send.at[k], halo_recv.at[k])

    def apply_scaled(k, copies, target, sums_to):
        for copy in copies:
            copy.wait()
        edges_in(ef, hd_r.at[k], hu_r.at[k], hl_r.at[k], hr_r.at[k])

        def body(j, sums):
            base = pl.multiple_of((j + 1) * STEP, 8)
            link = links(j, base)
            values, out = [], []
            for case in range(CASES):
                here, image = jacobian(ef, case, base, link)
                target[pl.ds(case * FIELD + base, ROWS), :] = image
                values.append(image)
                out.append(sums[case] + fold(here * image))
            block_columns(j, base, values, sums_to)
            return tuple(out)

        return lax.fori_loop(0, BLOCKS, body, (zero,) * CASES)


    send_restricted(0)
    start_sums = lax.fori_loop(0, BLOCKS, start_scaled, (zero,) * CASES)
    tile = jnp.where(sub8 == 1, by_case(start_sums), zero)
    copies = start_halo(0)
    send_chunk(0, tile)
    prepare_rest()
    send_product(0)
    apply_scaled(0, copies, uf, bu)
    send_correction(0, first=True)
    receive_correction(0, first=True)

    def solve(k, _):
        block_level()
        send_restricted(k)
        tile = next_direction()
        local[...] = tile
        copies = start_halo(k)
        send_chunk(k, tile)
        send_product(k)
        local_w[...] = by_case(apply_scaled(k, copies, wf, bw))
        send_correction(k)
        receive_correction(k)
        return 0

    lax.fori_loop(1, SOLVES, solve, 0)


    alpha = state[ALPHA]
    beta = state[BETA]
    energy = jnp.sum(block_level(final=True), axis=0, keepdims=True)
    dq, qq, rq, eu, qu = (row(local[...], i) for i in range(1, 6))
    energy = (
        energy
        + (eu - 2.0 * alpha * qu + alpha * alpha * local_w[...])
        + 2.0 * beta * (rq - alpha * qq)
        + beta * beta * dq
    )
    here = s * NC + c
    fs[...] = energy[0:1]
    for _, who in everyone:
        remote(fs, fr.at[here], last_send.at[0], last_recv.at[0], who).start()
    fr[here] = fs[...]
    next_direction(final=True)
    stores = [
        pltpu.make_async_copy(src, dst, out_sem.at[i])
        for i, (src, dst) in enumerate(((xn, xf_out), (dn, df_out), (vn, rf_out), (pn, qf_out)))
    ]
    for copy in stores:
        copy.start()
    arrived(fr.at[0 : NS * NC - 1], last_recv.at[0])
    alpha = state[RZ] / jnp.broadcast_to(jnp.sum(fr[...], axis=0), (8, 128))
    for case in range(CASES):
        alpha_out[case : case + 1, :] = jnp.broadcast_to(alpha[0:1, case * 32 : case * 32 + 1], (1, 2048))


    for copy in stores:
        copy.wait()

    for k in range(SOLVES):
        arrived(r1.at[k, 0 : NS - 1], send_sem.at[k, 0])
        arrived(r2.at[k, 0 : NC - 1], send_sem.at[k, 1])
        arrived(r3.at[k, 0 : NS - 1], send_sem.at[k, 2])
        arrived(r4.at[k, 0 : NC - 1], send_sem.at[k, 3])
    arrived(fr.at[0 : NS * NC - 1], last_send.at[0])


def shards(voltage, photocurrent, shunt, series, pattern, diode_mask, aggregate, coarse_inverse):
    field = (CASES * FIELD, 128)
    flat = (BLOCKS * ROWS, 128)

    def vmem(shape, dtype=F32):
        return pltpu.VMEM(shape, dtype)

    dma = pltpu.SemaphoreType.DMA
    scratch = [
        *[vmem((CASES, ROWS, 2048)) for _ in range(4)], vmem((ROWS, 2048)), vmem((ROWS, 2048)),
        vmem((BLOCKS, ROWS), jnp.int32), vmem((BLOCKS, ROWS), jnp.int32), vmem((BLOCKS, ROWS), jnp.int32),
        vmem((NC, 512, 128)), vmem((512, 256), BF16), vmem((512, 256), BF16),
        *[vmem(field) for _ in range(10)],
        vmem((FIELD, 128)), vmem(flat), vmem(flat), vmem(flat),
        vmem((FIELD, 128)), vmem((FIELD, 256), BF16), vmem((FIELD, 128), BF16), vmem((FIELD, 128)),
        vmem((FIELD, 128), jnp.int32), vmem((128, 512), BF16), vmem((256, 128), BF16), vmem((256, 512), BF16),
        *[vmem(flat) for _ in range(9)], vmem((512, 256), BF16),
        vmem((ROWS, 128)), vmem((128, 128)),
        vmem((72, 128)), vmem((88, 128)), vmem((8, 128)), vmem((8, 128)),
        vmem((72, 128)), vmem((88, 128)), vmem((8, 128)), vmem((8, 128)),
        vmem((SOLVES, 64, 128)), vmem((SOLVES, 64, 128)), vmem((SOLVES, 8, 128)), vmem((SOLVES, 8, 128)),
        vmem((SOLVES, 64, 128)), vmem((SOLVES, 64, 128)), vmem((SOLVES, 8, 128)), vmem((SOLVES, 8, 128)),
        vmem((SOLVES, NS, 8, 128)), vmem((SOLVES, NS, 8, 128)),
        vmem((SOLVES, 12, 128)), vmem((SOLVES, NC, 12, 128)),
        vmem((SOLVES, 20, 128)), vmem((SOLVES, NS, 20, 128)),
        vmem((SOLVES, 17, 128)), vmem((SOLVES, NC, 17, 128)),
        vmem((1, 128)), vmem((NS * NC, 1, 128)),
        vmem((16, 128)), vmem((16, 128)), vmem((8, 128)), vmem((6, 8, 128)), vmem((2, CASES, 8, 128)), vmem((8, 128)), vmem((8, 128)),
        dma((15,)), dma((4,)), dma((4,)), dma((4,)), dma((SOLVES, 4)), dma((SOLVES, 4)),
        dma((SOLVES, 4)), dma((SOLVES, 4)), dma((1,)), dma((1,)),
    ]
    tall = jax.ShapeDtypeStruct((CASES, ROWS, 2048), F32)
    step, direction, rest, image, alpha = pl.pallas_call(
        kernel,
        out_shape=[tall] * 4 + [jax.ShapeDtypeStruct((CASES, 2048), F32)],
        in_specs=[pl.BlockSpec(memory_space=pltpu.HBM)] * 8,
        out_specs=[pl.BlockSpec(memory_space=pltpu.HBM)] * 4 + [pl.BlockSpec(memory_space=pltpu.VMEM)],
        scratch_shapes=scratch,
        compiler_params=pltpu.CompilerParams(collective_id=0, has_side_effects=True, vmem_limit_bytes=54 * 2**20),
        name="newton",
    )(voltage, photocurrent, shunt, series, pattern.T, diode_mask.T, aggregate.T, coarse_inverse)
    alpha = alpha[:, None, :]
    return step + alpha * direction, rest - alpha * image


def solution(mesh):
    field = P(None, "str", "crs")
    plane = P("str", "crs")
    return jax.shard_map(
        shards,
        mesh=mesh,
        in_specs=(field, field, plane, plane, plane, plane, plane, P("crs", None)),
        out_specs=(field, field),
        check_vma=False,
    )
```

```python
import itertools

import jax
import jax.numpy as jnp
from jax import lax
from jax.experimental import pallas as pl
from jax.experimental.pallas import tpu as pltpu
from jax.sharding import PartitionSpec as P

MESH = pl.DeviceIdType.MESH
F32 = jnp.float32
BF16 = jnp.bfloat16

CASES = 4
ROWS = 32
BLOCKS = 16
STEP = 40
FIELD = (BLOCKS + 2) * STEP
NS = 16
NC = 8
SOLVES = 3
LEVELS = (0.25, 0.5, 1.0, 2.0)


def dot(a, b):
    return jnp.dot(a, b, preferred_element_type=F32)


def halves(x):
    high = x.astype(BF16)
    return high, (x - high.astype(F32)).astype(BF16)


def kernel(
    v_in, photo_in, shunt_in, series_in, pattern_in, mask_in, group_in, inverse_in,
    xf_out, df_out, rf_out, qf_out, alpha_out,
    xn, dn, vn, pn, shn, sn, patn, maskn, groupn, staged, a_high, a_low,
    ef, rf, qf, df, xf, uf, wf, dgf, inf, pcf,
    sf, rlf, llf, dmf,
    cb, gm, e_low, m_high, groups, e_turn, ones_pair, ones_wide,
    bu, bw, bq, br, sd, ss, su, er, el, lb,
    pk, turned, su_s, sd_s, sl_s, sr_s, su_r, sd_r, sl_r, sr_r,
    hu_s, hd_s, hl_s, hr_s, hu_r, hd_r, hl_r, hr_r,
    s1, r1, s2, r2, s3, r3, s4, r4, fs, fr,
    y_now, t_now, t_tile, state, per_case, local, local_w,
    in_sem, out_sem, setup_send, setup_recv, halo_send, halo_recv, send_sem, recv_sem, last_send, last_recv,
):
    s = lax.axis_index("str")
    c = lax.axis_index("crs")

    def at_str(k):
        return (lax.rem(s + k, NS), c)

    def at_crs(k):
        return (s, lax.rem(c + k, NC))

    str_at = {}
    for key in itertools.product(range(2), range(4), range(2)):
        x_lo, y, core = (lax.rem(p + k, n) for p, k, n in zip((s // 8, lax.rem(s // 2, 4), lax.rem(s, 2)), key, (2, 4, 2)))
        str_at[key] = (x_lo * 4 + y) * 2 + core
    crs_at = {}
    for key in itertools.product(range(2), range(4)):
        x_hi, z = (lax.rem(p + k, n) for p, k, n in zip((c // 4, lax.rem(c, 4)), key, (2, 4)))
        crs_at[key] = x_hi * 4 + z

    def far_first(key):
        x_lo, y, core, x_hi, z = key
        across = 1 if x_lo else 2 * x_hi
        return -(across + min(y, 4 - y) + min(z, 4 - z) + 0.5 * core)

    everyone = sorted(itertools.product(range(2), range(4), range(2), range(2), range(4)), key=far_first)[:-1]
    everyone = [(key, (str_at[key[:3]], crs_at[key[3:]])) for key in everyone]
    str_peers = [(who[0], c) for key, who in everyone if key[3:] == (0, 0)]
    crs_peers = [(s, who[1]) for key, who in everyone if key[:3] == (0, 0, 0)]

    barrier = pltpu.get_barrier_semaphore()
    for who in str_peers + crs_peers:
        pl.semaphore_signal(barrier, inc=1, device_id=who, device_id_type=MESH)

    loads = [
        pltpu.make_async_copy(v_in, vn, in_sem.at[0]),
        pltpu.make_async_copy(series_in, sn, in_sem.at[1]),
        pltpu.make_async_copy(pattern_in, patn, in_sem.at[2]),
        pltpu.make_async_copy(mask_in, maskn, in_sem.at[3]),
        pltpu.make_async_copy(group_in, groupn, in_sem.at[4]),
        pltpu.make_async_copy(shunt_in, shn, in_sem.at[5]),
        pltpu.make_async_copy(photo_in, pn, in_sem.at[6]),
    ]
    quarter = pl.multiple_of((s // 4) * 128, 128)
    for k in range(NC):
        loads.append(
            pltpu.make_async_copy(
                inverse_in.at[:, pl.ds(pl.multiple_of(k * 512 + quarter, 128), 128)], staged.at[k], in_sem.at[7 + k]
            )
        )
    for copy in loads:
        copy.start()

    lane = lax.broadcasted_iota(jnp.int32, (ROWS, 128), 1)
    case_of = lane // 32
    is_first = lane == 0
    is_last = lane == 127
    case8 = case_of[0:8]
    sub8 = lax.broadcasted_iota(jnp.int32, (8, 128), 0)
    spot = (lax.broadcasted_iota(jnp.int32, (ROWS, 128), 0) == lane - 32 * case_of).astype(F32)

    def remote(src, dst, send, recv, who):
        return pltpu.make_async_remote_copy(
            src_ref=src, dst_ref=dst, send_sem=send, recv_sem=recv, device_id=who, device_id_type=MESH
        )

    def arrived(ref, sem):
        pltpu.make_async_copy(ref, ref, sem).wait()

    def rows_of(case, row):
        return pl.ds(case * FIELD + STEP + row, BLOCKS, stride=STEP)

    def edges_out(f, up, down, left, right):
        for case in range(CASES):
            up[case * 16 : case * 16 + 16, :] = f[rows_of(case, 0), :]
            down[case * 16 : case * 16 + 16, :] = f[rows_of(case, ROWS - 1), :]
        for block, ref in ((0, left), (BLOCKS - 1, right)):
            first = (block + 1) * STEP
            tile = jnp.concatenate(
                [f[case * FIELD + first : case * FIELD + first + ROWS, :] for case in range(CASES)], axis=0
            ).T
            ref[0:8, :] = tile[0:8] if block == 0 else tile[120:128]

    def edges_in(f, above, below, left, right):
        for case in range(CASES):
            f[rows_of(case, -1), :] = above[case * 16 : case * 16 + 16, :]
            f[rows_of(case, ROWS), :] = below[case * 16 : case * 16 + 16, :]
        for first, row in ((0, left[7:8, :]), (17 * STEP, right[0:1, :])):
            tile = jnp.broadcast_to(row, (128, 128)).T
            for case in range(CASES):
                f[case * FIELD + first : case * FIELD + first + ROWS, :] = tile[case * ROWS : case * ROWS + ROWS]

    def exchange(bufs, send, recv):
        up_s, down_s, left_s, right_s, above_r, below_r, left_r, right_r = bufs
        copies = [
            remote(up_s, below_r, send.at[0], recv.at[0], at_str(NS - 1)),
            remote(down_s, above_r, send.at[1], recv.at[1], at_str(1)),
            remote(left_s, right_r, send.at[2], recv.at[2], at_crs(NC - 1)),
            remote(right_s, left_r, send.at[3], recv.at[3], at_crs(1)),
        ]
        for copy in copies:
            copy.start()
        return copies

    def neighbours(f, case, base):
        def part(shift):
            return f[pl.ds(case * FIELD + base + shift, ROWS), :]

        here = part(0)
        right = pltpu.roll(jnp.where(is_first, part(STEP), here), 127, 1)
        left = pltpu.roll(jnp.where(is_last, part(-STEP), here), 1, 1)
        return here, part(1), part(-1), right, left

    def links(j, base):
        flat = pl.ds(pl.multiple_of(j * ROWS, ROWS), ROWS)
        return sf[pl.ds(base, ROWS), :], sf[pl.ds(base - 1, ROWS), :], rlf[flat, :], llf[flat, :]

    def jacobian(f, case, base, link):
        down, up, right_link, left_link = link
        here, below, above, right, left = neighbours(f, case, base)
        diagonal = dgf[pl.ds(case * FIELD + base, ROWS), :]
        return here, diagonal * here - down * below - up * above - right_link * right - left_link * left

    def fold(x):
        return x[0:8] + x[8:16] + x[16:24] + x[24:32]

    def by_case(parts):
        total = jnp.zeros((8, 128), F32)
        for case in range(CASES):
            total = jnp.where(case8 == case, jnp.sum(parts[case], axis=(0, 1), keepdims=True), total)
        return total

    def case_sums(x):
        total = jnp.zeros((8, 128), F32)
        for case in range(CASES):
            one = jnp.sum(jnp.where(case8 == case, x, 0.0), axis=1, keepdims=True)
            total = jnp.where(case8 == case, one, total)
        return total


    def spread(x, column, rows=ROWS):
        return jnp.broadcast_to(x[:, column : column + 1], (rows, 128))

    def clear(i, _):
        rows = pl.ds(pl.multiple_of(i * 80, 16), 80)
        for f in (ef, wf, qf, df, xf):
            f[rows, :] = jnp.zeros((80, 128), F32)
        return 0

    lax.fori_loop(0, CASES * FIELD // 80, clear, 0)
    sf[...] = jnp.zeros_like(sf)
    bw[...] = jnp.zeros_like(bw)
    bq[...] = jnp.zeros_like(bq)
    state[...] = jnp.zeros_like(state)
    per_case[...] = jnp.zeros_like(per_case)
    for copy in loads[:5]:
        copy.wait()
    level = jnp.zeros((BLOCKS, ROWS), F32)
    for number in range(4):
        level = level + jnp.where(patn[...] == number, F32(LEVELS[number]), F32(0.0))
    turned[...] = jnp.zeros_like(turned)
    turned[0:16, 0:32] = groupn[...].astype(F32)
    turned[16:32, 0:32] = level
    turned[32:48, 0:32] = maskn[...].astype(F32) * 0.5
    pk[...] = turned[...].T[0:ROWS]
    packed = pk[...]

    def lay_out(j, _):
        base = pl.multiple_of((j + 1) * STEP, 8)
        cols = pl.ds(pl.multiple_of(j * 128, 128), 128)
        for case in range(CASES):
            ef[pl.ds(case * FIELD + base, ROWS), :] = vn[case, :, cols]
        sf[pl.ds(base, ROWS), :] = sn[:, cols]
        return 0

    lax.fori_loop(0, BLOCKS, lay_out, 0)
    edges_out(ef, su_s, sd_s, sl_s, sr_s)
    su_s[64:72, :] = packed[0:8]
    sd_s[64:72, :] = packed[24:32]
    sd_s[72:88, :] = sf[pl.ds(STEP + ROWS - 1, BLOCKS, stride=STEP), :]
    sl_s[1:2, :] = turned[0:1, :]
    sl_s[2:3, :] = turned[16:17, :]
    sr_s[1:2, :] = turned[15:16, :]
    sr_s[2:3, :] = turned[31:32, :]

    pl.semaphore_wait(barrier, NS - 1 + NC - 1)
    setup_copies = exchange((su_s, sd_s, sl_s, sr_s, sd_r, su_r, sl_r, sr_r), setup_send, setup_recv)

    groups[...] = jnp.zeros_like(groups)
    for j in range(BLOCKS):
        base = (j + 1) * STEP
        group = spread(packed, j).astype(jnp.int32)
        groups[base : base + ROWS, :] = group
        low = group // 32
        code = (low % 16) * 8 + low // 16
        lb[j * ROWS : j * ROWS + ROWS, 0:128] = (lane == code).astype(F32).astype(BF16)
        dmf[j * ROWS : j * ROWS + ROWS, :] = spread(packed, 32 + j)
    for k in range(4):
        e_turn[:, k * 128 : k * 128 + 128] = lb[k * 128 : k * 128 + 128, 0:128].astype(F32).T.astype(BF16)

    same = lax.broadcasted_iota(jnp.int32, (128, 128), 0) // 32
    across = lax.broadcasted_iota(jnp.int32, (128, 128), 1) // 32
    block_ones = (same == across).astype(F32).astype(BF16)
    ones_pair[0:128, :] = block_ones
    ones_pair[128:256, :] = block_ones
    for case in range(CASES):
        wide = (same == case).astype(F32).astype(BF16)
        ones_wide[0:128, case * 128 : case * 128 + 128] = wide
        ones_wide[128:256, case * 128 : case * 128 + 128] = wide

    row_levels = [spread(packed, 16 + j) for j in range(BLOCKS)]
    blank = jnp.zeros((ROWS, 128), F32)
    row_levels = [blank] + row_levels + [blank]
    for j in range(BLOCKS):
        here = row_levels[j + 1]
        right = jnp.minimum(here, row_levels[j + 2])
        left = jnp.minimum(here, row_levels[j])
        rlf[j * ROWS : j * ROWS + ROWS, :] = jnp.where(is_last, right, here)
        llf[j * ROWS : j * ROWS + ROWS, :] = jnp.where(is_first, left, here)
        er[j * ROWS : j * ROWS + ROWS, :] = right
        el[j * ROWS : j * ROWS + ROWS, :] = left

    def block_columns(j, base, sums, target):
        total = jnp.zeros((ROWS, 128), F32)
        for case in range(CASES):
            total = jnp.where(case_of == case, jnp.sum(sums[case], axis=1, keepdims=True), total)
        if target is not None:
            target[pl.ds(pl.multiple_of(j * ROWS, ROWS), ROWS), :] = total
        return total

    def to_scatter(j, base, total):
        flat = pl.ds(pl.multiple_of(j * ROWS, ROWS), ROWS)
        high, low = halves(total * m_high[pl.ds(base, ROWS), :])
        lb[flat, 0:128] = high
        lb[flat, 128:256] = low

    def codes(i, _):
        rows = pl.ds(pl.multiple_of(i * 80, 16), 80)
        group = groups[rows, :]
        lanes = lax.broadcasted_iota(jnp.int32, (80, 128), 1)
        e_low[rows, :] = (lanes == group // 32).astype(F32).astype(BF16)
        m_high[rows, :] = (lanes % 32 == group % 32).astype(F32)
        return 0

    lax.fori_loop(0, FIELD // 80, codes, 0)
    for copy in loads[5:7]:
        copy.wait()

    def start_rest(j, _):
        base = pl.multiple_of((j + 1) * STEP, 8)
        cols = pl.ds(pl.multiple_of(j * 128, 128), 128)
        flat = pl.ds(pl.multiple_of(j * ROWS, ROWS), ROWS)
        down, up, right_link, left_link = links(j, base)
        shunt = shn[:, cols]
        half = dmf[flat, :]
        rests = []
        for case in range(CASES):
            at = pl.ds(case * FIELD + base, ROWS)
            here, below, above, right, left = neighbours(ef, case, base)
            slope = half * jnp.exp(here)
            rest = pn[case, :, cols] - (
                shunt * here
                + down * (here - below)
                + up * (here - above)
                + right_link * (here - right)
                + left_link * (here - left)
                + slope
                - half
            )
            dgf[at, :] = slope
            rf[at, :] = rest
            rests.append(rest)
        block_columns(j, base, rests, br)
        return 0

    def start_scaled(j, sums):
        base = pl.multiple_of((j + 1) * STEP, 8)
        cols = pl.ds(pl.multiple_of(j * 128, 128), 128)
        flat = pl.ds(pl.multiple_of(j * ROWS, ROWS), ROWS)
        down, up, right_link, left_link = links(j, base)
        shunt = shn[:, cols]
        edge = jnp.where(is_last, right_link, 0.0) + jnp.where(is_first, left_link, 0.0)
        out, plain = [], []
        for case in range(CASES):
            at = pl.ds(case * FIELD + base, ROWS)
            ground = shunt + dgf[at, :] + down + up
            diagonal = ground + right_link + left_link
            inverse = 1.0 / diagonal
            rest = rf[at, :]
            scaled = rest * inverse
            dgf[at, :] = diagonal
            inf[at, :] = inverse
            ef[at, :] = scaled
            out.append(sums[case] + fold(rest * scaled))
            plain.append(ground + edge)
        block_columns(j, base, plain, sd)
        ss[flat, :] = jnp.broadcast_to(jnp.sum(down, axis=1, keepdims=True), (ROWS, 128))
        su[flat, :] = jnp.broadcast_to(jnp.sum(up, axis=1, keepdims=True), (ROWS, 128))
        return tuple(out)

    zero = jnp.zeros((8, 128), F32)
    lax.fori_loop(0, BLOCKS, start_rest, 0)

    for copy in setup_copies:
        copy.wait()
    edges_in(ef, sd_r, su_r, sl_r, sr_r)
    sf[pl.ds(STEP - 1, BLOCKS, stride=STEP), :] = sd_r[72:88, :]
    open_left = jnp.where(c == 0, 0.0, 1.0).astype(F32)
    open_right = jnp.where(c == NC - 1, 0.0, 1.0).astype(F32)
    level_left = jnp.broadcast_to(sl_r[2:3, :], (128, 128)).T[0:ROWS]
    level_right = jnp.broadcast_to(sr_r[2:3, :], (128, 128)).T[0:ROWS]
    for block, slot, level_there, is_open, is_edge, link, edge in (
        (0, 0, level_left, open_left, is_first, llf, el),
        (BLOCKS - 1, BLOCKS + 1, level_right, open_right, is_last, rlf, er),
    ):
        rows = pl.ds(block * ROWS, ROWS)
        here = row_levels[block + 1]
        value = jnp.minimum(here, level_there) * is_open
        link[rows, :] = jnp.where(is_edge, value, here)
        edge[rows, :] = value
        total = br[rows, :]
        for case in range(CASES):
            at = pl.ds(case * FIELD + (block + 1) * STEP, ROWS)
            there = ef[pl.ds(case * FIELD + slot * STEP, ROWS), :]
            more = jnp.where(is_edge, value * (there - ef[at, :]), 0.0)
            rf[at, :] = rf[at, :] + more
            total = total + jnp.where(case_of == case, jnp.sum(more, axis=1, keepdims=True), 0.0)
        br[rows, :] = total
    for first in (True, False):
        edge_row = 0 if first else ROWS - 1
        link = sf[pl.ds(STEP + (-1 if first else edge_row), BLOCKS, stride=STEP), :]
        rows = pl.ds(edge_row, BLOCKS, stride=ROWS)
        total = br[rows, :]
        for case in range(CASES):
            if first:
                more = link * (ef[rows_of(case, -1), :] - ef[rows_of(case, 0), :])
            else:
                more = link * ef[rows_of(case, ROWS), :]
            rf[rows_of(case, edge_row), :] = rf[rows_of(case, edge_row), :] + more
            total = total + jnp.where(case_of[0:BLOCKS] == case, jnp.sum(more, axis=1, keepdims=True), 0.0)
        br[rows, :] = total

    def scatter_rest(j, _):
        to_scatter(j, pl.multiple_of((j + 1) * STEP, 8), br[pl.ds(pl.multiple_of(j * ROWS, ROWS), ROWS), :])
        return 0

    lax.fori_loop(0, BLOCKS, scatter_rest, 0, unroll=4)

    def prepare_rest():
        above8 = sd_r[64:72, :]
        below8 = su_r[64:72, :]
        for j in range(BLOCKS):
            base = (j + 1) * STEP
            groups[base - 1 : base, :] = spread(above8, j, 8)[7:8].astype(jnp.int32)
            groups[base + ROWS : base + ROWS + 1, :] = spread(below8, j, 8)[0:1].astype(jnp.int32)
        for first, row_there in ((0, sl_r[1:2, :]), (17 * STEP, sr_r[1:2, :])):
            groups[first : first + ROWS, :] = jnp.broadcast_to(row_there, (128, 128)).T[0:ROWS].astype(jnp.int32)
        lax.fori_loop(0, FIELD // 80, codes, 0)
        for copy in loads[7:]:
            copy.wait()

        def pick(i, _):
            rows = pl.ds(pl.multiple_of(i * 32, 32), 32)
            for side in range(2):
                block = jnp.zeros((ROWS, 128), F32)
                for k in range(4):
                    turn = lax.rem(32 * k + 128 - 32 * lax.rem(s, 4), 128)
                    block = jnp.where(case_of == k, pltpu.roll(staged[side * 4 + k, rows, :], turn, 1), block)
                high, low = halves(block)
                a_high[rows, side * 128 : side * 128 + 128] = high
                a_low[rows, side * 128 : side * 128 + 128] = low
            return 0

        lax.fori_loop(0, 16, pick, 0)


    def send_restricted(k):
        out = dot(e_turn[...], lb[...])
        s1[k] = (out[:, 0:128] + out[:, 128:256]).reshape(NS, 8, 128)
        for who in str_peers:
            remote(s1.at[k, who[0]], r1.at[k, s], send_sem.at[k, 0], recv_sem.at[k, 0], who).start()
        r1[k, s] = s1[k, s]

    def send_chunk(k, tile):
        arrived(r1.at[k, 0 : NS - 1], recv_sem.at[k, 0])
        s2[k, 0:8, :] = jnp.sum(r1[k], axis=0)
        s2[k, 8:12, :] = tile[0:4]
        for who in crs_peers:
            remote(s2.at[k], r2.at[k, c], send_sem.at[k, 1], recv_sem.at[k, 1], who).start()
        r2[k, c] = s2[k]

    def send_product(k):
        arrived(r2.at[k, 0 : NC - 1], recv_sem.at[k, 1])
        total = jnp.sum(r2[k], axis=0)
        t = total[0:8]
        t_tile[...] = t
        placed = jnp.concatenate([jnp.broadcast_to(t[i : i + 1], (ROWS, 128)) * spot for i in range(NC)], axis=0)
        high, low = halves(placed)
        both = dot(jnp.concatenate([high, low], axis=0), ones_pair[0:128, :]).astype(BF16)
        right = jnp.concatenate([both[0:256], both[256:512]], axis=1)
        out = dot(a_high[...], right)
        out = out[:, 0:128] + out[:, 128:256] + dot(a_low[...], both[0:256])
        y = jnp.sum(out.reshape(16, ROWS, 128) * spot[None], axis=1)
        s3[k, 0:16, :] = y
        own = t_tile[pl.ds(c, 1), :]
        s3[k, 16:20, :] = jnp.where(sub8[0:4] == 0, jnp.broadcast_to(own, (4, 128)), total[8:12])
        for who in str_peers:
            remote(s3.at[k], r3.at[k, s], send_sem.at[k, 2], recv_sem.at[k, 2], who).start()
        r3[k, s] = s3[k]

    RZ, RR, ALPHA, BETA, RQ, QQ = range(6)

    def row(x, i):
        return jnp.broadcast_to(x[i : i + 1], (8, 128))

    def send_correction(k, first=False):
        arrived(r3.at[k, 0 : NS - 1], recv_sem.at[k, 2])
        total = jnp.sum(r3[k], axis=0)
        y = total[0:16]
        t = jnp.concatenate([r3[k, i, 16:17, :] for i in range(NS)], axis=0)
        sums = total[16:20]
        if first:
            state[RR] = row(sums, 1)
        else:
            alpha = state[RZ] / row(sums, 1)
            state[ALPHA] = alpha
            state[QQ] = row(sums, 2)
            state[RQ] = row(sums, 3)
            y = y_now[...] - alpha[0:1] * y
            t = t_now[...] - alpha[0:1] * t
        y_now[...] = y
        t_now[...] = t
        s4[k, 0:16, :] = y
        s4[k, 16:17, :] = jnp.sum(y * t, axis=0, keepdims=True)
        for who in crs_peers:
            remote(s4.at[k], r4.at[k, c], send_sem.at[k, 3], recv_sem.at[k, 3], who).start()
        r4[k, c] = s4[k]
        if not first:
            bu[...] = bu[...] - alpha[0:1] * bw[...]

    def to_cases(slot, x):
        for case in range(CASES):
            per_case[slot, case] = jnp.broadcast_to(x[:, case * 32 : case * 32 + 1], (8, 128))

    def receive_correction(k, first=False):
        arrived(r4.at[k, 0 : NC - 1], recv_sem.at[k, 3])
        correction = jnp.concatenate([r4[k, i, 0:16, :] for i in range(NC)], axis=0)
        high, low = halves(correction)
        picked = dot(e_low[...], jnp.concatenate([high, low], axis=1))
        mask = m_high[...]
        gm[:, 0:128] = (picked[:, 0:128] * mask).astype(BF16)
        gm[:, 128:256] = (picked[:, 128:256] * mask).astype(BF16)
        cb[...] = dot(gm[...], ones_pair[...])
        coarse = case_sums(jnp.broadcast_to(jnp.sum(r4[k, :, 16:17, :], axis=0), (8, 128)))
        if first:
            state[RZ] = state[RR] + coarse
        else:
            alpha = state[ALPHA]
            smooth = state[RR] - 2.0 * alpha * state[RQ] + alpha * alpha * state[QQ]
            fresh = smooth + coarse
            state[RR] = smooth
            state[BETA] = fresh / state[RZ]
            state[RZ] = fresh

    def block_level(final=False):
        beta = state[BETA][0:1]

        def body(j, energy):
            base = pl.multiple_of((j + 1) * STEP, 8)
            flat = pl.ds(pl.multiple_of(j * ROWS, ROWS), ROWS)
            value = bu[flat, :] + beta * bq[flat, :]
            here = cb[pl.ds(base, ROWS), :]
            stencil = (
                sd[flat, :] * here
                - ss[flat, :] * cb[pl.ds(base + 1, ROWS), :]
                - su[flat, :] * cb[pl.ds(base - 1, ROWS), :]
                - er[flat, :] * cb[pl.ds(base + STEP, ROWS), :]
                - el[flat, :] * cb[pl.ds(base - STEP, ROWS), :]
            )
            if final:
                return energy + fold(here * (stencil + 2.0 * value))
            value = value + stencil
            bq[flat, :] = value
            to_scatter(j, base, value)
            return energy

        return lax.fori_loop(0, BLOCKS, body, zero, unroll=4)


    def widen_correction():
        wide = dot(gm[...], ones_wide[...])
        for case in range(CASES):
            pcf[case * FIELD : case * FIELD + FIELD, :] = wide[:, case * 128 : case * 128 + 128]

    def next_direction(final=False):
        to_cases(0, state[ALPHA])
        to_cases(1, state[BETA])
        widen_correction()
        kinds = 0 if final else 5

        def body(j, sums):
            base = pl.multiple_of((j + 1) * STEP, 8)
            cols = pl.ds(pl.multiple_of(j * 128, 128), 128)
            link = links(j, base)
            out = []
            for case in range(CASES):
                at = pl.ds(case * FIELD + base, ROWS)
                here, image = jacobian(pcf, case, base, link)
                rest = rf[at, :]
                inverse = inf[at, :]
                alpha = per_case[0, case][0:1]
                beta = per_case[1, case][0:1]
                last_image = qf[at, :]
                last_direction = df[at, :]
                smooth = uf[at, :] - alpha * wf[at, :]
                image = image + beta * last_image + smooth
                rest = rest - alpha * last_image
                step = xf[at, :] + alpha * last_direction
                direction = rest * inverse + here + beta * last_direction
                if final:
                    xn[case, :, cols] = step
                    vn[case, :, cols] = rest
                    dn[case, :, cols] = direction
                    pn[case, :, cols] = image
                    continue
                uf[at, :] = smooth
                rf[at, :] = rest
                xf[at, :] = step
                qf[at, :] = image
                df[at, :] = direction
                scaled = image * inverse
                ef[at, :] = scaled
                terms = [direction * image, image * scaled, rest * scaled, rest * inverse * smooth, scaled * smooth]
                out.extend(sums[kinds * case + i] + fold(terms[i]) for i in range(kinds))
            return tuple(out)

        sums = lax.fori_loop(0, BLOCKS, body, (zero,) * (kinds * CASES))
        tile = zero
        for kind in range(kinds):
            one = by_case([sums[kinds * case + kind] for case in range(CASES)])
            tile = jnp.where(sub8 == kind + 1, one, tile)
        return tile

    def start_halo(k):
        edges_out(ef, hu_s.at[k], hd_s.at[k], hl_s.at[k], hr_s.at[k])
        bufs = [ref.at[k] for ref in (hu_s, hd_s, hl_s, hr_s, hd_r, hu_r, hl_r, hr_r)]
        return exchange(bufs, halo_send.at[k], halo_recv.at[k])

    def apply_scaled(k, copies, target, sums_to):
        for copy in copies:
            copy.wait()
        edges_in(ef, hd_r.at[k], hu_r.at[k], hl_r.at[k], hr_r.at[k])

        def body(j, sums):
            base = pl.multiple_of((j + 1) * STEP, 8)
            link = links(j, base)
            values, out = [], []
            for case in range(CASES):
                here, image = jacobian(ef, case, base, link)
                target[pl.ds(case * FIELD + base, ROWS), :] = image
                values.append(image)
                out.append(sums[case] + fold(here * image))
            block_columns(j, base, values, sums_to)
            return tuple(out)

        return lax.fori_loop(0, BLOCKS, body, (zero,) * CASES)


    send_restricted(0)
    start_sums = lax.fori_loop(0, BLOCKS, start_scaled, (zero,) * CASES)
    tile = jnp.where(sub8 == 1, by_case(start_sums), zero)
    copies = start_halo(0)
    send_chunk(0, tile)
    prepare_rest()
    send_product(0)
    apply_scaled(0, copies, uf, bu)
    send_correction(0, first=True)
    receive_correction(0, first=True)

    def solve(k, _):
        block_level()
        send_restricted(k)
        tile = next_direction()
        local[...] = tile
        copies = start_halo(k)
        send_chunk(k, tile)
        send_product(k)
        local_w[...] = by_case(apply_scaled(k, copies, wf, bw))
        send_correction(k)
        receive_correction(k)
        return 0

    lax.fori_loop(1, SOLVES, solve, 0)


    alpha = state[ALPHA]
    beta = state[BETA]
    energy = jnp.sum(block_level(final=True), axis=0, keepdims=True)
    dq, qq, rq, eu, qu = (row(local[...], i) for i in range(1, 6))
    energy = (
        energy
        + (eu - 2.0 * alpha * qu + alpha * alpha * local_w[...])
        + 2.0 * beta * (rq - alpha * qq)
        + beta * beta * dq
    )
    here = s * NC + c
    fs[...] = energy[0:1]
    for _, who in everyone:
        remote(fs, fr.at[here], last_send.at[0], last_recv.at[0], who).start()
    fr[here] = fs[...]
    next_direction(final=True)
    stores = [
        pltpu.make_async_copy(src, dst, out_sem.at[i])
        for i, (src, dst) in enumerate(((xn, xf_out), (dn, df_out), (vn, rf_out), (pn, qf_out)))
    ]
    for copy in stores:
        copy.start()
    arrived(fr.at[0 : NS * NC - 1], last_recv.at[0])
    alpha = state[RZ] / jnp.broadcast_to(jnp.sum(fr[...], axis=0), (8, 128))
    for case in range(CASES):
        alpha_out[case : case + 1, :] = jnp.broadcast_to(alpha[0:1, case * 32 : case * 32 + 1], (1, 2048))


    for copy in stores:
        copy.wait()

    for k in range(SOLVES):
        arrived(r1.at[k, 0 : NS - 1], send_sem.at[k, 0])
        arrived(r2.at[k, 0 : NC - 1], send_sem.at[k, 1])
        arrived(r3.at[k, 0 : NS - 1], send_sem.at[k, 2])
        arrived(r4.at[k, 0 : NC - 1], send_sem.at[k, 3])
    arrived(fr.at[0 : NS * NC - 1], last_send.at[0])


def last_update(step, direction, rest, image, alphas, step_out, rest_out, x, d, r, q, in_sem, out_sem):
    loads = [
        [pltpu.make_async_copy(src.at[case], dst.at[case], in_sem.at[i, case]) for i, (src, dst) in enumerate(pairs)]
        for pairs in [((step, x), (direction, d), (rest, r), (image, q))]
        for case in range(CASES)
    ]
    for copies in loads:
        for copy in copies:
            copy.start()
    stores = []
    for case in range(CASES):
        for copy in loads[case]:
            copy.wait()
        alpha = alphas[case : case + 1, :]
        x[case] = x[case] + alpha * d[case]
        r[case] = r[case] - alpha * q[case]
        for i, (src, dst) in enumerate(((x, step_out), (r, rest_out))):
            stores.append(pltpu.make_async_copy(src.at[case], dst.at[case], out_sem.at[i, case]))
            stores[-1].start()
    for copy in stores:
        copy.wait()


def shards(voltage, photocurrent, shunt, series, pattern, diode_mask, aggregate, coarse_inverse):
    field = (CASES * FIELD, 128)
    flat = (BLOCKS * ROWS, 128)

    def vmem(shape, dtype=F32):
        return pltpu.VMEM(shape, dtype)

    dma = pltpu.SemaphoreType.DMA
    scratch = [
        *[vmem((CASES, ROWS, 2048)) for _ in range(4)], vmem((ROWS, 2048)), vmem((ROWS, 2048)),
        vmem((BLOCKS, ROWS), jnp.int32), vmem((BLOCKS, ROWS), jnp.int32), vmem((BLOCKS, ROWS), jnp.int32),
        vmem((NC, 512, 128)), vmem((512, 256), BF16), vmem((512, 256), BF16),
        *[vmem(field) for _ in range(10)],
        vmem((FIELD, 128)), vmem(flat), vmem(flat), vmem(flat),
        vmem((FIELD, 128)), vmem((FIELD, 256), BF16), vmem((FIELD, 128), BF16), vmem((FIELD, 128)),
        vmem((FIELD, 128), jnp.int32), vmem((128, 512), BF16), vmem((256, 128), BF16), vmem((256, 512), BF16),
        *[vmem(flat) for _ in range(9)], vmem((512, 256), BF16),
        vmem((ROWS, 128)), vmem((128, 128)),
        vmem((72, 128)), vmem((88, 128)), vmem((8, 128)), vmem((8, 128)),
        vmem((72, 128)), vmem((88, 128)), vmem((8, 128)), vmem((8, 128)),
        vmem((SOLVES, 64, 128)), vmem((SOLVES, 64, 128)), vmem((SOLVES, 8, 128)), vmem((SOLVES, 8, 128)),
        vmem((SOLVES, 64, 128)), vmem((SOLVES, 64, 128)), vmem((SOLVES, 8, 128)), vmem((SOLVES, 8, 128)),
        vmem((SOLVES, NS, 8, 128)), vmem((SOLVES, NS, 8, 128)),
        vmem((SOLVES, 12, 128)), vmem((SOLVES, NC, 12, 128)),
        vmem((SOLVES, 20, 128)), vmem((SOLVES, NS, 20, 128)),
        vmem((SOLVES, 17, 128)), vmem((SOLVES, NC, 17, 128)),
        vmem((1, 128)), vmem((NS * NC, 1, 128)),
        vmem((16, 128)), vmem((16, 128)), vmem((8, 128)), vmem((6, 8, 128)), vmem((2, CASES, 8, 128)), vmem((8, 128)), vmem((8, 128)),
        dma((15,)), dma((4,)), dma((4,)), dma((4,)), dma((SOLVES, 4)), dma((SOLVES, 4)),
        dma((SOLVES, 4)), dma((SOLVES, 4)), dma((1,)), dma((1,)),
    ]
    tall = jax.ShapeDtypeStruct((CASES, ROWS, 2048), F32)
    step, direction, rest, image, alpha = pl.pallas_call(
        kernel,
        out_shape=[tall] * 4 + [jax.ShapeDtypeStruct((CASES, 2048), F32)],
        in_specs=[pl.BlockSpec(memory_space=pltpu.HBM)] * 8,
        out_specs=[pl.BlockSpec(memory_space=pltpu.HBM)] * 4 + [pl.BlockSpec(memory_space=pltpu.VMEM)],
        scratch_shapes=scratch,
        compiler_params=pltpu.CompilerParams(collective_id=0, has_side_effects=True, vmem_limit_bytes=54 * 2**20),
        name="newton",
    )(voltage, photocurrent, shunt, series, pattern.T, diode_mask.T, aggregate.T, coarse_inverse)
    return pl.pallas_call(
        last_update,
        out_shape=[tall] * 2,
        in_specs=[pl.BlockSpec(memory_space=pltpu.HBM)] * 4 + [pl.BlockSpec(memory_space=pltpu.VMEM)],
        out_specs=[pl.BlockSpec(memory_space=pltpu.HBM)] * 2,
        scratch_shapes=[vmem((CASES, ROWS, 2048)) for _ in range(4)] + [dma((4, CASES)), dma((2, CASES))],
        compiler_params=pltpu.CompilerParams(vmem_limit_bytes=56 * 2**20),
        name="last_update",
    )(step, direction, rest, image, alpha)


def solution(mesh):
    field = P(None, "str", "crs")
    plane = P("str", "crs")
    return jax.shard_map(
        shards,
        mesh=mesh,
        in_specs=(field, field, plane, plane, plane, plane, plane, P("crs", None)),
        out_specs=(field, field),
        check_vma=False,
    )
```
